32 devices in a mesh: section: 2 (over core), mp: 4 (over z), dp: 4 (over y, x).
Axes of the slice: x: 2, y: 2, z: 4, core: 2. Of those that a mesh axis runs over, the one named last changes fastest.
Arguments:
- inputs: bfloat16 [8, 1024, 768], P('dp', 'mp'), may hold values from -6 to 6
- cotangent: bfloat16 [8, 1024, 768], P('dp', 'mp'), may hold values from -6 to 6
- lengths: int32 [8, 4], P('dp'), may hold values from 1 to 832, 960 in all within a row
- norm_gains: float32 [2, 2, 768], P('section'), may hold values from 0.5 to 1.5
- norm_shifts: float32 [2, 2, 768], P('section'), may hold values from -3 to 3
- in_weight: bfloat16 [2, 768, 3, 768], P('section', None, None, 'mp'), may hold values from -0.21875 to 0.21875
- in_bias: float32 [2, 2, 768], P('section', None, 'mp'), may hold values from -3 to 3
- out_weight: bfloat16 [2, 768, 768], P('section', 'mp'), may hold values from -1.75 to 1.75
- up_weight: bfloat16 [2, 768, 3072], P('section', None, 'mp'), may hold values from -0.21875 to 0.21875
- up_bias: float32 [2, 3072], P('section', 'mp'), may hold values from -3 to 3
- down_weight: bfloat16 [2, 3072, 768], P('section', 'mp'), may hold values from -0.3125 to 0.3125
- branch_bias: float32 [2, 2, 768], P('section'), may hold values from -3 to 3
Outputs:
- section_outputs: bfloat16 [2, 8, 1024, 768], P('section', 'dp', 'mp')
- input_grads: float32 [2, 8, 1024, 768], P('section', 'dp', 'mp')
- grad_norm_gains: float32 [2, 2, 768], P('section')
- grad_norm_shifts: float32 [2, 2, 768], P('section')
- grad_in_weight: float32 [2, 768, 3, 768], P('section', None, None, 'mp')
- grad_in_bias: float32 [2, 2, 768], P('section', None, 'mp')
- grad_out_weight: float32 [2, 768, 768], P('section', 'mp')
- grad_up_weight: float32 [2, 768, 3072], P('section', None, 'mp')
- grad_up_bias: float32 [2, 3072], P('section', 'mp')
- grad_down_weight: float32 [2, 3072, 768], P('section', 'mp')
- grad_branch_bias: float32 [2, 2, 768], P('section')
The draws below stay inside these ranges and needn't reach their ends.
Inputs may be any that keep to these rules, and one draw needn't show every extreme that they name: `lengths`: the 4 documents of a row fill its first 960 tokens in order, and its last 64 tokens are padding; in every row one document has exactly 832 tokens.
All inputs are finite; a program needn't handle non-finite values.
Results may differ from the reference program's by a relative error of at most 0.019.
Values may be sent and summed in bfloat16 or wider, within the bound.
A program may use at most 192 MiB of HBM per device.

```python
import math
import jax
import jax.numpy as jnp
import numpy as np
from jax import lax

D = 768
HEADS = 12
HEAD = 64
FF = 3072
LENGTH = 1024
NDOC = 4
PAD = 64
LONGEST = 832
LAYERS = 2
ROWS = 8


def block_scale(key, shape, split, smallest, top_value):
    level = 1.0
    for axis_at, shards_of in split:
        steps = jax.random.uniform(jax.random.fold_in(jax.random.fold_in(key, 6), axis_at), (shards_of,), jnp.float32, smallest / len(split), top_value / len(split))
        level = level * jnp.repeat(jnp.exp(steps), shape[axis_at] // shards_of).reshape((-1,) + (1,) * (len(shape) - 1 - axis_at))
    return level


def length_profile(amount, total, bound, lean):
    loads = [(1 << 20) // math.isqrt(grade ** lean) + 1 for grade in range(2, amount + 1)]
    rest, given = total - bound - (amount - 1), [1] * (amount - 1)
    while rest > 0:
        movable = [i for i in range(amount - 1) if given[i] < bound]
        pool, budget = sum([loads[i] for i in movable]), rest
        for i in movable:
            more = min(bound - given[i], max(1, budget * loads[i] // pool), rest)
            given[i] = given[i] + more
            rest = rest - more
    return np.array([bound] + given)


def ragged(key, number_of, total, reach, lean):
    if number_of == 2:
        one = jax.random.randint(key, (), max(1, total - reach), min(reach, total - 1) + 1)
        return jnp.stack([one, total - one])
    sizes = jnp.asarray(length_profile(number_of, total, reach, lean), jnp.int32)
    twos = (number_of - 1) // 2
    donor, sink = sizes[1:1 + 2 * twos:2], sizes[2:2 + 2 * twos:2]
    slack = jnp.minimum(donor - 1, reach - sink)
    moved = jax.random.randint(jax.random.fold_in(key, 1), (twos,), 0, 1 << 20) % (slack + 1)
    sizes = sizes.at[1:1 + 2 * twos:2].set(donor - moved).at[2:2 + 2 * twos:2].set(sink + moved)
    return sizes[jax.random.permutation(jax.random.fold_in(key, 2), number_of)]


def bell_draw(own_key, shape, scale, bound, cuts=(), kind=jnp.bfloat16):
    array = scale * jax.random.normal(own_key, shape, jnp.float32)
    if cuts:
        array = array * block_scale(own_key, shape, cuts, -0.22, 0.18)
    return jnp.clip(array, -bound, bound).astype(kind)


def setup_inputs(seed: int = 0) -> dict:
    seeds = jax.random.split(jax.random.key(seed), 13)
    return {
        "inputs": bell_draw(seeds[0], (ROWS, LENGTH, D), 1.0, 6.0, ((0, 4), (1, 4))),
        "cotangent": bell_draw(seeds[1], (ROWS, LENGTH, D), 1.0, 6.0, ((0, 4), (1, 4))),
        "lengths": jax.vmap(lambda own: ragged(own, NDOC, LENGTH - PAD, LONGEST, 2))(jax.random.split(seeds[2], ROWS)).reshape((ROWS, NDOC)).astype(jnp.int32),
        "norm_gains": jnp.clip(1.0 + 0.1 * jax.random.normal(seeds[3], (LAYERS, 2, D), jnp.float32), 0.5, 1.5),
        "norm_shifts": bell_draw(seeds[4], (LAYERS, 2, D), 0.5, 3.0, ((0, 2),), jnp.float32),
        "in_weight": bell_draw(seeds[5], (LAYERS, D, 3, D), D ** -0.5, 0.21875, ((0, 2), (3, 4))),
        "in_bias": bell_draw(seeds[6], (LAYERS, 2, D), 0.5, 3.0, ((0, 2), (2, 4)), jnp.float32),
        "out_weight": bell_draw(seeds[7], (LAYERS, D, D), (D // 64) ** -0.5, 1.75, ((0, 2), (1, 4))),
        "up_weight": bell_draw(seeds[8], (LAYERS, D, FF), D ** -0.5, 0.21875, ((0, 2), (2, 4))),
        "up_bias": bell_draw(seeds[9], (LAYERS, FF), 0.5, 3.0, ((0, 2), (1, 4)), jnp.float32),
        "down_weight": bell_draw(seeds[10], (LAYERS, FF, D), (FF // 8) ** -0.5, 0.3125, ((0, 2), (1, 4))),
        "branch_bias": bell_draw(seeds[11], (LAYERS, 2, D), 0.5, 3.0, ((0, 2),), jnp.float32),
    }


highest = lax.Precision.HIGHEST
branch_scale = 12.0 ** (-0.5)
norm_eps = 1e-05
masked_score = -1000000000.0

@jax.custom_vjp
def low(v):
    return lax.optimization_barrier(v.astype(jnp.bfloat16)).astype(jnp.float32)

@jax.custom_vjp
def low_back(v):
    return v

def low_keep(v):
    return (low(v), None)

def low_pass(kept, grad):
    return (grad,)

def back_keep(v):
    return (v, None)

def back_low(kept, grad):
    return (low(grad),)
low.defvjp(low_keep, low_pass)
low_back.defvjp(back_keep, back_low)

def layer_norm(values, gain, shift):
    mean = lax.optimization_barrier(jnp.mean(values, axis=-1, keepdims=True))
    centred = values - mean
    spread = lax.optimization_barrier(jnp.mean(centred * centred, axis=-1, keepdims=True))
    return centred * lax.rsqrt(spread + norm_eps) * gain + shift

def segment_ids(lengths, length):
    ends = jnp.cumsum(lengths, axis=-1).astype(jnp.int32)
    positions = jnp.arange(length, dtype=jnp.int32)
    return lax.optimization_barrier(jnp.sum((positions[None, :, None] >= ends[:, None, :]).astype(jnp.int32), axis=-1)).astype(jnp.int32)

def allowed(segs):
    length = segs.shape[0]
    positions = jnp.arange(length, dtype=jnp.int32)
    same = segs[None, :] == segs[:, None]
    causal = positions[None, :] <= positions[:, None]
    real = (segs[None, :] < NDOC) | (positions[None, :] == positions[:, None])
    return same & causal & real

def layer_apply(state, weights, segs):
    gains, shifts, in_w, in_b, out_w, up_w, up_b, down_w, branch_b = weights
    length = state.shape[0]
    normed = low(layer_norm(state, gains[0], shifts[0]))
    mixed = jnp.dot(normed, in_w.reshape(D, 3 * D), precision=highest)
    queries = low_back(low(mixed[:, :D] + in_b[0]))
    keys = low_back(low(mixed[:, D:2 * D]))
    values = low_back(low(mixed[:, 2 * D:] + in_b[1]))
    queries = queries.reshape(length, HEADS, HEAD).transpose(1, 0, 2)
    keys = keys.reshape(length, HEADS, HEAD).transpose(1, 0, 2)
    values = values.reshape(length, HEADS, HEAD).transpose(1, 0, 2)
    scores = low_back(jnp.einsum('hqd,hkd->hqk', queries, keys, precision=highest) * HEAD ** (-0.5))
    probs = jax.nn.softmax(jnp.where(allowed(segs)[None], scores, masked_score), axis=-1)
    attended = jnp.einsum('hqk,hkd->hqd', low(probs), values, precision=highest)
    attended = low_back(low(attended.transpose(1, 0, 2).reshape(length, D)))
    branch = low_back(jnp.dot(attended, out_w, precision=highest))
    middle = state + branch_scale * (branch + branch_b[0])
    upper = low(layer_norm(middle, gains[1], shifts[1]))
    pre = low_back(jnp.dot(upper, up_w, precision=highest) + up_b)
    hidden = low(jax.nn.gelu(pre, approximate=True))
    down = low_back(jnp.dot(hidden, down_w, precision=highest))
    return middle + branch_scale * (down + branch_b[1])

def reference(inputs, cotangent, lengths, norm_gains, norm_shifts, in_weight, in_bias, out_weight, up_weight, up_bias, down_weight, branch_bias):
    weights = tuple((item.astype(jnp.float32) for item in (norm_gains, norm_shifts, in_weight, in_bias, out_weight, up_weight, up_bias, down_weight, branch_bias)))
    states = inputs.astype(jnp.float32)
    segs = segment_ids(lengths, LENGTH)
    probes = jnp.zeros((ROWS, LAYERS, LENGTH, D), jnp.float32)

    def run(weights, probes):

        def row_step(carry, item):
            state, row_probes, row_segs = item
            finished = []
            for layer in range(LAYERS):
                layer_weights = tuple((entry[layer] for entry in weights))
                state = layer_apply(state + row_probes[layer], layer_weights, row_segs)
                if layer + 1 < LAYERS:
                    state = low(state)
                    finished.append(state)
                    state = low_back(state)
                else:
                    finished.append(state)
            return (carry, (state, jnp.stack(finished)))
        carry, (final, layer_outs) = lax.scan(jax.checkpoint(row_step), jnp.zeros((), jnp.float32), (states, probes, segs))
        return (final, layer_outs)
    final, back, layer_outs = jax.vjp(run, weights, probes, has_aux=True)
    grad_weights, grad_probes = back(cotangent.astype(jnp.float32))
    section_outputs = layer_outs.transpose(1, 0, 2, 3).astype(jnp.bfloat16)
    input_grads = grad_probes.transpose(1, 0, 2, 3)
    return (section_outputs, input_grads, grad_weights[0], grad_weights[1], grad_weights[2], grad_weights[3], grad_weights[4], grad_weights[5], grad_weights[6], grad_weights[7], grad_weights[8])
```

```python
from functools import partial

import jax
import jax.numpy as jnp
from jax import lax
from jax.experimental import pallas as pl
from jax.experimental.pallas import tpu as pltpu
from jax.sharding import PartitionSpec as P

HEAD = 64
branch_scale = 12.0 ** (-0.5)
norm_eps = 1e-05
masked_score = -1000000000.0
block = 256
cube = 0.044715
root = 0.7978845608

f32 = jnp.float32
bf16 = jnp.bfloat16


def mm(left, right):
    return jnp.dot(left, right, preferred_element_type=f32)


def mm_nt(left, right):
    return lax.dot_general(left, right, (((1,), (1,)), ((), ())), preferred_element_type=f32)


def mm_tn(left, right):
    return lax.dot_general(left, right, (((0,), (0,)), ((), ())), preferred_element_type=f32)


def normalize(values):
    mean = jnp.mean(values, axis=-1, keepdims=True)
    centred = values - mean
    spread = jnp.mean(centred * centred, axis=-1, keepdims=True)
    rstd = lax.rsqrt(spread + norm_eps)
    return centred * rstd, rstd


def norm_back(normal, rstd, grad, gain):
    scaled = grad * gain
    first = jnp.mean(scaled, axis=-1, keepdims=True)
    second = jnp.mean(scaled * normal, axis=-1, keepdims=True)
    return (scaled - first - normal * second) * rstd


def head_lanes(heads):
    found = []
    for head in range(heads):
        start = (head // 2) * 2 * HEAD
        width = min(2 * HEAD, heads * HEAD - start)
        found.append((start, width, head % 2))
    return found


def own_lanes(value, width, upper):
    if width == HEAD:
        return value
    lane = lax.broadcasted_iota(jnp.int32, value.shape, 1)
    keep = (lane >= HEAD) if upper else (lane < HEAD)
    return jnp.where(keep, value, jnp.zeros_like(value))


def block_mask(seg_col, seg_row, rows, count):
    same = seg_col[0:count, :] == seg_row[:, rows]
    key = lax.broadcasted_iota(jnp.int32, (count, rows.stop - rows.start), 0)
    query = lax.broadcasted_iota(jnp.int32, (count, rows.stop - rows.start), 1) + rows.start
    return same & (key <= query)


def attend_kernel(q_ref, k_ref, v_ref, seg_col, seg_row, out_ref, logsum_ref):
    length, width = q_ref.shape
    for start in range(0, length, block):
        rows = slice(start, start + block)
        count = start + block
        mask = block_mask(seg_col, seg_row, rows, count)
        mixed = []
        for head, (lane, lanes, upper) in enumerate(head_lanes(width // HEAD)):
            cols = slice(lane, lane + lanes)
            queries = own_lanes(q_ref[rows, cols], lanes, upper) * bf16(HEAD ** (-0.5))
            scores = mm_nt(k_ref[0:count, cols], queries)
            scores = jnp.where(mask, scores, masked_score)
            top = jnp.max(scores, axis=0, keepdims=True)
            weights = jnp.exp(scores - top)
            total = jnp.sum(weights, axis=0, keepdims=True)
            result = mm_tn(v_ref[0:count, cols], weights.astype(bf16)) / total
            logsum_ref[head : head + 1, rows] = top + jnp.log(total)
            mixed.append((lanes, result))
        for pair in range(0, len(mixed), 2):
            lane = pair * HEAD
            lanes, result = mixed[pair]
            if lanes > HEAD:
                result = jnp.concatenate([result[:HEAD], mixed[pair + 1][1][HEAD:]], axis=0)
            out_ref[rows, lane : lane + lanes] = result.T.astype(bf16)


def attend(q, k, v, seg_col, seg_row):
    length, width = q.shape
    return pl.pallas_call(
        attend_kernel,
        out_shape=(
            jax.ShapeDtypeStruct((length, width), bf16),
            jax.ShapeDtypeStruct((width // HEAD, length), f32),
        ),
        in_specs=[pl.BlockSpec(memory_space=pltpu.VMEM)] * 5,
        out_specs=[pl.BlockSpec(memory_space=pltpu.VMEM)] * 2,
        compiler_params=pltpu.CompilerParams(vmem_limit_bytes=40 * 2**20),
        name="attend",
    )(q, k, v, seg_col, seg_row)


def attend_back_kernel(
    q_ref, k_ref, v_ref, grad_ref, logsum_ref, seg_col, seg_row, dq_ref, dk_ref, dv_ref, dk_sum, dv_sum
):
    length, width = q_ref.shape
    dk_sum[...] = jnp.zeros_like(dk_sum)
    dv_sum[...] = jnp.zeros_like(dv_sum)
    scale = bf16(HEAD ** (-0.5))
    for start in range(0, length, block):
        rows = slice(start, start + block)
        count = start + block
        mask = block_mask(seg_col, seg_row, rows, count)
        mixed = []
        for head, (lane, lanes, upper) in enumerate(head_lanes(width // HEAD)):
            cols = slice(lane, lane + lanes)
            queries = own_lanes(q_ref[rows, cols], lanes, upper) * scale
            grads = own_lanes(grad_ref[rows, cols], lanes, upper)
            keys = k_ref[0:count, cols]
            scores = mm_nt(keys, queries)
            scores = jnp.where(mask, scores, masked_score)
            probs = jnp.exp(scores - logsum_ref[head : head + 1, rows])
            grad_probs = mm_nt(v_ref[0:count, cols], grads)
            dv_sum[0:count, cols] += mm(probs.astype(bf16), grads)
            term = probs * grad_probs
            delta = jnp.sum(term, axis=0, keepdims=True)
            grad_scores = (term - probs * delta).astype(bf16)
            dk_sum[0:count, cols] += mm(grad_scores, queries)
            mixed.append((lanes, mm_tn(keys, grad_scores)))
        for pair in range(0, len(mixed), 2):
            lane = pair * HEAD
            lanes, result = mixed[pair]
            if lanes > HEAD:
                result = jnp.concatenate([result[:HEAD], mixed[pair + 1][1][HEAD:]], axis=0)
            dq_ref[rows, lane : lane + lanes] = (result.T * HEAD ** (-0.5)).astype(bf16)
    dk_ref[...] = dk_sum[...].astype(bf16)
    dv_ref[...] = dv_sum[...].astype(bf16)


def attend_back(q, k, v, grad, logsum, seg_col, seg_row):
    length, width = q.shape
    like = jax.ShapeDtypeStruct((length, width), bf16)
    return pl.pallas_call(
        attend_back_kernel,
        out_shape=(like, like, like),
        in_specs=[pl.BlockSpec(memory_space=pltpu.VMEM)] * 7,
        out_specs=[pl.BlockSpec(memory_space=pltpu.VMEM)] * 3,
        scratch_shapes=[pltpu.VMEM((length, width), f32)] * 2,
        compiler_params=pltpu.CompilerParams(vmem_limit_bytes=40 * 2**20),
        name="attend_back",
    )(q, k, v, grad, logsum, seg_col, seg_row)


def segment_ids(lengths, length):
    ends = jnp.cumsum(lengths)
    positions = jnp.arange(length, dtype=jnp.int32)
    segs = jnp.sum((positions[:, None] >= ends[None, :]).astype(jnp.int32), axis=-1)
    docs = lengths.shape[0]
    return jnp.where(segs < docs, segs, docs + positions)


def per_device(
    inputs,
    cotangent,
    lengths,
    norm_gains,
    norm_shifts,
    in_weight,
    in_bias,
    out_weight,
    up_weight,
    up_bias,
    down_weight,
    branch_bias,
):
    core = lax.axis_index("section")
    z = lax.axis_index("mp")
    dp = lax.axis_index("dp")
    copies = lax.axis_size("dp")
    mine = z // 2
    side = z % 2
    quarter, width = inputs.shape[1:]
    half = 2 * quarter
    length = 4 * quarter
    local = in_weight.shape[3]
    units = up_weight.shape[2]

    def at(c, m):
        return c * 4 + m

    every = [(c, m) for c in range(2) for m in range(4)]

    def route(value, pairs):
        return lax.ppermute(value, ("section", "mp"), pairs)

    swap_core = [(at(c, m), at(1 - c, m)) for c, m in every]
    swap_side = [(at(c, m), at(c, m ^ 1)) for c, m in every]
    swap_pair = [(at(c, m), at(c, m ^ 2)) for c, m in every]

    def pick(flag, yes, no):
        return jnp.where(flag, yes, no)

    def rows_in(array):
        pairs = [(at(c, m), at(c, m ^ 2)) for c, m in every if c == m // 2]
        far = route(pick(mine == 0, array[1], array[0]), pairs)
        here = pick(core == mine, pick(mine == 0, array[0], array[1]), far)
        there = route(here, swap_side)
        return pick(
            side == 0,
            jnp.concatenate([here, there], axis=0),
            jnp.concatenate([there, here], axis=0),
        )

    def fetch(array):
        part = array.shape[0] // copies
        piece = lax.dynamic_slice_in_dim(array, dp * part, part, 0)
        piece = route(piece, swap_pair)
        return lax.all_gather(piece, "dp", axis=0, tiled=True)

    def both_layers(array):
        other = route(array, swap_core)
        return [pick(core == layer, array, other) for layer in range(2)]

    mixing = in_weight[0].reshape(width, 3 * local)
    in_own, in_far = both_layers(mixing), both_layers(fetch(mixing))
    out_own, out_far = both_layers(out_weight[0]), both_layers(fetch(out_weight[0]))
    up_own, up_far = both_layers(up_weight[0]), both_layers(fetch(up_weight[0]))
    down_own, down_far = both_layers(down_weight[0]), both_layers(fetch(down_weight[0]))
    shard_vec = jnp.concatenate([in_bias[0].reshape(-1), up_bias[0]])
    far_vec = route(shard_vec, swap_pair)
    whole_vec = jnp.concatenate(
        [norm_gains[0].reshape(-1), norm_shifts[0].reshape(-1), branch_bias[0].reshape(-1)]
    )
    vecs = both_layers(jnp.concatenate([shard_vec, far_vec, whole_vec]))

    def unpack(vec):
        found = []
        at_ = 0
        for size, shape in (
            (2 * local, (2, local)),
            (units, (units,)),
            (2 * local, (2, local)),
            (units, (units,)),
            (2 * width, (2, width)),
            (2 * width, (2, width)),
            (2 * width, (2, width)),
        ):
            found.append(vec[at_ : at_ + size].reshape(shape))
            at_ += size
        return found

    row_lengths = pick(mine == 0, lengths[0], lengths[1])
    segs = segment_ids(row_lengths, length)
    seg_col, seg_row = segs[:, None], segs[None, :]

    def to_heads(packed):
        keep = pick(core == 0, packed[0], packed[1])
        give = pick(core == 0, packed[1], packed[0])
        got = route(give, swap_core)
        return pick(
            core == 0,
            jnp.concatenate([keep, got], axis=0),
            jnp.concatenate([got, keep], axis=0),
        )

    def to_tokens(whole):
        keep = lax.dynamic_slice_in_dim(whole, core * half, half, 0)
        give = lax.dynamic_slice_in_dim(whole, (1 - core) * half, half, 0)
        got = route(give, swap_core)
        return pick(core == 0, jnp.stack([keep, got]), jnp.stack([got, keep]))

    def pair_sum(partial_sum):
        low = partial_sum.astype(bf16)
        return low.astype(f32) + route(low, swap_side).astype(f32)

    state = rows_in(inputs)
    grad = rows_in(cotangent).astype(f32)
    saved = []
    outputs = []
    for layer in range(2):
        bias_own, up_b_own, bias_far, up_b_far, gains, shifts, branch = unpack(vecs[layer])
        w_in = (in_own[layer], in_far[layer])
        zero = jnp.zeros((local,), f32)
        qkv_bias = [jnp.concatenate([b[0], zero, b[1]]) for b in (bias_own, bias_far)]
        start = state.astype(f32)
        normal, rstd = normalize(start)
        normed = (normal * gains[0] + shifts[0]).astype(bf16)
        packed = jnp.stack([(mm(normed, w_in[k]) + qkv_bias[k]).astype(bf16) for k in range(2)])
        heads = to_heads(packed)
        q, k, v = (heads[:, j * local : (j + 1) * local] for j in range(3))
        mixed, logsum = attend(q, k, v, seg_col, seg_row)
        attended = to_tokens(mixed)
        part = mm(attended[0], out_own[layer]) + mm(attended[1], out_far[layer])
        middle = start + branch_scale * (pair_sum(part) + branch[0])
        normal2, rstd2 = normalize(middle)
        upper = (normal2 * gains[1] + shifts[1]).astype(bf16)
        hidden, slope = [], []
        for w, b in ((up_own[layer], up_b_own), (up_far[layer], up_b_far)):
            pre = mm(upper, w) + b
            curve = jnp.tanh(root * (pre + cube * pre * pre * pre))
            hidden.append((0.5 * pre * (1.0 + curve)).astype(bf16))
            slope.append(
                (
                    0.5 * (1.0 + curve)
                    + 0.5 * pre * (1.0 - curve * curve) * root * (1.0 + 3.0 * cube * pre * pre)
                ).astype(bf16)
            )
        part = mm(hidden[0], down_own[layer]) + mm(hidden[1], down_far[layer])
        result = middle + branch_scale * (pair_sum(part) + branch[1])
        saved.append((start, normed, q, k, v, logsum, attended, middle, upper, hidden, slope))
        state = result.astype(bf16)
        outputs.append(state)

    partials = [None, None]
    vectors = [None, None]
    grads_out = [None, None]
    for layer in (1, 0):
        start, normed, q, k, v, logsum, attended, middle, upper, hidden, slope = saved[layer]
        bias_own, up_b_own, bias_far, up_b_far, gains, shifts, branch = unpack(vecs[layer])
        gz = branch_scale * grad
        d_branch1 = jnp.sum(gz, axis=0)
        gz = gz.astype(bf16)
        d_pre, d_up, d_down, d_up_bias = [], [], [], []
        for i, w in enumerate((down_own[layer], down_far[layer])):
            dp_ = (mm_nt(gz, w) * slope[i].astype(f32)).astype(bf16)
            d_pre.append(dp_)
            d_down.append(mm_tn(hidden[i], gz).astype(bf16))
            d_up.append(mm_tn(upper, dp_).astype(bf16))
            d_up_bias.append(jnp.sum(dp_.astype(f32), axis=0))
        part = mm_nt(d_pre[0], up_own[layer]) + mm_nt(d_pre[1], up_far[layer])
        d_upper = pair_sum(part)
        normal2, rstd2 = normalize(middle)
        d_gain1 = jnp.sum(d_upper * normal2, axis=0)
        d_shift1 = jnp.sum(d_upper, axis=0)
        d_middle = grad + norm_back(normal2, rstd2, d_upper, gains[1])
        gy = branch_scale * d_middle
        d_branch0 = jnp.sum(gy, axis=0)
        gy = gy.astype(bf16)
        d_out = [mm_tn(attended[i], gy).astype(bf16) for i in range(2)]
        d_att = jnp.stack(
            [mm_nt(gy, w).astype(bf16) for w in (out_own[layer], out_far[layer])]
        )
        d_heads = to_heads(d_att)
        dq, dk, dv = attend_back(q, k, v, d_heads, logsum, seg_col, seg_row)
        d_mix = to_tokens(jnp.concatenate([dq, dk, dv], axis=1))
        d_in = [mm_tn(normed, d_mix[i]).astype(bf16) for i in range(2)]
        d_mix_sum = jnp.sum(d_mix.astype(f32), axis=1)
        part = mm_nt(d_mix[0], in_own[layer]) + mm_nt(d_mix[1], in_far[layer])
        d_normed = pair_sum(part)
        normal, rstd = normalize(start)
        d_gain0 = jnp.sum(d_normed * normal, axis=0)
        d_shift0 = jnp.sum(d_normed, axis=0)
        d_state = d_middle + norm_back(normal, rstd, d_normed, gains[0])
        low = d_state.astype(bf16)
        grads_out[layer] = low
        grad = low.astype(f32)
        partials[layer] = (d_in, d_out, d_up, d_down)
        shard_terms = [
            jnp.concatenate([d_mix_sum[i, :local], d_mix_sum[i, 2 * local :], d_up_bias[i]])
            for i in range(2)
        ]
        vectors[layer] = (
            shard_terms,
            jnp.concatenate([d_gain0, d_gain1, d_shift0, d_shift1, d_branch0, d_branch1]),
        )

    def reduce_layer(index, layer):
        own, far = partials[layer][index]
        got = route(pick(core == 0, far, own), swap_core)
        total = (pick(core == 0, own, far).astype(f32) + got.astype(f32)).astype(bf16)
        piece = lax.psum_scatter(total, "dp", scatter_dimension=0, tiled=True)
        cross = route(piece, [(at(1, m), at(0, m ^ 2)) for m in range(4)])
        return piece + cross

    final = []
    for index in range(4):
        first = reduce_layer(index, 0)
        second = reduce_layer(index, 1)
        second = route(second, [(at(0, m), at(1, m)) for m in range(4)])
        final.append(lax.all_gather(pick(core == 0, first, second), "dp", axis=0, tiled=True).astype(f32))
    g_in, g_out, g_up, g_down = final

    shard_sum, whole_sum = [], []
    for layer in range(2):
        (own, far), whole = vectors[layer]
        shard_sum.append(jnp.stack([own, far]))
        whole_sum.append(whole)
    shard_sum = jnp.stack(shard_sum)
    across = route(shard_sum[:, 1], swap_pair)
    shard_sum = lax.psum(shard_sum[:, 0] + across, ("section", "dp"))
    whole_sum = lax.psum(jnp.stack(whole_sum), ("section", "mp", "dp")) * 0.5
    shard_mine = pick(core == 0, shard_sum[0], shard_sum[1])
    whole_mine = pick(core == 0, whole_sum[0], whole_sum[1]).reshape(3, 2, width)

    def rows_out(pair):
        both = jnp.stack(pair)
        send = lax.dynamic_slice_in_dim(both, side * quarter, quarter, 1)
        far = route(send, [(at(c, m), at(c, m ^ 2)) for c, m in every if c != m // 2])
        rows = pick(mine == 0, jnp.stack([send, far], 1), jnp.stack([far, send], 1))
        other = route(
            pick(mine == 0, rows[1], rows[0]),
            [(at(c, m), at(1 - c, m)) for c, m in every if c == m // 2],
        )
        here = pick(core == 0, rows[0], rows[1])
        return pick(core == mine, here, other)

    section_outputs = rows_out(outputs)
    input_grads = rows_out(grads_out).astype(f32)
    return (
        section_outputs[None],
        input_grads[None],
        whole_mine[0][None],
        whole_mine[1][None],
        g_in.reshape(1, width, 3, local),
        shard_mine[: 2 * local].reshape(1, 2, local),
        g_out[None],
        g_up[None],
        shard_mine[2 * local :][None],
        g_down[None],
        whole_mine[2][None],
    )


def solution(mesh):
    in_specs = (
        P("dp", "mp", None),
        P("dp", "mp", None),
        P("dp", None),
        P("section", None, None),
        P("section", None, None),
        P("section", None, None, "mp"),
        P("section", None, "mp"),
        P("section", "mp", None),
        P("section", None, "mp"),
        P("section", "mp"),
        P("section", "mp", None),
        P("section", None, None),
    )
    out_specs = (
        P("section", "dp", "mp", None),
        P("section", "dp", "mp", None),
        P("section", None, None),
        P("section", None, None),
        P("section", None, None, "mp"),
        P("section", None, "mp"),
        P("section", "mp", None),
        P("section", None, "mp"),
        P("section", "mp"),
        P("section", "mp", None),
        P("section", None, None),
    )
    return jax.shard_map(
        per_device, mesh=mesh, in_specs=in_specs, out_specs=out_specs, check_vma=False
    )
```

```python
from functools import partial

import jax
import jax.numpy as jnp
from jax import lax
from jax.experimental import pallas as pl
from jax.experimental.pallas import tpu as pltpu
from jax.sharding import PartitionSpec as P

HEAD = 64
branch_scale = 12.0 ** (-0.5)
norm_eps = 1e-05
masked_score = -1000000000.0
block = 256
cube = 0.044715
root = 0.7978845608

f32 = jnp.float32
bf16 = jnp.bfloat16


def mm(left, right):
    return jnp.dot(left, right, preferred_element_type=f32)


def mm_nt(left, right):
    return lax.dot_general(left, right, (((1,), (1,)), ((), ())), preferred_element_type=f32)


def mm_tn(left, right):
    return lax.dot_general(left, right, (((0,), (0,)), ((), ())), preferred_element_type=f32)


def normalize(values):
    mean = jnp.mean(values, axis=-1, keepdims=True)
    centred = values - mean
    spread = jnp.mean(centred * centred, axis=-1, keepdims=True)
    rstd = lax.rsqrt(spread + norm_eps)
    return centred * rstd, rstd


def norm_back(normal, rstd, grad, gain):
    scaled = grad * gain
    first = jnp.mean(scaled, axis=-1, keepdims=True)
    second = jnp.mean(scaled * normal, axis=-1, keepdims=True)
    return (scaled - first - normal * second) * rstd


def head_lanes(heads):
    found = []
    for head in range(heads):
        start = (head // 2) * 2 * HEAD
        width = min(2 * HEAD, heads * HEAD - start)
        found.append((start, width, head % 2))
    return found


def own_lanes(value, width, upper):
    if width == HEAD:
        return value
    lane = lax.broadcasted_iota(jnp.int32, value.shape, 1)
    keep = (lane >= HEAD) if upper else (lane < HEAD)
    return jnp.where(keep, value, jnp.zeros_like(value))


def block_mask(seg_col, seg_row, rows, count):
    same = seg_col[0:count, :] == seg_row[:, rows]
    key = lax.broadcasted_iota(jnp.int32, (count, rows.stop - rows.start), 0)
    query = lax.broadcasted_iota(jnp.int32, (count, rows.stop - rows.start), 1) + rows.start
    return same & (key <= query)


def attend_back_kernel(
    q_ref, k_ref, v_ref, grad_ref, logsum_ref, seg_col, seg_row, dq_ref, dk_ref, dv_ref, dk_sum, dv_sum
):
    length, width = q_ref.shape
    dk_sum[...] = jnp.zeros_like(dk_sum)
    dv_sum[...] = jnp.zeros_like(dv_sum)
    scale = bf16(HEAD ** (-0.5))
    for start in range(0, length, block):
        rows = slice(start, start + block)
        count = start + block
        mask = block_mask(seg_col, seg_row, rows, count)
        mixed = []
        for head, (lane, lanes, upper) in enumerate(head_lanes(width // HEAD)):
            cols = slice(lane, lane + lanes)
            queries = own_lanes(q_ref[rows, cols], lanes, upper) * scale
            grads = own_lanes(grad_ref[rows, cols], lanes, upper)
            keys = k_ref[0:count, cols]
            scores = mm_nt(keys, queries)
            scores = jnp.where(mask, scores, masked_score)
            probs = jnp.exp(scores - logsum_ref[head : head + 1, rows])
            grad_probs = mm_nt(v_ref[0:count, cols], grads)
            dv_sum[0:count, cols] += mm(probs.astype(bf16), grads)
            term = probs * grad_probs
            delta = jnp.sum(term, axis=0, keepdims=True)
            grad_scores = (term - probs * delta).astype(bf16)
            dk_sum[0:count, cols] += mm(grad_scores, queries)
            mixed.append((lanes, mm_tn(keys, grad_scores)))
        for pair in range(0, len(mixed), 2):
            lane = pair * HEAD
            lanes, result = mixed[pair]
            if lanes > HEAD:
                result = jnp.concatenate([result[:HEAD], mixed[pair + 1][1][HEAD:]], axis=0)
            dq_ref[rows, lane : lane + lanes] = (result.T * HEAD ** (-0.5)).astype(bf16)
    dk_ref[...] = dk_sum[...].astype(bf16)
    dv_ref[...] = dv_sum[...].astype(bf16)


def attend_back(q, k, v, grad, logsum, seg_col, seg_row):
    length, width = q.shape
    like = jax.ShapeDtypeStruct((length, width), bf16)
    return pl.pallas_call(
        attend_back_kernel,
        out_shape=(like, like, like),
        in_specs=[pl.BlockSpec(memory_space=pltpu.VMEM)] * 7,
        out_specs=[pl.BlockSpec(memory_space=pltpu.VMEM)] * 3,
        scratch_shapes=[pltpu.VMEM((length, width), f32)] * 2,
        compiler_params=pltpu.CompilerParams(vmem_limit_bytes=40 * 2**20),
        name="attend_back",
    )(q, k, v, grad, logsum, seg_col, seg_row)


MESH = pl.DeviceIdType.MESH


def send(src, dst, sems, index, device):
    return pltpu.make_async_remote_copy(
        src_ref=src,
        dst_ref=dst,
        send_sem=sems.at[0, index],
        recv_sem=sems.at[1, index],
        device_id=device,
        device_id_type=MESH,
    )


def attend_block(qkv_ref, mask, rows, count, logsum_ref):
    heads = qkv_ref.shape[2] // HEAD
    mixed = []
    for head, (lane, lanes, upper) in enumerate(head_lanes(heads)):
        cols = slice(lane, lane + lanes)
        queries = own_lanes(qkv_ref[0, rows, cols], lanes, upper) * bf16(HEAD ** (-0.5))
        scores = mm_nt(qkv_ref[1, 0:count, cols], queries)
        scores = jnp.where(mask, scores, masked_score)
        top = jnp.max(scores, axis=0, keepdims=True)
        weights = jnp.exp(scores - top)
        total = jnp.sum(weights, axis=0, keepdims=True)
        result = mm_tn(qkv_ref[2, 0:count, cols], weights.astype(bf16)) / total
        logsum_ref[head : head + 1, rows] = top + jnp.log(total)
        mixed.append((lanes, result))
    found = []
    for pair in range(0, heads, 2):
        lanes, result = mixed[pair]
        if lanes > HEAD:
            result = jnp.concatenate([result[:HEAD], mixed[pair + 1][1][HEAD:]], axis=0)
        found.append((pair * HEAD, lanes, result.T.astype(bf16)))
    return found


def forward_kernel(
    state_ref,
    w_in,
    w_out,
    w_up,
    w_down,
    b_in,
    b_up,
    vec_ref,
    seg_col,
    seg_row,
    out_ref,
    normed_ref,
    qkv_ref,
    logsum_ref,
    att_ref,
    middle_ref,
    upper_ref,
    hidden_ref,
    slope_ref,
    qkv_out,
    att_out,
    low,
    got,
    qkv_sems,
    att_sems,
    pair_sems,
):
    core = lax.axis_index("section")
    z = lax.axis_index("mp")
    dp = lax.axis_index("dp")
    sibling = (1 - core, z, dp)
    partner = (core, z + 1 - 2 * lax.rem(z, 2), dp)
    barrier = pltpu.get_barrier_semaphore()
    for device in (sibling, partner):
        pl.semaphore_signal(barrier, inc=1, device_id=device, device_id_type=MESH)
    pl.semaphore_wait(barrier, 2)

    half = state_ref.shape[0]
    blocks = half // block
    first = pl.multiple_of(core * half, half)

    copies = []
    for j in range(blocks):
        rows = slice(j * block, (j + 1) * block)
        normal, _ = normalize(state_ref[rows, :].astype(f32))
        normed = (normal * vec_ref[0:1, :] + vec_ref[2:3, :]).astype(bf16)
        normed_ref[rows, :] = normed
        for part in range(3):
            qkv_out[j, part] = (mm(normed, w_in[1 - core, part]) + b_in[1 - core, part]).astype(bf16)
        there = pl.ds(pl.multiple_of(first + j * block, block), block)
        copy = send(qkv_out.at[j], qkv_ref.at[:, there, :], qkv_sems, j, sibling)
        copy.start()
        copies.append(copy)
        for part in range(3):
            qkv_ref[part, there, :] = (mm(normed, w_in[core, part]) + b_in[core, part]).astype(bf16)
    for copy in copies:
        copy.wait()

    def send_low(index, rows, value):
        low[index, rows, :] = value.astype(bf16)
        copy = send(low.at[index, rows], got.at[index, rows], pair_sems, index * blocks + rows.start // block, partner)
        copy.start()

    def received(index, rows):
        copy = send(low.at[index, rows], got.at[index, rows], pair_sems, index * blocks + rows.start // block, partner)
        copy.wait()
        return low[index, rows, :].astype(f32) + got[index, rows, :].astype(f32)

    for i in range(2 * blocks):
        owner, j = i // blocks, i % blocks
        rows = slice(i * block, (i + 1) * block)
        own = slice(j * block, (j + 1) * block)
        count = (i + 1) * block
        mask = block_mask(seg_col, seg_row, rows, count)
        found = attend_block(qkv_ref, mask, rows, count, logsum_ref)
        copy = send(att_out.at[j], att_ref.at[core, own], att_sems, j, sibling)

        @pl.when(core == owner)
        def _():
            for lane, lanes, result in found:
                att_ref[core, own, lane : lane + lanes] = result
            copy.wait_recv()
            send_low(0, own, mm(att_ref[0, own, :], w_out[0]) + mm(att_ref[1, own, :], w_out[1]))

        @pl.when(core != owner)
        def _():
            for lane, lanes, result in found:
                att_out[j, :, lane : lane + lanes] = result
            copy.start()

    for j in range(blocks):
        own = slice(j * block, (j + 1) * block)
        send(att_out.at[j], att_ref.at[core, own], att_sems, j, sibling).wait_send()

    for j in range(blocks):
        rows = slice(j * block, (j + 1) * block)
        middle = state_ref[rows, :].astype(f32) + branch_scale * (received(0, rows) + vec_ref[4:5, :])
        middle_ref[rows, :] = middle
        normal, _ = normalize(middle)
        upper = (normal * vec_ref[1:2, :] + vec_ref[3:4, :]).astype(bf16)
        upper_ref[rows, :] = upper
        total = None
        for k in range(2):
            pre = mm(upper, w_up[k]) + b_up[k]
            square = pre * pre
            curve = jnp.tanh(root * pre * (1.0 + cube * square))
            rise = 0.5 * (1.0 + curve)
            hidden = (pre * rise).astype(bf16)
            hidden_ref[k, rows, :] = hidden
            slope = rise + pre * (rise * (1.0 - curve)) * (root * (1.0 + 3.0 * cube * square))
            slope_ref[k, rows, :] = slope.astype(bf16)
            term = mm(hidden, w_down[k])
            total = term if total is None else total + term
        send_low(1, rows, total)

    for j in range(blocks):
        rows = slice(j * block, (j + 1) * block)
        result = middle_ref[rows, :] + branch_scale * (received(1, rows) + vec_ref[5:6, :])
        out_ref[rows, :] = result.astype(bf16)


def forward_layer(state, w_in, w_out, w_up, w_down, b_in, b_up, vec, seg_col, seg_row):
    half, width = state.shape
    length = seg_col.shape[0]
    local = w_in.shape[3]
    units = w_up.shape[2]
    blocks = half // block
    vmem = pl.BlockSpec(memory_space=pltpu.VMEM)
    shape = jax.ShapeDtypeStruct
    return pl.pallas_call(
        forward_kernel,
        out_shape=(
            shape((half, width), bf16),
            shape((half, width), bf16),
            shape((3, length, local), bf16),
            shape((local // HEAD, length), f32),
            shape((2, half, local), bf16),
            shape((half, width), f32),
            shape((half, width), bf16),
            shape((2, half, units), bf16),
            shape((2, half, units), bf16),
        ),
        in_specs=[vmem] * 10,
        out_specs=[vmem] * 9,
        scratch_shapes=[
            pltpu.VMEM((blocks, 3, block, local), bf16),
            pltpu.VMEM((blocks, block, local), bf16),
            pltpu.VMEM((2, half, width), bf16),
            pltpu.VMEM((2, half, width), bf16),
            pltpu.SemaphoreType.DMA((2, blocks)),
            pltpu.SemaphoreType.DMA((2, blocks)),
            pltpu.SemaphoreType.DMA((2, 2 * blocks)),
        ],
        compiler_params=pltpu.CompilerParams(
            vmem_limit_bytes=50 * 2**20, collective_id=1, has_side_effects=True
        ),
        name="forward_layer",
    )(state, w_in, w_out, w_up, w_down, b_in, b_up, vec, seg_col, seg_row)


def segment_ids(lengths, length):
    ends = jnp.cumsum(lengths)
    positions = jnp.arange(length, dtype=jnp.int32)
    segs = jnp.sum((positions[:, None] >= ends[None, :]).astype(jnp.int32), axis=-1)
    docs = lengths.shape[0]
    return jnp.where(segs < docs, segs, docs + positions)


def per_device(
    inputs,
    cotangent,
    lengths,
    norm_gains,
    norm_shifts,
    in_weight,
    in_bias,
    out_weight,
    up_weight,
    up_bias,
    down_weight,
    branch_bias,
):
    core = lax.axis_index("section")
    z = lax.axis_index("mp")
    dp = lax.axis_index("dp")
    copies = lax.axis_size("dp")
    mine = z // 2
    side = z % 2
    quarter, width = inputs.shape[1:]
    half = 2 * quarter
    length = 4 * quarter
    local = in_weight.shape[3]
    units = up_weight.shape[2]

    def at(c, m):
        return c * 4 + m

    every = [(c, m) for c in range(2) for m in range(4)]

    def route(value, pairs):
        return lax.ppermute(value, ("section", "mp"), pairs)

    swap_core = [(at(c, m), at(1 - c, m)) for c, m in every]
    swap_side = [(at(c, m), at(c, m ^ 1)) for c, m in every]
    swap_pair = [(at(c, m), at(c, m ^ 2)) for c, m in every]

    def pick(flag, yes, no):
        return jnp.where(flag, yes, no)

    def rows_in(array):
        pairs = [(at(c, m), at(c, m ^ 2)) for c, m in every if c == m // 2]
        far = route(pick(mine == 0, array[1], array[0]), pairs)
        here = pick(core == mine, pick(mine == 0, array[0], array[1]), far)
        there = route(here, swap_side)
        return pick(
            side == 0,
            jnp.concatenate([here, there], axis=0),
            jnp.concatenate([there, here], axis=0),
        )

    def fetch(array, axis):
        part = array.shape[axis] // copies
        piece = lax.dynamic_slice_in_dim(array, dp * part, part, axis)
        piece = route(piece, swap_pair)
        return lax.all_gather(piece, "dp", axis=axis, tiled=True)

    def both_layers(array):
        other = route(array, swap_core)
        return [pick(core == layer, array, other) for layer in range(2)]

    mixing = in_weight[0].transpose(1, 0, 2)

    def slots(array, axis):
        far = fetch(array, axis)
        return [jnp.stack(pair) for pair in zip(both_layers(array), both_layers(far))]

    w_in = slots(mixing, 1)
    w_out = slots(out_weight[0], 0)
    w_up = slots(up_weight[0], 0)
    w_down = slots(down_weight[0], 0)
    shard_vec = jnp.concatenate([in_bias[0].reshape(-1), up_bias[0]])
    far_vec = route(shard_vec, swap_pair)
    whole_vec = jnp.concatenate(
        [norm_gains[0].reshape(-1), norm_shifts[0].reshape(-1), branch_bias[0].reshape(-1)]
    )
    vecs = both_layers(jnp.concatenate([shard_vec, far_vec, whole_vec]))

    def unpack(vec):
        found = []
        at_ = 0
        for size, shape in (
            (2 * local, (2, local)),
            (units, (units,)),
            (2 * local, (2, local)),
            (units, (units,)),
            (2 * width, (2, width)),
            (2 * width, (2, width)),
            (2 * width, (2, width)),
        ):
            found.append(vec[at_ : at_ + size].reshape(shape))
            at_ += size
        return found

    row_lengths = pick(mine == 0, lengths[0], lengths[1])
    segs = segment_ids(row_lengths, length)
    seg_col, seg_row = segs[:, None], segs[None, :]

    def to_heads(packed):
        keep = pick(core == 0, packed[0], packed[1])
        give = pick(core == 0, packed[1], packed[0])
        got = route(give, swap_core)
        return pick(
            core == 0,
            jnp.concatenate([keep, got], axis=0),
            jnp.concatenate([got, keep], axis=0),
        )

    def to_tokens(whole):
        keep = lax.dynamic_slice_in_dim(whole, core * half, half, 0)
        give = lax.dynamic_slice_in_dim(whole, (1 - core) * half, half, 0)
        got = route(give, swap_core)
        return pick(core == 0, jnp.stack([keep, got]), jnp.stack([got, keep]))

    def pair_sum(partial_sum):
        low = partial_sum.astype(bf16)
        return low.astype(f32) + route(low, swap_side).astype(f32)

    state = rows_in(inputs)
    grad = rows_in(cotangent).astype(f32)
    saved = []
    outputs = []
    for layer in range(2):
        bias_own, up_b_own, bias_far, up_b_far, gains, shifts, branch = unpack(vecs[layer])
        zero = jnp.zeros((local,), f32)
        b_in = jnp.stack([jnp.stack([b[0], zero, b[1]]) for b in (bias_own, bias_far)])[:, :, None]
        b_up = jnp.stack([up_b_own, up_b_far])[:, None]
        vec = jnp.concatenate([gains, shifts, branch], axis=0)
        start = state
        state, *kept = forward_layer(
            state, w_in[layer], w_out[layer], w_up[layer], w_down[layer], b_in, b_up, vec, seg_col, seg_row
        )
        saved.append((start, *kept))
        outputs.append(state)

    partials = [None, None]
    vectors = [None, None]
    grads_out = [None, None]
    for layer in (1, 0):
        start, normed, qkv, logsum, attended, middle, upper, hidden, slope = saved[layer]
        q, k, v = qkv[0], qkv[1], qkv[2]
        start = start.astype(f32)
        bias_own, up_b_own, bias_far, up_b_far, gains, shifts, branch = unpack(vecs[layer])
        gz = branch_scale * grad
        d_branch1 = jnp.sum(gz, axis=0)
        gz = gz.astype(bf16)
        d_pre, d_up, d_down, d_up_bias = [], [], [], []
        for i, w in enumerate(w_down[layer]):
            dp_ = (mm_nt(gz, w) * slope[i].astype(f32)).astype(bf16)
            d_pre.append(dp_)
            d_down.append(mm_tn(hidden[i], gz).astype(bf16))
            d_up.append(mm_tn(upper, dp_).astype(bf16))
            d_up_bias.append(jnp.sum(dp_.astype(f32), axis=0))
        part = mm_nt(d_pre[0], w_up[layer][0]) + mm_nt(d_pre[1], w_up[layer][1])
        d_upper = pair_sum(part)
        normal2, rstd2 = normalize(middle)
        d_gain1 = jnp.sum(d_upper * normal2, axis=0)
        d_shift1 = jnp.sum(d_upper, axis=0)
        d_middle = grad + norm_back(normal2, rstd2, d_upper, gains[1])
        gy = branch_scale * d_middle
        d_branch0 = jnp.sum(gy, axis=0)
        gy = gy.astype(bf16)
        d_out = [mm_tn(attended[i], gy).astype(bf16) for i in range(2)]
        d_att = jnp.stack(
            [mm_nt(gy, w).astype(bf16) for w in w_out[layer]]
        )
        d_heads = to_heads(d_att)
        dq, dk, dv = attend_back(q, k, v, d_heads, logsum, seg_col, seg_row)
        d_mix = to_tokens(jnp.concatenate([dq, dk, dv], axis=1))
        d_in = [jnp.stack([mm_tn(normed, d_mix[i][:, j * local : (j + 1) * local]).astype(bf16) for j in range(3)]) for i in range(2)]
        d_mix_sum = jnp.sum(d_mix.astype(f32), axis=1)
        part = sum(mm_nt(d_mix[i][:, j * local : (j + 1) * local], w_in[layer][i, j]) for i in range(2) for j in range(3))
        d_normed = pair_sum(part)
        normal, rstd = normalize(start)
        d_gain0 = jnp.sum(d_normed * normal, axis=0)
        d_shift0 = jnp.sum(d_normed, axis=0)
        d_state = d_middle + norm_back(normal, rstd, d_normed, gains[0])
        low = d_state.astype(bf16)
        grads_out[layer] = low
        grad = low.astype(f32)
        partials[layer] = (d_in, d_out, d_up, d_down)
        shard_terms = [
            jnp.concatenate([d_mix_sum[i, :local], d_mix_sum[i, 2 * local :], d_up_bias[i]])
            for i in range(2)
        ]
        vectors[layer] = (
            shard_terms,
            jnp.concatenate([d_gain0, d_gain1, d_shift0, d_shift1, d_branch0, d_branch1]),
        )

    def reduce_layer(index, layer):
        own, far = partials[layer][index]
        got = route(pick(core == 0, far, own), swap_core)
        total = (pick(core == 0, own, far).astype(f32) + got.astype(f32)).astype(bf16)
        piece = lax.psum_scatter(total, "dp", scatter_dimension=total.ndim - 2, tiled=True)
        cross = route(piece, [(at(1, m), at(0, m ^ 2)) for m in range(4)])
        return piece + cross

    final = []
    for index in range(4):
        first = reduce_layer(index, 0)
        second = reduce_layer(index, 1)
        second = route(second, [(at(0, m), at(1, m)) for m in range(4)])
        final.append(lax.all_gather(pick(core == 0, first, second), "dp", axis=first.ndim - 2, tiled=True).astype(f32))
    g_in, g_out, g_up, g_down = final

    shard_sum, whole_sum = [], []
    for layer in range(2):
        (own, far), whole = vectors[layer]
        shard_sum.append(jnp.stack([own, far]))
        whole_sum.append(whole)
    shard_sum = jnp.stack(shard_sum)
    across = route(shard_sum[:, 1], swap_pair)
    shard_sum = lax.psum(shard_sum[:, 0] + across, ("section", "dp"))
    whole_sum = lax.psum(jnp.stack(whole_sum), ("section", "mp", "dp")) * 0.5
    shard_mine = pick(core == 0, shard_sum[0], shard_sum[1])
    whole_mine = pick(core == 0, whole_sum[0], whole_sum[1]).reshape(3, 2, width)

    def rows_out(pair):
        both = jnp.stack(pair)
        send = lax.dynamic_slice_in_dim(both, side * quarter, quarter, 1)
        far = route(send, [(at(c, m), at(c, m ^ 2)) for c, m in every if c != m // 2])
        rows = pick(mine == 0, jnp.stack([send, far], 1), jnp.stack([far, send], 1))
        other = route(
            pick(mine == 0, rows[1], rows[0]),
            [(at(c, m), at(1 - c, m)) for c, m in every if c == m // 2],
        )
        here = pick(core == 0, rows[0], rows[1])
        return pick(core == mine, here, other)

    section_outputs = rows_out(outputs)
    input_grads = rows_out(grads_out).astype(f32)
    return (
        section_outputs[None],
        input_grads[None],
        whole_mine[0][None],
        whole_mine[1][None],
        g_in.transpose(1, 0, 2)[None],
        shard_mine[: 2 * local].reshape(1, 2, local),
        g_out[None],
        g_up[None],
        shard_mine[2 * local :][None],
        g_down[None],
        whole_mine[2][None],
    )


def solution(mesh):
    in_specs = (
        P("dp", "mp", None),
        P("dp", "mp", None),
        P("dp", None),
        P("section", None, None),
        P("section", None, None),
        P("section", None, None, "mp"),
        P("section", None, "mp"),
        P("section", "mp", None),
        P("section", None, "mp"),
        P("section", "mp"),
        P("section", "mp", None),
        P("section", None, None),
    )
    out_specs = (
        P("section", "dp", "mp", None),
        P("section", "dp", "mp", None),
        P("section", None, None),
        P("section", None, None),
        P("section", None, None, "mp"),
        P("section", None, "mp"),
        P("section", "mp", None),
        P("section", None, "mp"),
        P("section", "mp"),
        P("section", "mp", None),
        P("section", None, None),
    )
    return jax.shard_map(
        per_device, mesh=mesh, in_specs=in_specs, out_specs=out_specs, check_vma=False
    )
```

```python
from functools import partial

import jax
import jax.numpy as jnp
from jax import lax
from jax.experimental import pallas as pl
from jax.experimental.pallas import tpu as pltpu
from jax.sharding import PartitionSpec as P

HEAD = 64
branch_scale = 12.0 ** (-0.5)
norm_eps = 1e-05
masked_score = -1000000000.0
block = 256
cube = 0.044715
root = 0.7978845608

f32 = jnp.float32
bf16 = jnp.bfloat16


def mm(left, right):
    return jnp.dot(left, right, preferred_element_type=f32)


def mm_nt(left, right):
    return lax.dot_general(left, right, (((1,), (1,)), ((), ())), preferred_element_type=f32)


def mm_tn(left, right):
    return lax.dot_general(left, right, (((0,), (0,)), ((), ())), preferred_element_type=f32)


def normalize(values):
    mean = jnp.mean(values, axis=-1, keepdims=True)
    centred = values - mean
    spread = jnp.mean(centred * centred, axis=-1, keepdims=True)
    rstd = lax.rsqrt(spread + norm_eps)
    return centred * rstd, rstd


def norm_back(normal, rstd, grad, gain):
    scaled = grad * gain
    first = jnp.mean(scaled, axis=-1, keepdims=True)
    second = jnp.mean(scaled * normal, axis=-1, keepdims=True)
    return (scaled - first - normal * second) * rstd


def head_lanes(heads):
    found = []
    for head in range(heads):
        start = (head // 2) * 2 * HEAD
        width = min(2 * HEAD, heads * HEAD - start)
        found.append((start, width, head % 2))
    return found


def own_lanes(value, width, upper):
    if width == HEAD:
        return value
    lane = lax.broadcasted_iota(jnp.int32, value.shape, 1)
    keep = (lane >= HEAD) if upper else (lane < HEAD)
    return jnp.where(keep, value, jnp.zeros_like(value))


def block_mask(seg_col, seg_row, rows, count):
    same = seg_col[0:count, :] == seg_row[:, rows]
    key = lax.broadcasted_iota(jnp.int32, (count, rows.stop - rows.start), 0)
    query = lax.broadcasted_iota(jnp.int32, (count, rows.stop - rows.start), 1) + rows.start
    return same & (key <= query)


MESH = pl.DeviceIdType.MESH


def send(src, dst, sems, index, device):
    return pltpu.make_async_remote_copy(
        src_ref=src,
        dst_ref=dst,
        send_sem=sems.at[0, index],
        recv_sem=sems.at[1, index],
        device_id=device,
        device_id_type=MESH,
    )


def attend_block(qkv_ref, mask, rows, count, logsum_ref):
    heads = qkv_ref.shape[2] // HEAD
    mixed = []
    for head, (lane, lanes, upper) in enumerate(head_lanes(heads)):
        cols = slice(lane, lane + lanes)
        queries = own_lanes(qkv_ref[0, rows, cols], lanes, upper) * bf16(HEAD ** (-0.5))
        scores = mm_nt(qkv_ref[1, 0:count, cols], queries)
        scores = jnp.where(mask, scores, masked_score)
        top = jnp.max(scores, axis=0, keepdims=True)
        weights = jnp.exp(scores - top)
        total = jnp.sum(weights, axis=0, keepdims=True)
        result = mm_tn(qkv_ref[2, 0:count, cols], weights.astype(bf16)) / total
        logsum_ref[head : head + 1, rows] = top + jnp.log(total)
        mixed.append((lanes, result))
    found = []
    for pair in range(0, heads, 2):
        lanes, result = mixed[pair]
        if lanes > HEAD:
            result = jnp.concatenate([result[:HEAD], mixed[pair + 1][1][HEAD:]], axis=0)
        found.append((pair * HEAD, lanes, result.T.astype(bf16)))
    return found


def forward_kernel(
    state_ref,
    w_in,
    w_out,
    w_up,
    w_down,
    b_in,
    b_up,
    vec_ref,
    seg_col,
    seg_row,
    out_ref,
    normed_ref,
    qkv_ref,
    logsum_ref,
    att_ref,
    middle_ref,
    upper_ref,
    hidden_ref,
    slope_ref,
    qkv_out,
    att_out,
    low,
    got,
    qkv_sems,
    att_sems,
    pair_sems,
):
    core = lax.axis_index("section")
    z = lax.axis_index("mp")
    dp = lax.axis_index("dp")
    sibling = (1 - core, z, dp)
    partner = (core, z + 1 - 2 * lax.rem(z, 2), dp)
    barrier = pltpu.get_barrier_semaphore()
    for device in (sibling, partner):
        pl.semaphore_signal(barrier, inc=1, device_id=device, device_id_type=MESH)
    pl.semaphore_wait(barrier, 2)

    half = state_ref.shape[0]
    blocks = half // block
    first = pl.multiple_of(core * half, half)

    copies = []
    for j in range(blocks):
        rows = slice(j * block, (j + 1) * block)
        normal, _ = normalize(state_ref[rows, :].astype(f32))
        normed = (normal * vec_ref[0:1, :] + vec_ref[2:3, :]).astype(bf16)
        normed_ref[rows, :] = normed
        for part in range(3):
            qkv_out[j, part] = (mm(normed, w_in[1 - core, part]) + b_in[1 - core, part]).astype(bf16)
        there = pl.ds(pl.multiple_of(first + j * block, block), block)
        copy = send(qkv_out.at[j], qkv_ref.at[:, there, :], qkv_sems, j, sibling)
        copy.start()
        copies.append(copy)
        for part in range(3):
            qkv_ref[part, there, :] = (mm(normed, w_in[core, part]) + b_in[core, part]).astype(bf16)
    for copy in copies:
        copy.wait()

    def send_low(index, rows, value):
        low[index, rows, :] = value.astype(bf16)
        copy = send(low.at[index, rows], got.at[index, rows], pair_sems, index * blocks + rows.start // block, partner)
        copy.start()

    def received(index, rows):
        copy = send(low.at[index, rows], got.at[index, rows], pair_sems, index * blocks + rows.start // block, partner)
        copy.wait()
        return low[index, rows, :].astype(f32) + got[index, rows, :].astype(f32)

    for i in range(2 * blocks):
        owner, j = i // blocks, i % blocks
        rows = slice(i * block, (i + 1) * block)
        own = slice(j * block, (j + 1) * block)
        count = (i + 1) * block
        mask = block_mask(seg_col, seg_row, rows, count)
        found = attend_block(qkv_ref, mask, rows, count, logsum_ref)
        copy = send(att_out.at[j], att_ref.at[core, own], att_sems, j, sibling)

        @pl.when(core == owner)
        def _():
            for lane, lanes, result in found:
                att_ref[core, own, lane : lane + lanes] = result
            copy.wait_recv()
            send_low(0, own, mm(att_ref[0, own, :], w_out[0]) + mm(att_ref[1, own, :], w_out[1]))

        @pl.when(core != owner)
        def _():
            for lane, lanes, result in found:
                att_out[j, :, lane : lane + lanes] = result
            copy.start()

    for j in range(blocks):
        own = slice(j * block, (j + 1) * block)
        send(att_out.at[j], att_ref.at[core, own], att_sems, j, sibling).wait_send()

    for j in range(blocks):
        rows = slice(j * block, (j + 1) * block)
        middle = state_ref[rows, :].astype(f32) + branch_scale * (received(0, rows) + vec_ref[4:5, :])
        middle_ref[rows, :] = middle
        normal, _ = normalize(middle)
        upper = (normal * vec_ref[1:2, :] + vec_ref[3:4, :]).astype(bf16)
        upper_ref[rows, :] = upper
        total = None
        for k in range(2):
            pre = mm(upper, w_up[k]) + b_up[k]
            square = pre * pre
            curve = jnp.tanh(root * pre * (1.0 + cube * square))
            rise = 0.5 * (1.0 + curve)
            hidden = (pre * rise).astype(bf16)
            hidden_ref[k, rows, :] = hidden
            slope = rise + pre * (rise * (1.0 - curve)) * (root * (1.0 + 3.0 * cube * square))
            slope_ref[k, rows, :] = slope.astype(bf16)
            term = mm(hidden, w_down[k])
            total = term if total is None else total + term
        send_low(1, rows, total)

    for j in range(blocks):
        rows = slice(j * block, (j + 1) * block)
        result = middle_ref[rows, :] + branch_scale * (received(1, rows) + vec_ref[5:6, :])
        out_ref[rows, :] = result.astype(bf16)


def forward_layer(state, w_in, w_out, w_up, w_down, b_in, b_up, vec, seg_col, seg_row):
    half, width = state.shape
    length = seg_col.shape[0]
    local = w_in.shape[3]
    units = w_up.shape[2]
    blocks = half // block
    vmem = pl.BlockSpec(memory_space=pltpu.VMEM)
    shape = jax.ShapeDtypeStruct
    return pl.pallas_call(
        forward_kernel,
        out_shape=(
            shape((half, width), bf16),
            shape((half, width), bf16),
            shape((3, length, local), bf16),
            shape((local // HEAD, length), f32),
            shape((2, half, local), bf16),
            shape((half, width), f32),
            shape((half, width), bf16),
            shape((2, half, units), bf16),
            shape((2, half, units), bf16),
        ),
        in_specs=[vmem] * 10,
        out_specs=[vmem] * 9,
        scratch_shapes=[
            pltpu.VMEM((blocks, 3, block, local), bf16),
            pltpu.VMEM((blocks, block, local), bf16),
            pltpu.VMEM((2, half, width), bf16),
            pltpu.VMEM((2, half, width), bf16),
            pltpu.SemaphoreType.DMA((2, blocks)),
            pltpu.SemaphoreType.DMA((2, blocks)),
            pltpu.SemaphoreType.DMA((2, 2 * blocks)),
        ],
        compiler_params=pltpu.CompilerParams(
            vmem_limit_bytes=50 * 2**20, collective_id=1, has_side_effects=True
        ),
        name="forward_layer",
    )(state, w_in, w_out, w_up, w_down, b_in, b_up, vec, seg_col, seg_row)


def attend_back_block(qkv_ref, grad_ref, mask, rows, count, logsum_ref, dqkv_ref, dk_sum, dv_sum):
    heads = qkv_ref.shape[2] // HEAD
    scale = bf16(HEAD ** (-0.5))
    mixed = []
    for head, (lane, lanes, upper) in enumerate(head_lanes(heads)):
        cols = slice(lane, lane + lanes)
        queries = own_lanes(qkv_ref[0, rows, cols], lanes, upper) * scale
        grads = own_lanes(grad_ref[rows, cols], lanes, upper)
        keys = qkv_ref[1, 0:count, cols]
        scores = mm_nt(keys, queries)
        scores = jnp.where(mask, scores, masked_score)
        probs = jnp.exp(scores - logsum_ref[head : head + 1, rows])
        grad_probs = mm_nt(qkv_ref[2, 0:count, cols], grads)
        dv_sum[0:count, cols] += mm(probs.astype(bf16), grads)
        term = probs * grad_probs
        delta = jnp.sum(term, axis=0, keepdims=True)
        grad_scores = (term - probs * delta).astype(bf16)
        dk_sum[0:count, cols] += mm(grad_scores, queries)
        mixed.append((lanes, mm_tn(keys, grad_scores)))
    for pair in range(0, heads, 2):
        lane = pair * HEAD
        lanes, result = mixed[pair]
        if lanes > HEAD:
            result = jnp.concatenate([result[:HEAD], mixed[pair + 1][1][HEAD:]], axis=0)
        dqkv_ref[0, rows, lane : lane + lanes] = (result.T * HEAD ** (-0.5)).astype(bf16)


def backward_kernel(
    grad_ref,
    start_ref,
    normed_ref,
    qkv_ref,
    logsum_ref,
    att_ref,
    middle_ref,
    upper_ref,
    hidden_ref,
    slope_ref,
    w_in,
    w_out,
    w_up,
    w_down,
    vec_ref,
    seg_col,
    seg_row,
    out_ref,
    d_in,
    d_out,
    d_up,
    d_down,
    d_vec,
    d_b_up,
    d_b_in,
    gz_ref,
    dpre_ref,
    dmiddle_ref,
    gy_ref,
    datt_out,
    datt_ref,
    dqkv_ref,
    dk_sum,
    dv_sum,
    dmix_ref,
    low,
    got,
    att_sems,
    mix_sems,
    pair_sems,
):
    core = lax.axis_index("section")
    z = lax.axis_index("mp")
    dp = lax.axis_index("dp")
    sibling = (1 - core, z, dp)
    partner = (core, z + 1 - 2 * lax.rem(z, 2), dp)
    barrier = pltpu.get_barrier_semaphore()
    for device in (sibling, partner):
        pl.semaphore_signal(barrier, inc=1, device_id=device, device_id_type=MESH)
    pl.semaphore_wait(barrier, 2)

    half = grad_ref.shape[0]
    blocks = half // block
    first = pl.multiple_of(core * half, half)
    order = list(range(blocks))[::-1]

    def pair_copy(index, rows):
        return send(low.at[index, rows], got.at[index, rows], pair_sems, index * blocks + rows.start // block, partner)

    def send_low(index, rows, value):
        low[index, rows, :] = value.astype(bf16)
        pair_copy(index, rows).start()

    def received(index, rows):
        pair_copy(index, rows).wait()
        return low[index, rows, :].astype(f32) + got[index, rows, :].astype(f32)

    def own_rows(j):
        return slice(j * block, (j + 1) * block)

    def total(value):
        return jnp.sum(value, axis=0, keepdims=True)

    d_vec[...] = jnp.zeros_like(d_vec)
    dk_sum[...] = jnp.zeros_like(dk_sum)
    dv_sum[...] = jnp.zeros_like(dv_sum)

    for j in order:
        rows = own_rows(j)
        gz = branch_scale * grad_ref[rows, :].astype(f32)
        d_vec[5:6, :] += total(gz)
        gz = gz.astype(bf16)
        gz_ref[rows, :] = gz
        part = None
        for k in range(2):
            dpre = (mm_nt(gz, w_down[k]) * slope_ref[k, rows, :].astype(f32)).astype(bf16)
            dpre_ref[k, rows, :] = dpre
            term = mm_nt(dpre, w_up[k])
            part = term if part is None else part + term
        send_low(0, rows, part)
    for k in range(2):
        d_down[k] = mm_tn(hidden_ref[k], gz_ref[...]).astype(bf16)
        d_up[k] = mm_tn(upper_ref[...], dpre_ref[k]).astype(bf16)
        d_b_up[k] = total(dpre_ref[k].astype(f32))

    def datt_copy(j):
        there = pl.ds(pl.multiple_of(first + j * block, block), block)
        return send(datt_out.at[j], datt_ref.at[there, :], att_sems, j, sibling)

    for j in order:
        rows = own_rows(j)
        d_upper = received(0, rows)
        normal, rstd = normalize(middle_ref[rows, :])
        d_vec[1:2, :] += total(d_upper * normal)
        d_vec[3:4, :] += total(d_upper)
        d_middle = grad_ref[rows, :].astype(f32) + norm_back(normal, rstd, d_upper, vec_ref[1:2, :])
        dmiddle_ref[rows, :] = d_middle
        gy = branch_scale * d_middle
        d_vec[4:5, :] += total(gy)
        gy = gy.astype(bf16)
        gy_ref[rows, :] = gy
        datt_out[j] = mm_nt(gy, w_out[1 - core]).astype(bf16)
        datt_copy(j).start()
        there = pl.ds(pl.multiple_of(first + j * block, block), block)
        datt_ref[there, :] = mm_nt(gy, w_out[core]).astype(bf16)

    def mix_copy(j):
        return send(
            dqkv_ref.at[:, pl.ds(pl.multiple_of(half - first + j * block, block), block), :],
            dmix_ref.at[core, :, pl.ds(j * block, block), :],
            mix_sems,
            j,
            sibling,
        )

    def finish(i):
        owner, j = i // blocks, i % blocks
        rows = slice(i * block, (i + 1) * block)
        dqkv_ref[1, rows, :] = dk_sum[rows, :].astype(bf16)
        dqkv_ref[2, rows, :] = dv_sum[rows, :].astype(bf16)

        @pl.when(core == owner)
        def _():
            dmix_ref[core, :, own_rows(j), :] = dqkv_ref[:, rows, :]

        @pl.when(core != owner)
        def _():
            mix_copy(j).start()

    left = list(range(2 * blocks))
    for j in order:
        datt_copy(j).wait()
        for i in (blocks + j, j):
            rows = slice(i * block, (i + 1) * block)
            count = (i + 1) * block
            mask = block_mask(seg_col, seg_row, rows, count)
            attend_back_block(qkv_ref, datt_ref, mask, rows, count, logsum_ref, dqkv_ref, dk_sum, dv_sum)
            left.remove(i)
            if j == 0:
                for done in [n for n in range(2 * blocks) if n > max(left, default=-1) and n // blocks == i // blocks][::-1]:
                    finish(done)
    for k in range(2):
        d_out[k] = mm_tn(att_ref[k], gy_ref[...]).astype(bf16)

    for j in order:
        rows = own_rows(j)
        mix_copy(j).wait_recv()
        part = None
        for k in range(2):
            for p in range(3):
                term = mm_nt(dmix_ref[k, p, rows, :], w_in[k, p])
                part = term if part is None else part + term
        send_low(1, rows, part)
    for k in range(2):
        for p in range(3):
            d_in[k, p] = mm_tn(normed_ref[...], dmix_ref[k, p]).astype(bf16)
            d_b_in[k, p : p + 1, :] = total(dmix_ref[k, p].astype(f32))
    for j in order:
        rows = own_rows(j)
        d_normed = received(1, rows)
        normal, rstd = normalize(start_ref[rows, :].astype(f32))
        d_vec[0:1, :] += total(d_normed * normal)
        d_vec[2:3, :] += total(d_normed)
        d_state = dmiddle_ref[rows, :] + norm_back(normal, rstd, d_normed, vec_ref[0:1, :])
        out_ref[rows, :] = d_state.astype(bf16)
    for j in order:
        mix_copy(j).wait_send()


def backward_layer(grad, kept, w_in, w_out, w_up, w_down, vec, seg_col, seg_row):
    half, width = grad.shape
    length = seg_col.shape[0]
    local = w_in.shape[3]
    units = w_up.shape[2]
    blocks = half // block
    vmem = pl.BlockSpec(memory_space=pltpu.VMEM)
    shape = jax.ShapeDtypeStruct
    return pl.pallas_call(
        backward_kernel,
        out_shape=(
            shape((half, width), bf16),
            shape(w_in.shape, bf16),
            shape(w_out.shape, bf16),
            shape(w_up.shape, bf16),
            shape(w_down.shape, bf16),
            shape((8, width), f32),
            shape((2, 1, units), f32),
            shape((2, 3, local), f32),
        ),
        in_specs=[vmem] * 17,
        out_specs=[vmem] * 8,
        scratch_shapes=[
            pltpu.VMEM((half, width), bf16),
            pltpu.VMEM((2, half, units), bf16),
            pltpu.VMEM((half, width), f32),
            pltpu.VMEM((half, width), bf16),
            pltpu.VMEM((blocks, block, local), bf16),
            pltpu.VMEM((length, local), bf16),
            pltpu.VMEM((3, length, local), bf16),
            pltpu.VMEM((length, local), f32),
            pltpu.VMEM((length, local), f32),
            pltpu.VMEM((2, 3, half, local), bf16),
            pltpu.VMEM((2, half, width), bf16),
            pltpu.VMEM((2, half, width), bf16),
            pltpu.SemaphoreType.DMA((2, blocks)),
            pltpu.SemaphoreType.DMA((2, blocks)),
            pltpu.SemaphoreType.DMA((2, 2 * blocks)),
        ],
        compiler_params=pltpu.CompilerParams(
            vmem_limit_bytes=56 * 2**20, collective_id=2, has_side_effects=True
        ),
        name="backward_layer",
    )(grad, *kept, w_in, w_out, w_up, w_down, vec, seg_col, seg_row)


def segment_ids(lengths, length):
    ends = jnp.cumsum(lengths)
    positions = jnp.arange(length, dtype=jnp.int32)
    segs = jnp.sum((positions[:, None] >= ends[None, :]).astype(jnp.int32), axis=-1)
    docs = lengths.shape[0]
    return jnp.where(segs < docs, segs, docs + positions)


def per_device(
    inputs,
    cotangent,
    lengths,
    norm_gains,
    norm_shifts,
    in_weight,
    in_bias,
    out_weight,
    up_weight,
    up_bias,
    down_weight,
    branch_bias,
):
    core = lax.axis_index("section")
    z = lax.axis_index("mp")
    dp = lax.axis_index("dp")
    copies = lax.axis_size("dp")
    mine = z // 2
    side = z % 2
    quarter, width = inputs.shape[1:]
    half = 2 * quarter
    length = 4 * quarter
    local = in_weight.shape[3]
    units = up_weight.shape[2]

    def at(c, m):
        return c * 4 + m

    every = [(c, m) for c in range(2) for m in range(4)]

    def route(value, pairs):
        return lax.ppermute(value, ("section", "mp"), pairs)

    swap_core = [(at(c, m), at(1 - c, m)) for c, m in every]
    swap_side = [(at(c, m), at(c, m ^ 1)) for c, m in every]
    swap_pair = [(at(c, m), at(c, m ^ 2)) for c, m in every]

    def pick(flag, yes, no):
        return jnp.where(flag, yes, no)

    def rows_in(array):
        pairs = [(at(c, m), at(c, m ^ 2)) for c, m in every if c == m // 2]
        far = route(pick(mine == 0, array[1], array[0]), pairs)
        here = pick(core == mine, pick(mine == 0, array[0], array[1]), far)
        there = route(here, swap_side)
        return pick(
            side == 0,
            jnp.concatenate([here, there], axis=0),
            jnp.concatenate([there, here], axis=0),
        )

    def fetch(array, axis):
        part = array.shape[axis] // copies
        piece = lax.dynamic_slice_in_dim(array, dp * part, part, axis)
        piece = route(piece, swap_pair)
        return lax.all_gather(piece, "dp", axis=axis, tiled=True)

    def both_layers(array):
        other = route(array, swap_core)
        return [pick(core == layer, array, other) for layer in range(2)]

    mixing = in_weight[0].transpose(1, 0, 2)

    def slots(array, axis):
        far = fetch(array, axis)
        return [jnp.stack(pair) for pair in zip(both_layers(array), both_layers(far))]

    w_in = slots(mixing, 1)
    w_out = slots(out_weight[0], 0)
    w_up = slots(up_weight[0], 0)
    w_down = slots(down_weight[0], 0)
    shard_vec = jnp.concatenate([in_bias[0].reshape(-1), up_bias[0]])
    far_vec = route(shard_vec, swap_pair)
    whole_vec = jnp.concatenate(
        [norm_gains[0].reshape(-1), norm_shifts[0].reshape(-1), branch_bias[0].reshape(-1)]
    )
    vecs = both_layers(jnp.concatenate([shard_vec, far_vec, whole_vec]))

    def unpack(vec):
        found = []
        at_ = 0
        for size, shape in (
            (2 * local, (2, local)),
            (units, (units,)),
            (2 * local, (2, local)),
            (units, (units,)),
            (2 * width, (2, width)),
            (2 * width, (2, width)),
            (2 * width, (2, width)),
        ):
            found.append(vec[at_ : at_ + size].reshape(shape))
            at_ += size
        return found

    row_lengths = pick(mine == 0, lengths[0], lengths[1])
    segs = segment_ids(row_lengths, length)
    seg_col, seg_row = segs[:, None], segs[None, :]

    def to_heads(packed):
        keep = pick(core == 0, packed[0], packed[1])
        give = pick(core == 0, packed[1], packed[0])
        got = route(give, swap_core)
        return pick(
            core == 0,
            jnp.concatenate([keep, got], axis=0),
            jnp.concatenate([got, keep], axis=0),
        )

    def to_tokens(whole):
        keep = lax.dynamic_slice_in_dim(whole, core * half, half, 0)
        give = lax.dynamic_slice_in_dim(whole, (1 - core) * half, half, 0)
        got = route(give, swap_core)
        return pick(core == 0, jnp.stack([keep, got]), jnp.stack([got, keep]))

    def pair_sum(partial_sum):
        low = partial_sum.astype(bf16)
        return low.astype(f32) + route(low, swap_side).astype(f32)

    state = rows_in(inputs)
    grad = rows_in(cotangent)
    saved = []
    outputs = []
    for layer in range(2):
        bias_own, up_b_own, bias_far, up_b_far, gains, shifts, branch = unpack(vecs[layer])
        zero = jnp.zeros((local,), f32)
        b_in = jnp.stack([jnp.stack([b[0], zero, b[1]]) for b in (bias_own, bias_far)])[:, :, None]
        b_up = jnp.stack([up_b_own, up_b_far])[:, None]
        vec = jnp.concatenate([gains, shifts, branch], axis=0)
        start = state
        state, *kept = forward_layer(
            state, w_in[layer], w_out[layer], w_up[layer], w_down[layer], b_in, b_up, vec, seg_col, seg_row
        )
        saved.append(((start, *kept), vec))
        outputs.append(state)

    partials = [None, None]
    vectors = [None, None]
    grads_out = [None, None]
    for layer in (1, 0):
        kept, vec = saved[layer]
        grad, d_in, d_out, d_up, d_down, d_vec, d_b_up, d_b_in = backward_layer(
            grad, kept, w_in[layer], w_out[layer], w_up[layer], w_down[layer], vec, seg_col, seg_row
        )
        grads_out[layer] = grad
        partials[layer] = (d_in, d_out, d_up, d_down)
        shard_terms = [
            jnp.concatenate([d_b_in[i, 0], d_b_in[i, 2], d_b_up[i, 0]]) for i in range(2)
        ]
        vectors[layer] = (shard_terms, d_vec[:6].reshape(-1))

    def reduce_layer(index, layer):
        own, far = partials[layer][index]
        got = route(pick(core == 0, far, own), swap_core)
        total = (pick(core == 0, own, far).astype(f32) + got.astype(f32)).astype(bf16)
        piece = lax.psum_scatter(total, "dp", scatter_dimension=total.ndim - 2, tiled=True)
        cross = route(piece, [(at(1, m), at(0, m ^ 2)) for m in range(4)])
        return piece + cross

    final = []
    for index in range(4):
        first = reduce_layer(index, 0)
        second = reduce_layer(index, 1)
        second = route(second, [(at(0, m), at(1, m)) for m in range(4)])
        final.append(lax.all_gather(pick(core == 0, first, second), "dp", axis=first.ndim - 2, tiled=True).astype(f32))
    g_in, g_out, g_up, g_down = final

    shard_sum, whole_sum = [], []
    for layer in range(2):
        (own, far), whole = vectors[layer]
        shard_sum.append(jnp.stack([own, far]))
        whole_sum.append(whole)
    shard_sum = jnp.stack(shard_sum)
    across = route(shard_sum[:, 1], swap_pair)
    shard_sum = lax.psum(shard_sum[:, 0] + across, ("section", "dp"))
    whole_sum = lax.psum(jnp.stack(whole_sum), ("section", "mp", "dp")) * 0.5
    shard_mine = pick(core == 0, shard_sum[0], shard_sum[1])
    whole_mine = pick(core == 0, whole_sum[0], whole_sum[1]).reshape(3, 2, width)

    def rows_out(pair):
        both = jnp.stack(pair)
        send = lax.dynamic_slice_in_dim(both, side * quarter, quarter, 1)
        far = route(send, [(at(c, m), at(c, m ^ 2)) for c, m in every if c != m // 2])
        rows = pick(mine == 0, jnp.stack([send, far], 1), jnp.stack([far, send], 1))
        other = route(
            pick(mine == 0, rows[1], rows[0]),
            [(at(c, m), at(1 - c, m)) for c, m in every if c == m // 2],
        )
        here = pick(core == 0, rows[0], rows[1])
        return pick(core == mine, here, other)

    section_outputs = rows_out(outputs)
    input_grads = rows_out(grads_out).astype(f32)
    return (
        section_outputs[None],
        input_grads[None],
        whole_mine[0][None],
        whole_mine[1][None],
        g_in.transpose(1, 0, 2)[None],
        shard_mine[: 2 * local].reshape(1, 2, local),
        g_out[None],
        g_up[None],
        shard_mine[2 * local :][None],
        g_down[None],
        whole_mine[2][None],
    )


def solution(mesh):
    in_specs = (
        P("dp", "mp", None),
        P("dp", "mp", None),
        P("dp", None),
        P("section", None, None),
        P("section", None, None),
        P("section", None, None, "mp"),
        P("section", None, "mp"),
        P("section", "mp", None),
        P("section", None, "mp"),
        P("section", "mp"),
        P("section", "mp", None),
        P("section", None, None),
    )
    out_specs = (
        P("section", "dp", "mp", None),
        P("section", "dp", "mp", None),
        P("section", None, None),
        P("section", None, None),
        P("section", None, None, "mp"),
        P("section", None, "mp"),
        P("section", "mp", None),
        P("section", None, "mp"),
        P("section", "mp"),
        P("section", "mp", None),
        P("section", None, None),
    )
    return jax.shard_map(
        per_device, mesh=mesh, in_specs=in_specs, out_specs=out_specs, check_vma=False
    )
```

```python
from functools import partial

import jax
import jax.numpy as jnp
from jax import lax
from jax.experimental import pallas as pl
from jax.experimental.pallas import tpu as pltpu
from jax.sharding import PartitionSpec as P

HEAD = 64
branch_scale = 12.0 ** (-0.5)
norm_eps = 1e-05
masked_score = -1000000000.0
block = 256
cube = 0.044715
root = 0.7978845608

f32 = jnp.float32
bf16 = jnp.bfloat16


def mm(left, right):
    return jnp.dot(left, right, preferred_element_type=f32)


def mm_nt(left, right):
    return lax.dot_general(left, right, (((1,), (1,)), ((), ())), preferred_element_type=f32)


def mm_tn(left, right):
    return lax.dot_general(left, right, (((0,), (0,)), ((), ())), preferred_element_type=f32)


def normalize(values):
    mean = jnp.mean(values, axis=-1, keepdims=True)
    centred = values - mean
    spread = jnp.mean(centred * centred, axis=-1, keepdims=True)
    rstd = lax.rsqrt(spread + norm_eps)
    return centred * rstd, rstd


def norm_back(normal, rstd, grad, gain):
    scaled = grad * gain
    first = jnp.mean(scaled, axis=-1, keepdims=True)
    second = jnp.mean(scaled * normal, axis=-1, keepdims=True)
    return (scaled - first - normal * second) * rstd


def head_lanes(heads):
    found = []
    for head in range(heads):
        start = (head // 2) * 2 * HEAD
        width = min(2 * HEAD, heads * HEAD - start)
        found.append((start, width, head % 2))
    return found


def own_lanes(value, width, upper):
    if width == HEAD:
        return value
    lane = lax.broadcasted_iota(jnp.int32, value.shape, 1)
    keep = (lane >= HEAD) if upper else (lane < HEAD)
    return jnp.where(keep, value, jnp.zeros_like(value))


def block_mask(seg_col, seg_row, rows, count):
    same = seg_col[0:count, :] == seg_row[:, rows]
    key = lax.broadcasted_iota(jnp.int32, (count, rows.stop - rows.start), 0)
    query = lax.broadcasted_iota(jnp.int32, (count, rows.stop - rows.start), 1) + rows.start
    return same & (key <= query)


MESH = pl.DeviceIdType.MESH


def send(src, dst, sems, index, device):
    return pltpu.make_async_remote_copy(
        src_ref=src,
        dst_ref=dst,
        send_sem=sems.at[0, index],
        recv_sem=sems.at[1, index],
        device_id=device,
        device_id_type=MESH,
    )


def attend_block(qkv_ref, mask, rows, count, logsum_ref):
    heads = qkv_ref.shape[2] // HEAD
    mixed = []
    for head, (lane, lanes, upper) in enumerate(head_lanes(heads)):
        cols = slice(lane, lane + lanes)
        queries = own_lanes(qkv_ref[0, rows, cols], lanes, upper) * bf16(HEAD ** (-0.5))
        scores = mm_nt(qkv_ref[1, 0:count, cols], queries)
        scores = jnp.where(mask, scores, masked_score)
        top = jnp.max(scores, axis=0, keepdims=True)
        weights = jnp.exp(scores - top)
        total = jnp.sum(weights, axis=0, keepdims=True)
        result = mm_tn(qkv_ref[2, 0:count, cols], weights.astype(bf16)) / total
        logsum_ref[head : head + 1, rows] = top + jnp.log(total)
        mixed.append((lanes, result))
    found = []
    for pair in range(0, heads, 2):
        lanes, result = mixed[pair]
        if lanes > HEAD:
            result = jnp.concatenate([result[:HEAD], mixed[pair + 1][1][HEAD:]], axis=0)
        found.append((pair * HEAD, lanes, result.T.astype(bf16)))
    return found


class Places:
    def __init__(self, local, units, width):
        self.qkv = [slice(part * local, (part + 1) * local) for part in range(3)]
        self.out = slice(3 * local, 4 * local)
        self.up = slice(4 * local, 4 * local + width)
        self.down = slice(4 * local + width, 4 * local + width + units)
        self.rows = 4 * local + width + units


def forward_kernel(
    where,
    state_ref,
    w_ref,
    b_in,
    b_up,
    vec_ref,
    seg_col,
    seg_row,
    out_ref,
    normed_ref,
    qkv_ref,
    logsum_ref,
    att_ref,
    middle_ref,
    upper_ref,
    hidden_ref,
    slope_ref,
    qkv_out,
    att_out,
    low,
    got,
    qkv_sems,
    att_sems,
    pair_sems,
):
    core = lax.axis_index("section")
    z = lax.axis_index("mp")
    dp = lax.axis_index("dp")
    sibling = (1 - core, z, dp)
    partner = (core, z + 1 - 2 * lax.rem(z, 2), dp)
    barrier = pltpu.get_barrier_semaphore()
    for device in (sibling, partner):
        pl.semaphore_signal(barrier, inc=1, device_id=device, device_id_type=MESH)
    pl.semaphore_wait(barrier, 2)

    half = state_ref.shape[0]
    blocks = half // block
    first = pl.multiple_of(core * half, half)

    copies = []
    for j in range(blocks):
        rows = slice(j * block, (j + 1) * block)
        normal, _ = normalize(state_ref[rows, :].astype(f32))
        normed = (normal * vec_ref[0:1, :] + vec_ref[2:3, :]).astype(bf16)
        normed_ref[rows, :] = normed
        for part in range(3):
            qkv_out[j, part] = (mm_nt(normed, w_ref[1 - core, where.qkv[part], :]) + b_in[1 - core, part]).astype(bf16)
        there = pl.ds(pl.multiple_of(first + j * block, block), block)
        copy = send(qkv_out.at[j], qkv_ref.at[:, there, :], qkv_sems, j, sibling)
        copy.start()
        copies.append(copy)
        for part in range(3):
            qkv_ref[part, there, :] = (mm_nt(normed, w_ref[core, where.qkv[part], :]) + b_in[core, part]).astype(bf16)
    for copy in copies:
        copy.wait()

    def send_low(index, rows, value):
        low[index, rows, :] = value.astype(bf16)
        copy = send(low.at[index, rows], got.at[index, rows], pair_sems, index * blocks + rows.start // block, partner)
        copy.start()

    def received(index, rows):
        copy = send(low.at[index, rows], got.at[index, rows], pair_sems, index * blocks + rows.start // block, partner)
        copy.wait()
        return low[index, rows, :].astype(f32) + got[index, rows, :].astype(f32)

    for i in range(2 * blocks):
        owner, j = i // blocks, i % blocks
        rows = slice(i * block, (i + 1) * block)
        own = slice(j * block, (j + 1) * block)
        count = (i + 1) * block
        mask = block_mask(seg_col, seg_row, rows, count)
        found = attend_block(qkv_ref, mask, rows, count, logsum_ref)
        copy = send(att_out.at[j], att_ref.at[core, own], att_sems, j, sibling)

        @pl.when(core == owner)
        def _():
            for lane, lanes, result in found:
                att_ref[core, own, lane : lane + lanes] = result
            copy.wait_recv()
            send_low(0, own, sum(mm(att_ref[k, own, :], w_ref[k, where.out, :]) for k in range(2)))

        @pl.when(core != owner)
        def _():
            for lane, lanes, result in found:
                att_out[j, :, lane : lane + lanes] = result
            copy.start()

    for j in range(blocks):
        own = slice(j * block, (j + 1) * block)
        send(att_out.at[j], att_ref.at[core, own], att_sems, j, sibling).wait_send()

    for j in range(blocks):
        rows = slice(j * block, (j + 1) * block)
        middle = state_ref[rows, :].astype(f32) + branch_scale * (received(0, rows) + vec_ref[4:5, :])
        middle_ref[rows, :] = middle
        normal, _ = normalize(middle)
        upper = (normal * vec_ref[1:2, :] + vec_ref[3:4, :]).astype(bf16)
        upper_ref[rows, :] = upper
        total = None
        for k in range(2):
            pre = mm(upper, w_ref[k, where.up, :]) + b_up[k]
            square = pre * pre
            curve = jnp.tanh(root * pre * (1.0 + cube * square))
            rise = 0.5 * (1.0 + curve)
            hidden = (pre * rise).astype(bf16)
            hidden_ref[k, rows, :] = hidden
            slope = rise + pre * (rise * (1.0 - curve)) * (root * (1.0 + 3.0 * cube * square))
            slope_ref[k, rows, :] = slope.astype(bf16)
            term = mm(hidden, w_ref[k, where.down, :])
            total = term if total is None else total + term
        send_low(1, rows, total)

    for j in range(blocks):
        rows = slice(j * block, (j + 1) * block)
        result = middle_ref[rows, :] + branch_scale * (received(1, rows) + vec_ref[5:6, :])
        out_ref[rows, :] = result.astype(bf16)


def forward_layer(where, state, weights, b_in, b_up, vec, seg_col, seg_row):
    half, width = state.shape
    length = seg_col.shape[0]
    local = where.qkv[0].stop
    units = b_up.shape[2]
    blocks = half // block
    vmem = pl.BlockSpec(memory_space=pltpu.VMEM)
    shape = jax.ShapeDtypeStruct
    return pl.pallas_call(
        partial(forward_kernel, where),
        out_shape=(
            shape((half, width), bf16),
            shape((half, width), bf16),
            shape((3, length, local), bf16),
            shape((local // HEAD, length), f32),
            shape((2, half, local), bf16),
            shape((half, width), f32),
            shape((half, width), bf16),
            shape((2, half, units), bf16),
            shape((2, half, units), bf16),
        ),
        in_specs=[vmem] * 7,
        out_specs=[vmem] * 9,
        scratch_shapes=[
            pltpu.VMEM((blocks, 3, block, local), bf16),
            pltpu.VMEM((blocks, block, local), bf16),
            pltpu.VMEM((2, half, width), bf16),
            pltpu.VMEM((2, half, width), bf16),
            pltpu.SemaphoreType.DMA((2, blocks)),
            pltpu.SemaphoreType.DMA((2, blocks)),
            pltpu.SemaphoreType.DMA((2, 2 * blocks)),
        ],
        compiler_params=pltpu.CompilerParams(
            vmem_limit_bytes=50 * 2**20, collective_id=1, has_side_effects=True
        ),
        name="forward_layer",
    )(state, weights, b_in, b_up, vec, seg_col, seg_row)


def attend_back_block(qkv_ref, grad_ref, mask, rows, count, logsum_ref, dqkv_ref, dk_sum, dv_sum):
    heads = qkv_ref.shape[2] // HEAD
    scale = bf16(HEAD ** (-0.5))
    mixed = []
    for head, (lane, lanes, upper) in enumerate(head_lanes(heads)):
        cols = slice(lane, lane + lanes)
        queries = own_lanes(qkv_ref[0, rows, cols], lanes, upper) * scale
        grads = own_lanes(grad_ref[rows, cols], lanes, upper)
        keys = qkv_ref[1, 0:count, cols]
        scores = mm_nt(keys, queries)
        scores = jnp.where(mask, scores, masked_score)
        probs = jnp.exp(scores - logsum_ref[head : head + 1, rows])
        grad_probs = mm_nt(qkv_ref[2, 0:count, cols], grads)
        dv_sum[0:count, cols] += mm(probs.astype(bf16), grads)
        term = probs * grad_probs
        delta = jnp.sum(term, axis=0, keepdims=True)
        grad_scores = (term - probs * delta).astype(bf16)
        dk_sum[0:count, cols] += mm(grad_scores, queries)
        mixed.append((lanes, mm_tn(keys, grad_scores)))
    for pair in range(0, heads, 2):
        lane = pair * HEAD
        lanes, result = mixed[pair]
        if lanes > HEAD:
            result = jnp.concatenate([result[:HEAD], mixed[pair + 1][1][HEAD:]], axis=0)
        dqkv_ref[0, rows, lane : lane + lanes] = (result.T * HEAD ** (-0.5)).astype(bf16)


def backward_kernel(
    where,
    grad_ref,
    start_ref,
    normed_ref,
    qkv_ref,
    logsum_ref,
    att_ref,
    middle_ref,
    upper_ref,
    hidden_ref,
    slope_ref,
    w_ref,
    vec_ref,
    seg_col,
    seg_row,
    out_ref,
    d_ref,
    d_vec,
    gz_ref,
    dpre_ref,
    dmiddle_ref,
    gy_ref,
    datt_out,
    datt_ref,
    dqkv_ref,
    dk_sum,
    dv_sum,
    dmix_ref,
    low,
    got,
    att_sems,
    mix_sems,
    pair_sems,
):
    core = lax.axis_index("section")
    z = lax.axis_index("mp")
    dp = lax.axis_index("dp")
    sibling = (1 - core, z, dp)
    partner = (core, z + 1 - 2 * lax.rem(z, 2), dp)
    barrier = pltpu.get_barrier_semaphore()
    for device in (sibling, partner):
        pl.semaphore_signal(barrier, inc=1, device_id=device, device_id_type=MESH)
    pl.semaphore_wait(barrier, 2)

    half = grad_ref.shape[0]
    blocks = half // block
    first = pl.multiple_of(core * half, half)
    order = list(range(blocks))[::-1]

    def pair_copy(index, rows):
        return send(low.at[index, rows], got.at[index, rows], pair_sems, index * blocks + rows.start // block, partner)

    def send_low(index, rows, value):
        low[index, rows, :] = value.astype(bf16)
        pair_copy(index, rows).start()

    def received(index, rows):
        pair_copy(index, rows).wait()
        return low[index, rows, :].astype(f32) + got[index, rows, :].astype(f32)

    def own_rows(j):
        return slice(j * block, (j + 1) * block)

    def total(value):
        return jnp.sum(value, axis=0, keepdims=True)

    d_vec[...] = jnp.zeros_like(d_vec)
    dk_sum[...] = jnp.zeros_like(dk_sum)
    dv_sum[...] = jnp.zeros_like(dv_sum)

    for j in order:
        rows = own_rows(j)
        gz = branch_scale * grad_ref[rows, :].astype(f32)
        d_vec[5:6, :] += total(gz)
        gz = gz.astype(bf16)
        gz_ref[rows, :] = gz
        part = None
        for k in range(2):
            dpre = (mm_nt(gz, w_ref[k, where.down, :]) * slope_ref[k, rows, :].astype(f32)).astype(bf16)
            dpre_ref[k, rows, :] = dpre
            term = mm_nt(dpre, w_ref[k, where.up, :])
            part = term if part is None else part + term
        send_low(0, rows, part)
    for k in range(2):
        d_ref[k, where.down, :] = mm_tn(hidden_ref[k], gz_ref[...]).astype(bf16)
        d_ref[k, where.up, :] = mm_tn(upper_ref[...], dpre_ref[k]).astype(bf16)
        d_vec[8 + 2 * k : 9 + 2 * k, :] = total(dpre_ref[k].astype(f32))

    def datt_copy(j):
        there = pl.ds(pl.multiple_of(first + j * block, block), block)
        return send(datt_out.at[j], datt_ref.at[there, :], att_sems, j, sibling)

    for j in order:
        rows = own_rows(j)
        d_upper = received(0, rows)
        normal, rstd = normalize(middle_ref[rows, :])
        d_vec[1:2, :] += total(d_upper * normal)
        d_vec[3:4, :] += total(d_upper)
        d_middle = grad_ref[rows, :].astype(f32) + norm_back(normal, rstd, d_upper, vec_ref[1:2, :])
        dmiddle_ref[rows, :] = d_middle
        gy = branch_scale * d_middle
        d_vec[4:5, :] += total(gy)
        gy = gy.astype(bf16)
        gy_ref[rows, :] = gy
        datt_out[j] = mm_nt(gy, w_ref[1 - core, where.out, :]).astype(bf16)
        datt_copy(j).start()
        there = pl.ds(pl.multiple_of(first + j * block, block), block)
        datt_ref[there, :] = mm_nt(gy, w_ref[core, where.out, :]).astype(bf16)

    def mix_copy(j):
        return send(
            dqkv_ref.at[:, pl.ds(pl.multiple_of(half - first + j * block, block), block), :],
            dmix_ref.at[core, :, pl.ds(j * block, block), :],
            mix_sems,
            j,
            sibling,
        )

    def finish(i):
        owner, j = i // blocks, i % blocks
        rows = slice(i * block, (i + 1) * block)
        dqkv_ref[1, rows, :] = dk_sum[rows, :].astype(bf16)
        dqkv_ref[2, rows, :] = dv_sum[rows, :].astype(bf16)

        @pl.when(core == owner)
        def _():
            dmix_ref[core, :, own_rows(j), :] = dqkv_ref[:, rows, :]

        @pl.when(core != owner)
        def _():
            mix_copy(j).start()

    left = list(range(2 * blocks))
    for j in order:
        datt_copy(j).wait()
        for i in (blocks + j, j):
            rows = slice(i * block, (i + 1) * block)
            count = (i + 1) * block
            mask = block_mask(seg_col, seg_row, rows, count)
            attend_back_block(qkv_ref, datt_ref, mask, rows, count, logsum_ref, dqkv_ref, dk_sum, dv_sum)
            left.remove(i)
            if j == 0:
                for done in [n for n in range(2 * blocks) if n > max(left, default=-1) and n // blocks == i // blocks][::-1]:
                    finish(done)
    for k in range(2):
        d_ref[k, where.out, :] = mm_tn(att_ref[k], gy_ref[...]).astype(bf16)

    for j in order:
        rows = own_rows(j)
        mix_copy(j).wait_recv()
        part = None
        for k in range(2):
            for p in range(3):
                term = mm(dmix_ref[k, p, rows, :], w_ref[k, where.qkv[p], :])
                part = term if part is None else part + term
        send_low(1, rows, part)
    for k in range(2):
        for p in range(3):
            d_ref[k, where.qkv[p], :] = mm_tn(dmix_ref[k, p], normed_ref[...]).astype(bf16)
        for n, p in enumerate((0, 2)):
            local = dmix_ref.shape[3]
            d_vec[9 + 2 * k : 10 + 2 * k, n * 2 * block : n * 2 * block + local] = total(dmix_ref[k, p].astype(f32))
    for j in order:
        rows = own_rows(j)
        d_normed = received(1, rows)
        normal, rstd = normalize(start_ref[rows, :].astype(f32))
        d_vec[0:1, :] += total(d_normed * normal)
        d_vec[2:3, :] += total(d_normed)
        d_state = dmiddle_ref[rows, :] + norm_back(normal, rstd, d_normed, vec_ref[0:1, :])
        out_ref[rows, :] = d_state.astype(bf16)
    for j in order:
        mix_copy(j).wait_send()


def backward_layer(where, grad, kept, weights, vec, seg_col, seg_row):
    half, width = grad.shape
    length = seg_col.shape[0]
    local = where.qkv[0].stop
    units = kept[7].shape[2]
    blocks = half // block
    vmem = pl.BlockSpec(memory_space=pltpu.VMEM)
    shape = jax.ShapeDtypeStruct
    return pl.pallas_call(
        partial(backward_kernel, where),
        out_shape=(
            shape((half, width), bf16),
            shape(weights.shape, bf16),
            shape((16, width), f32),
        ),
        in_specs=[vmem] * 14,
        out_specs=[vmem] * 3,
        scratch_shapes=[
            pltpu.VMEM((half, width), bf16),
            pltpu.VMEM((2, half, units), bf16),
            pltpu.VMEM((half, width), f32),
            pltpu.VMEM((half, width), bf16),
            pltpu.VMEM((blocks, block, local), bf16),
            pltpu.VMEM((length, local), bf16),
            pltpu.VMEM((3, length, local), bf16),
            pltpu.VMEM((length, local), f32),
            pltpu.VMEM((length, local), f32),
            pltpu.VMEM((2, 3, half, local), bf16),
            pltpu.VMEM((2, half, width), bf16),
            pltpu.VMEM((2, half, width), bf16),
            pltpu.SemaphoreType.DMA((2, blocks)),
            pltpu.SemaphoreType.DMA((2, blocks)),
            pltpu.SemaphoreType.DMA((2, 2 * blocks)),
        ],
        compiler_params=pltpu.CompilerParams(
            vmem_limit_bytes=56 * 2**20, collective_id=2, has_side_effects=True
        ),
        name="backward_layer",
    )(grad, *kept, weights, vec, seg_col, seg_row)


def others(dp, copies):
    return [dp + 1 - 2 * lax.rem(dp, 2), dp + 2 - 4 * lax.rem(dp // 2, 2)]


def more_bits(copies):
    return [1 << n for n in range(2, copies.bit_length()) if (1 << n) < copies]


def flipped(dp, bit):
    return dp + bit - 2 * bit * lax.rem(dp // bit, 2)


class GradSum:
    kinds = 10

    def __init__(self, layer, part, twin, first, second, cross, groups, final, sems, pieces, copies):
        self.layer, self.part, self.twin, self.first, self.second = layer, part, twin, first, second
        self.cross, self.final, self.sems, self.pieces = cross, final, sems, pieces
        self.core = lax.axis_index("section")
        self.z = lax.axis_index("mp")
        self.dp = lax.axis_index("dp")
        self.bits_above = more_bits(copies)
        self.groups = groups
        self.stages = 6 + len(self.bits_above)
        self.rows = part.shape[1] // pieces
        self.slot = lax.rem(self.core + layer, 2)
        self.near = others(self.dp, copies)
        self.bits = [lax.rem(self.dp, 2), lax.rem(self.dp // 2, 2)]
        self.pair = self.z + 2 - 4 * (self.z // 2)

    def copy(self, piece, kind, src, dst, device):
        return send(src, dst, self.sems, piece * self.kinds + kind, device)

    def span(self, piece, start, count):
        return pl.ds(pl.multiple_of(piece * self.rows + start, 16), count)

    def chunk(self, half, outer, inner):
        eighth = self.rows // 8
        return half * 4 * eighth + outer * 2 * eighth + inner * eighth

    def twin_copy(self, piece):
        rows = self.span(piece, 0, self.rows)
        return self.copy(
            piece, 0, self.part.at[1 - self.slot, rows], self.twin.at[rows], (1 - self.core, self.z, self.dp)
        )

    def first_copy(self, piece, half):
        count = self.rows // 4
        axis = half
        src = self.span(piece, self.chunk(half, 1 - self.bits[axis], 0), count)
        dst = self.span(piece, 0, count)
        dst = pl.ds(pl.multiple_of((piece * 2 + half) * count, 16), count)
        return self.copy(
            piece, 1 + half, self.part.at[self.slot, src], self.first.at[dst], (self.core, self.z, self.near[axis])
        )

    def second_copy(self, piece, half):
        count = self.rows // 8
        axis = 1 - half
        src = self.span(piece, self.chunk(half, self.bits[half], 1 - self.bits[axis]), count)
        dst = pl.ds(pl.multiple_of((piece * 2 + half) * count, 16), count)
        return self.copy(
            piece, 3 + half, self.part.at[self.slot, src], self.second.at[dst], (self.core, self.z, self.near[axis])
        )

    def own(self, piece, half):
        return self.span(piece, self.chunk(half, self.bits[half], self.bits[1 - half]), self.rows // 8)

    def cross_copy(self, piece, half):
        count = self.rows // 8
        dst = pl.ds(pl.multiple_of((piece * 2 + half) * count, 16), count)
        return self.copy(
            piece,
            5 + half,
            self.part.at[self.slot, self.own(piece, half)],
            self.cross.at[dst],
            (1 - self.core, self.pair, self.dp),
        )

    def gather_copies(self, piece, half):
        rows = self.own(piece, half)
        near, far = self.near[half], self.near[1 - half]
        both = near + far - self.dp
        return [
            send(
                self.final.at[rows],
                self.final.at[rows],
                self.sems,
                (self.pieces * self.kinds) + (piece * 2 + half) * 3 + n,
                (self.core, self.z, device),
            )
            for n, device in enumerate((near, far, both))
        ]

    def group_copy(self, step, piece, half):
        count = self.rows // 8
        rows = self.own(piece, half)
        dst = pl.ds(pl.multiple_of((piece * 2 + half) * count, 16), count)
        index = self.pieces * (self.kinds + 6) + (step * self.pieces + piece) * 2 + half
        device = (self.core, self.z, flipped(self.dp, self.bits_above[step]))
        return send(self.final.at[rows], self.groups.at[step, dst], self.sems, index, device)

    @staticmethod
    def semaphores(pieces, copies):
        return pieces * (GradSum.kinds + 6 + 2 * len(more_bits(copies)))

    def stage(self, number, piece):
        if number < 4:
            (self.stage0, self.stage1, self.stage2, self.stage3)[number](piece)
        elif number < self.stages - 1:
            self.stage4(number - 4, piece)
        else:
            self.stage5(piece)

    def add(self, dst_rows, other):
        value = self.part[self.slot, dst_rows, :].astype(f32) + other.astype(f32)
        self.part[self.slot, dst_rows, :] = value.astype(bf16)

    def stage0(self, piece):
        self.twin_copy(piece).start()

    def stage1(self, piece):
        self.twin_copy(piece).wait_recv()
        rows = self.span(piece, 0, self.rows)
        self.add(rows, self.twin[rows, :])
        for half in range(2):
            self.first_copy(piece, half).start()

    def stage2(self, piece):
        count = self.rows // 4
        for half in range(2):
            self.first_copy(piece, half).wait()
            rows = self.span(piece, self.chunk(half, self.bits[half], 0), count)
            self.add(rows, self.first[pl.ds(pl.multiple_of((piece * 2 + half) * count, 16), count), :])
            self.second_copy(piece, half).start()

    def stage3(self, piece):
        count = self.rows // 8
        for half in range(2):
            self.second_copy(piece, half).wait()
            self.add(self.own(piece, half), self.second[pl.ds(pl.multiple_of((piece * 2 + half) * count, 16), count), :])

            @pl.when(self.core != self.layer)
            def _():
                self.cross_copy(piece, half).start()

    def stage4(self, step, piece):
        count = self.rows // 8

        @pl.when(self.core == self.layer)
        def _():
            for half in range(2):
                rows = self.own(piece, half)
                slot = pl.ds(pl.multiple_of((piece * 2 + half) * count, 16), count)
                if step == 0:
                    self.cross_copy(piece, half).wait_recv()
                    value = self.part[self.slot, rows, :].astype(f32) + self.cross[slot, :].astype(f32)
                else:
                    self.group_copy(step - 1, piece, half).wait()
                    value = self.final[rows, :].astype(f32) + self.groups[step - 1, slot, :].astype(f32)
                self.final[rows, :] = value.astype(bf16)
                if step < len(self.bits_above):
                    self.group_copy(step, piece, half).start()
                else:
                    for copy in self.gather_copies(piece, half):
                        copy.start()

    def stage5(self, piece):
        self.twin_copy(piece).wait_send()

        @pl.when(self.core == self.layer)
        def _():
            for half in range(2):
                for copy in self.gather_copies(piece, half):
                    copy.wait()

        @pl.when(self.core != self.layer)
        def _():
            for half in range(2):
                self.cross_copy(piece, half).wait_send()


class VectorSum:
    def __init__(self, layer, part, got, out, sems, copies):
        self.layer, self.part, self.got, self.out, self.sems = layer, part, got, out, sems
        core, z, dp = (lax.axis_index(name) for name in ("section", "mp", "dp"))
        self.devices = [(1 - core, z, dp)] + [(core, z, near) for near in others(dp, copies)]
        self.devices += [(core, z, flipped(dp, bit)) for bit in more_bits(copies)]
        self.devices.append((core, z + 2 - 4 * (z // 2), dp))
        self.last = len(self.devices) - 1

    def copy(self, step):
        return send(self.part, self.got.at[step], self.sems, step, self.devices[step])

    def start(self, step):
        self.copy(step).start()

    def add(self, step):
        self.copy(step).wait()
        if step < self.last:
            self.part[...] += self.got[step]
            self.start(step + 1)
        else:
            self.out[0:8, :] = self.part[0:8, :] + self.got[step, 0:8, :]
            self.out[8:10, :] = self.part[8:10, :] + self.got[step, 10:12, :]
            self.out[10:16, :] = jnp.zeros_like(self.out[10:16, :])


def grads_kernel(
    copies,
    pieces,
    part1,
    part0,
    vec1,
    vec0,
    final,
    out1,
    out0,
    sum1,
    sum0,
    twin1,
    first1,
    second1,
    cross1,
    groups1,
    twin0,
    first0,
    second0,
    cross0,
    groups0,
    got1,
    got0,
    work1,
    work0,
    sems1,
    sems0,
    vec_sems1,
    vec_sems0,
    load_sems,
):
    core, z, dp = (lax.axis_index(name) for name in ("section", "mp", "dp"))
    near = others(dp, copies)
    pair = z + 2 - 4 * (z // 2)
    devices = [
        (1 - core, z, dp),
        (core, z, near[0]),
        (core, z, near[1]),
        (core, z, near[0] + near[1] - dp),
        (core, pair, dp),
        (1 - core, pair, dp),
    ] + [(core, z, flipped(dp, bit)) for bit in more_bits(copies)]
    barrier = pltpu.get_barrier_semaphore()
    for device in devices:
        pl.semaphore_signal(barrier, inc=1, device_id=device, device_id_type=MESH)
    loads = [
        pltpu.make_async_copy(src, dst, load_sems.at[n])
        for n, (src, dst) in enumerate(((part1, sum1), (part0, sum0)))
    ]
    for load in loads:
        load.start()
    pl.semaphore_wait(barrier, len(devices))
    work1[...] = vec1[...]
    work0[...] = vec0[...]
    vectors = [
        VectorSum(1, work1, got1, out1, vec_sems1, copies),
        VectorSum(0, work0, got0, out0, vec_sems0, copies),
    ]
    sums = [
        GradSum(1, sum1, twin1, first1, second1, cross1, groups1, final, sems1, pieces, copies),
        GradSum(0, sum0, twin0, first0, second0, cross0, groups0, final, sems0, pieces, copies),
    ]
    for vector in vectors:
        vector.start(0)
    for load in loads:
        load.wait()
    work = [(one, piece) for one in sums for piece in range(pieces)]
    stages = sums[0].stages
    for tick in range(max(len(work) + stages - 1, vectors[0].last + 1)):
        for stage in range(stages):
            n = tick - stage
            if 0 <= n < len(work):
                one, piece = work[n]
                one.stage(stage, piece)
        if tick <= vectors[0].last:
            for vector in vectors:
                vector.add(tick)


def sum_grads(copies, part1, part0, vec1, vec0):
    pieces = 6
    above = len(more_bits(copies))
    _, rows, width = part1.shape
    vmem = pl.BlockSpec(memory_space=pltpu.VMEM)
    hbm = pl.BlockSpec(memory_space=pl.ANY)
    shape = jax.ShapeDtypeStruct
    buffers = [
        pltpu.VMEM((rows, width), bf16),
        pltpu.VMEM((rows // 2, width), bf16),
        pltpu.VMEM((rows // 4, width), bf16),
        pltpu.VMEM((rows // 4, width), bf16),
        pltpu.VMEM((max(1, above), rows // 4 if above else 16, width), bf16),
    ]
    return pl.pallas_call(
        partial(grads_kernel, copies, pieces),
        out_shape=(shape((rows, width), bf16), shape(vec1.shape, f32), shape(vec1.shape, f32)),
        in_specs=[hbm, hbm, vmem, vmem],
        out_specs=[vmem] * 3,
        scratch_shapes=[pltpu.VMEM(part1.shape, bf16)] * 2
        + buffers * 2
        + [pltpu.VMEM((4 + above, *vec1.shape), f32)] * 2
        + [pltpu.VMEM(vec1.shape, f32)] * 2
        + [pltpu.SemaphoreType.DMA((2, GradSum.semaphores(pieces, copies)))] * 2
        + [pltpu.SemaphoreType.DMA((2, 4 + above))] * 2
        + [pltpu.SemaphoreType.DMA((2,))],
        compiler_params=pltpu.CompilerParams(
            vmem_limit_bytes=56 * 2**20, collective_id=3, has_side_effects=True
        ),
        name="sum_grads",
    )(part1, part0, vec1, vec0)


def segment_ids(lengths, length):
    ends = jnp.cumsum(lengths)
    positions = jnp.arange(length, dtype=jnp.int32)
    segs = jnp.sum((positions[:, None] >= ends[None, :]).astype(jnp.int32), axis=-1)
    docs = lengths.shape[0]
    return jnp.where(segs < docs, segs, docs + positions)


def per_device(
    inputs,
    cotangent,
    lengths,
    norm_gains,
    norm_shifts,
    in_weight,
    in_bias,
    out_weight,
    up_weight,
    up_bias,
    down_weight,
    branch_bias,
):
    core = lax.axis_index("section")
    z = lax.axis_index("mp")
    dp = lax.axis_index("dp")
    copies = lax.axis_size("dp")
    mine = z // 2
    side = z % 2
    quarter, width = inputs.shape[1:]
    half = 2 * quarter
    length = 4 * quarter
    local = in_weight.shape[3]
    units = up_weight.shape[2]

    def at(c, m):
        return c * 4 + m

    every = [(c, m) for c in range(2) for m in range(4)]

    def route(value, pairs):
        return lax.ppermute(value, ("section", "mp"), pairs)

    swap_core = [(at(c, m), at(1 - c, m)) for c, m in every]
    swap_side = [(at(c, m), at(c, m ^ 1)) for c, m in every]
    swap_pair = [(at(c, m), at(c, m ^ 2)) for c, m in every]

    def pick(flag, yes, no):
        return jnp.where(flag, yes, no)

    def rows_in(array):
        pairs = [(at(c, m), at(c, m ^ 2)) for c, m in every if c == m // 2]
        far = route(pick(mine == 0, array[1], array[0]), pairs)
        here = pick(core == mine, pick(mine == 0, array[0], array[1]), far)
        there = route(here, swap_side)
        return pick(
            side == 0,
            jnp.concatenate([here, there], axis=0),
            jnp.concatenate([there, here], axis=0),
        )

    def fetch(array, axis):
        part = array.shape[axis] // copies
        piece = lax.dynamic_slice_in_dim(array, dp * part, part, axis)
        piece = route(piece, swap_pair)
        return lax.all_gather(piece, "dp", axis=axis, tiled=True)

    def both_layers(array):
        other = route(array, swap_core)
        return [pick(core == layer, array, other) for layer in range(2)]

    where = Places(local, units, width)
    shard = jnp.concatenate(
        [in_weight[0].transpose(1, 2, 0).reshape(3 * local, width), out_weight[0], up_weight[0], down_weight[0]]
    )
    far = fetch(shard, 0)
    weights = [jnp.stack(pair) for pair in zip(both_layers(shard), both_layers(far))]
    shard_vec = jnp.concatenate([in_bias[0].reshape(-1), up_bias[0]])
    far_vec = route(shard_vec, swap_pair)
    whole_vec = jnp.concatenate(
        [norm_gains[0].reshape(-1), norm_shifts[0].reshape(-1), branch_bias[0].reshape(-1)]
    )
    vecs = both_layers(jnp.concatenate([shard_vec, far_vec, whole_vec]))

    def unpack(vec):
        found = []
        at_ = 0
        for size, shape in (
            (2 * local, (2, local)),
            (units, (units,)),
            (2 * local, (2, local)),
            (units, (units,)),
            (2 * width, (2, width)),
            (2 * width, (2, width)),
            (2 * width, (2, width)),
        ):
            found.append(vec[at_ : at_ + size].reshape(shape))
            at_ += size
        return found

    row_lengths = pick(mine == 0, lengths[0], lengths[1])
    segs = segment_ids(row_lengths, length)
    seg_col, seg_row = segs[:, None], segs[None, :]

    def to_heads(packed):
        keep = pick(core == 0, packed[0], packed[1])
        give = pick(core == 0, packed[1], packed[0])
        got = route(give, swap_core)
        return pick(
            core == 0,
            jnp.concatenate([keep, got], axis=0),
            jnp.concatenate([got, keep], axis=0),
        )

    def to_tokens(whole):
        keep = lax.dynamic_slice_in_dim(whole, core * half, half, 0)
        give = lax.dynamic_slice_in_dim(whole, (1 - core) * half, half, 0)
        got = route(give, swap_core)
        return pick(core == 0, jnp.stack([keep, got]), jnp.stack([got, keep]))

    def pair_sum(partial_sum):
        low = partial_sum.astype(bf16)
        return low.astype(f32) + route(low, swap_side).astype(f32)

    state = rows_in(inputs)
    grad = rows_in(cotangent)
    saved = []
    outputs = []
    for layer in range(2):
        bias_own, up_b_own, bias_far, up_b_far, gains, shifts, branch = unpack(vecs[layer])
        zero = jnp.zeros((local,), f32)
        b_in = jnp.stack([jnp.stack([b[0], zero, b[1]]) for b in (bias_own, bias_far)])[:, :, None]
        b_up = jnp.stack([up_b_own, up_b_far])[:, None]
        vec = jnp.concatenate([gains, shifts, branch], axis=0)
        start = state
        state, *kept = forward_layer(
            where, state, weights[layer], b_in, b_up, vec, seg_col, seg_row
        )
        saved.append(((start, *kept), vec))
        outputs.append(state)

    partials = [None, None]
    vectors = [None, None]
    grads_out = [None, None]
    for layer in (1, 0):
        kept, vec = saved[layer]
        grad, partials[layer], vectors[layer] = backward_layer(
            where, grad, kept, weights[layer], vec, seg_col, seg_row
        )
        grads_out[layer] = grad
    final, vec1, vec0 = sum_grads(copies, partials[1], partials[0], vectors[1], vectors[0])
    vec = pick(core == 0, vec0, vec1)
    g_in = final[: 3 * local].astype(f32).reshape(3, local, width).transpose(2, 0, 1)
    g_out, g_up, g_down = (final[rows].astype(f32) for rows in (where.out, where.up, where.down))
    b_in = jnp.stack([vec[9, :local], vec[9, 2 * block : 2 * block + local]])

    def rows_out(pair):
        both = jnp.stack(pair)
        send = lax.dynamic_slice_in_dim(both, side * quarter, quarter, 1)
        far = route(send, [(at(c, m), at(c, m ^ 2)) for c, m in every if c != m // 2])
        rows = pick(mine == 0, jnp.stack([send, far], 1), jnp.stack([far, send], 1))
        other = route(
            pick(mine == 0, rows[1], rows[0]),
            [(at(c, m), at(1 - c, m)) for c, m in every if c == m // 2],
        )
        here = pick(core == 0, rows[0], rows[1])
        return pick(core == mine, here, other)

    section_outputs = rows_out(outputs)
    input_grads = rows_out(grads_out).astype(f32)
    return (
        section_outputs[None],
        input_grads[None],
        vec[0:2][None],
        vec[2:4][None],
        g_in[None],
        b_in[None],
        g_out[None],
        g_up[None],
        vec[8][None],
        g_down[None],
        vec[4:6][None],
    )


def solution(mesh):
    in_specs = (
        P("dp", "mp", None),
        P("dp", "mp", None),
        P("dp", None),
        P("section", None, None),
        P("section", None, None),
        P("section", None, None, "mp"),
        P("section", None, "mp"),
        P("section", "mp", None),
        P("section", None, "mp"),
        P("section", "mp"),
        P("section", "mp", None),
        P("section", None, None),
    )
    out_specs = (
        P("section", "dp", "mp", None),
        P("section", "dp", "mp", None),
        P("section", None, None),
        P("section", None, None),
        P("section", None, None, "mp"),
        P("section", None, "mp"),
        P("section", "mp", None),
        P("section", None, "mp"),
        P("section", "mp"),
        P("section", "mp", None),
        P("section", None, None),
    )
    return jax.shard_map(
        per_device, mesh=mesh, in_specs=in_specs, out_specs=out_specs, check_vma=False
    )
```

```python
from functools import partial

import jax
import jax.numpy as jnp
from jax import lax
from jax.experimental import pallas as pl
from jax.experimental.pallas import tpu as pltpu
from jax.sharding import PartitionSpec as P

HEAD = 64
branch_scale = 12.0 ** (-0.5)
norm_eps = 1e-05
masked_score = -1000000000.0
block = 256
cube = 0.044715
root = 0.7978845608

f32 = jnp.float32
bf16 = jnp.bfloat16


def mm(left, right):
    return jnp.dot(left, right, preferred_element_type=f32)


def mm_nt(left, right):
    return lax.dot_general(left, right, (((1,), (1,)), ((), ())), preferred_element_type=f32)


def mm_tn(left, right):
    return lax.dot_general(left, right, (((0,), (0,)), ((), ())), preferred_element_type=f32)


def normalize(values):
    mean = jnp.mean(values, axis=-1, keepdims=True)
    centred = values - mean
    spread = jnp.mean(centred * centred, axis=-1, keepdims=True)
    rstd = lax.rsqrt(spread + norm_eps)
    return centred * rstd, rstd


def norm_back(normal, rstd, grad, gain):
    scaled = grad * gain
    first = jnp.mean(scaled, axis=-1, keepdims=True)
    second = jnp.mean(scaled * normal, axis=-1, keepdims=True)
    return (scaled - first - normal * second) * rstd


def head_lanes(heads):
    found = []
    for head in range(heads):
        start = (head // 2) * 2 * HEAD
        width = min(2 * HEAD, heads * HEAD - start)
        found.append((start, width, head % 2))
    return found


def own_lanes(value, width, upper):
    if width == HEAD:
        return value
    lane = lax.broadcasted_iota(jnp.int32, value.shape, 1)
    keep = (lane >= HEAD) if upper else (lane < HEAD)
    return jnp.where(keep, value, jnp.zeros_like(value))


def block_mask(seg_col, seg_row, rows, count):
    same = seg_col[0:count, :] == seg_row[:, rows]
    key = lax.broadcasted_iota(jnp.int32, (count, rows.stop - rows.start), 0)
    query = lax.broadcasted_iota(jnp.int32, (count, rows.stop - rows.start), 1) + rows.start
    return same & (key <= query)


MESH = pl.DeviceIdType.MESH


def attend_block(qkv_ref, mask, rows, count, logsum_ref):
    heads = qkv_ref.shape[2] // HEAD
    mixed = []
    for head, (lane, lanes, upper) in enumerate(head_lanes(heads)):
        cols = slice(lane, lane + lanes)
        queries = own_lanes(qkv_ref[0, rows, cols], lanes, upper) * bf16(HEAD ** (-0.5))
        scores = mm_nt(qkv_ref[1, 0:count, cols], queries)
        scores = jnp.where(mask, scores, masked_score)
        top = jnp.max(scores, axis=0, keepdims=True)
        weights = jnp.exp(scores - top)
        total = jnp.sum(weights, axis=0, keepdims=True)
        result = mm_tn(qkv_ref[2, 0:count, cols], weights.astype(bf16)) / total
        logsum_ref[head : head + 1, rows] = top + jnp.log(total)
        mixed.append((lanes, result))
    found = []
    for pair in range(0, heads, 2):
        lanes, result = mixed[pair]
        if lanes > HEAD:
            result = jnp.concatenate([result[:HEAD], mixed[pair + 1][1][HEAD:]], axis=0)
        found.append((pair * HEAD, lanes, result.T.astype(bf16)))
    return found


class Places:
    def __init__(self, local, units, width):
        self.qkv = [slice(part * local, (part + 1) * local) for part in range(3)]
        self.out = slice(3 * local, 4 * local)
        self.up = slice(4 * local, 4 * local + width)
        self.down = slice(4 * local + width, 4 * local + width + units)
        self.rows = 4 * local + width + units


class Places:
    def __init__(self, local, units, width):
        self.qkv = [slice(part * local, (part + 1) * local) for part in range(3)]
        self.out = slice(3 * local, 4 * local)
        self.up = slice(4 * local, 4 * local + width)
        self.down = slice(4 * local + width, 4 * local + width + units)
        self.rows = 4 * local + width + units


class Mail:
    def __init__(self, sems):
        self.sems, self.names = sems, {}

    def number(self, name):
        return self.names.setdefault(name, len(self.names))

    def copy(self, name, src, dst, device, sent=None):
        return pltpu.make_async_remote_copy(
            src_ref=src,
            dst_ref=dst,
            send_sem=self.sems.at[0, self.number(sent or name)],
            recv_sem=self.sems.at[1, self.number(name)],
            device_id=device,
            device_id_type=MESH,
        )


class Moves:
    def __init__(self, sems):
        self.sems, self.names, self.open = sems, {}, []

    def copy(self, name, src, dst):
        return pltpu.make_async_copy(src, dst, self.sems.at[self.names.setdefault(name, len(self.names))])

    def start(self, name, src, dst):
        copy = self.copy(name, src, dst)
        copy.start()
        self.open.append(copy)

    def finish(self):
        for copy in self.open:
            copy.wait()


def others(dp, copies):
    return [dp + 1 - 2 * lax.rem(dp, 2), dp + 2 - 4 * lax.rem(dp // 2, 2)]


class Here:
    def __init__(self):
        self.core, self.z, self.dp = (lax.axis_index(name) for name in ("section", "mp", "dp"))
        self.mine, self.side = self.z // 2, lax.rem(self.z, 2)
        self.next_z = self.z + 1 - 2 * self.side
        self.far_z = self.z + 2 - 4 * self.mine
        self.sibling = (1 - self.core, self.z, self.dp)
        self.partner = (self.core, self.next_z, self.dp)
        near = others(self.dp, 4)
        self.copies = near + [near[0] + near[1] - self.dp]
        self.peers = [(self.core, self.z, dp) for dp in self.copies]


def meet(devices):
    barrier = pltpu.get_barrier_semaphore()
    for device in devices:
        pl.semaphore_signal(barrier, inc=1, device_id=device, device_id_type=MESH)
    pl.semaphore_wait(barrier, len(devices))


def fill_segments(lengths_ref, row, seg_col, seg_row):
    docs = lengths_ref.shape[1]
    for ref, axis in ((seg_col, 0), (seg_row, 1)):
        positions = lax.broadcasted_iota(jnp.int32, ref.shape, axis)
        segs = jnp.zeros(ref.shape, jnp.int32)
        end = 0
        for doc in range(docs):
            end = end + lengths_ref[row, doc]
            segs = segs + (positions >= end).astype(jnp.int32)
        ref[...] = jnp.where(segs < docs, segs, docs + positions)


class RowsIn:
    def __init__(self, name, src, dst, here, mail, moves):
        self.name, self.src, self.dst, self.here, self.mail, self.moves = name, src, dst, here, mail, moves
        self.quarter = src.shape[1]

    def place(self, side):
        return self.dst.at[pl.ds(pl.multiple_of(side * self.quarter, self.quarter), self.quarter)]

    def near(self, src):
        return self.mail.copy((self.name, "near"), src, self.place(self.here.side), self.here.partner)

    def far(self):
        here = self.here
        return self.mail.copy(
            (self.name, "far"), self.src.at[1 - here.mine], self.place(here.side), (here.core, here.far_z, here.dp)
        )

    def own(self):
        return self.moves.copy((self.name, "own"), self.src.at[self.here.mine], self.place(self.here.side))

    def start(self):
        @pl.when(self.here.core == self.here.mine)
        def _():
            self.far().start()
            self.near(self.src.at[self.here.mine]).start()
            self.own().start()

    def forward(self):
        @pl.when(self.here.core != self.here.mine)
        def _():
            self.far().wait_recv()
            self.near(self.place(self.here.side)).start()

    def ready(self):
        self.mail.copy(
            (self.name, "near"), self.src.at[0], self.place(1 - self.here.side), self.here.partner
        ).wait_recv()

        @pl.when(self.here.core == self.here.mine)
        def _():
            self.own().wait()

    def finish(self):
        self.near(self.place(self.here.side)).wait_send()

        @pl.when(self.here.core == self.here.mine)
        def _():
            self.far().wait_send()


class ShardsIn:
    def __init__(self, layer, src, dst, here, mail, moves, pieces):
        self.layer, self.src, self.dst, self.here, self.mail, self.moves = layer, src, dst, here, mail, moves
        self.pieces = pieces

    def whole(self, piece):
        start, count, _ = self.pieces[piece]
        return slice(start, start + count)

    def given(self, piece):
        start, count, before = self.pieces[piece]
        return self.src[piece].at[slice(start - before, start - before + count)]

    def eighth(self, piece, dp, core, given=False):
        start, count, before = self.pieces[piece]
        part = count // 8
        start -= before if given else 0
        return pl.ds(pl.multiple_of(start + (lax.rem(dp, 4) * 2 + core) * part, 16), part)

    def own(self, piece):
        rows = self.whole(piece)
        return self.moves.copy((self.layer, "own", piece), self.given(piece), self.dst.at[0, rows])

    def twin(self, piece):
        rows = self.whole(piece)
        return self.mail.copy((self.layer, "twin", piece), self.given(piece), self.dst.at[0, rows], self.here.sibling)

    def far(self, piece, core):
        here = self.here
        rows = self.eighth(piece, here.dp, core)
        return self.mail.copy(
            (self.layer, "far", piece),
            self.src[piece].at[self.eighth(piece, here.dp, core, given=True)],
            self.dst.at[1, rows],
            (core, here.far_z, here.dp),
            sent=(self.layer, "far", piece, core),
        )

    def spread(self, piece, n):
        rows = self.eighth(piece, self.here.dp, self.here.core)
        return self.mail.copy(
            (self.layer, "spread", piece, n), self.dst.at[1, rows], self.dst.at[1, rows], self.here.peers[n]
        )

    def across(self, piece, n):
        dp = self.here.dp if n == 3 else self.here.copies[n]
        rows = self.eighth(piece, dp, self.here.core)
        return self.mail.copy(
            (self.layer, "across", piece, n), self.dst.at[1, rows], self.dst.at[1, rows], self.here.sibling
        )

    def start(self, piece):
        @pl.when(self.here.core == self.layer)
        def _():
            for core in range(2):
                self.far(piece, core).start()
            self.own(piece).start()
            self.twin(piece).start()

    def relay(self, piece):
        self.far(piece, 0).wait_recv()
        for n in range(3):
            self.spread(piece, n).start()
        self.across(piece, 3).start()

    def share(self, piece):
        for n in range(3):
            self.spread(piece, n).wait_recv()
            self.across(piece, n).start()

    def ready(self, piece):
        for n in range(4):
            self.across(piece, n).wait_recv()

        @pl.when(self.here.core == self.layer)
        def _():
            self.own(piece).wait()

        @pl.when(self.here.core != self.layer)
        def _():
            self.twin(piece).wait_recv()

    def finish(self, piece):
        for n in range(3):
            self.spread(piece, n).wait_send()
        for n in range(4):
            self.across(piece, n).wait_send()

        @pl.when(self.here.core == self.layer)
        def _():
            for core in range(2):
                self.far(piece, core).wait_send()
            self.twin(piece).wait_send()


class Vectors:
    def __init__(self, src, dst, here, mail):
        self.src, self.dst, self.here, self.mail = src, dst, here, mail

    def copies(self):
        here, mail = self.here, self.mail
        own, far = self.dst.at[here.core, 0], self.dst.at[here.core, 1]
        return [
            mail.copy("vec twin", self.src, own, here.sibling),
            mail.copy("vec far", self.src, far, (here.core, here.far_z, here.dp)),
            mail.copy("vec cross", self.src, far, (1 - here.core, here.far_z, here.dp)),
        ]

    def start(self):
        for copy in self.copies():
            copy.start()
        self.dst[self.here.core, 0] = self.src[...]

    def ready(self):
        for copy in self.copies():
            copy.wait()


KEPT = ("normed", "qkv", "logsum", "att", "middle", "upper", "hidden", "slope")
row_gain, row_shift, row_branch, row_up, row_query, row_value = 0, 2, 4, 6, 7, 8


def forward_kernel(
    where,
    pieces,
    inputs_ref,
    cotangent_ref,
    top_ref,
    up_ref,
    down_ref,
    gains_ref,
    shifts_ref,
    branch_ref,
    up_bias_ref,
    in_bias_ref,
    lengths_ref,
    *refs,
):
    names = ("weights", "vec", "grad", "states", "tail") + KEPT
    count = len(names)
    out = dict(zip(names, refs[:count]))
    kept = dict(zip(("weights", "grad", "states", "tail") + KEPT, refs[count : 2 * count - 1]))
    vec = out["vec"]
    seg_col, seg_row, pack_ref, qkv_out, att_out, low, got, mail_sems, move_sems = refs[2 * count - 1 :]
    here = Here()
    core = here.core
    mail, moves = Mail(mail_sems), Moves(move_sems)
    states = kept["states"]
    half = states.shape[1]
    local = where.qkv[0].stop
    blocks = half // block
    first = pl.multiple_of(core * half, half)
    rows_in = RowsIn("state", inputs_ref, states.at[0], here, mail, moves)
    grad_in = RowsIn("grad", cotangent_ref, kept["grad"], here, mail, moves)
    sources = (top_ref, top_ref, up_ref, down_ref)
    shards = [ShardsIn(n, sources, kept["weights"].at[n], here, mail, moves, pieces) for n in range(2)]
    vectors = Vectors(pack_ref, vec, here, mail)
    pack_ref[...] = jnp.zeros_like(pack_ref)
    pack_ref[row_gain : row_gain + 2, :] = gains_ref[...]
    pack_ref[row_shift : row_shift + 2, :] = shifts_ref[...]
    pack_ref[row_branch : row_branch + 2, :] = branch_ref[...]
    pack_ref[row_up : row_up + 1, :] = up_bias_ref[...]
    pack_ref[row_query : row_query + 1, 0:local] = in_bias_ref[0:1, :]
    pack_ref[row_value : row_value + 1, 0:local] = in_bias_ref[1:2, :]

    meet(
        [here.sibling, here.partner]
        + here.peers
        + [(here.core, here.far_z, here.dp), (1 - here.core, here.far_z, here.dp)]
    )
    rows_in.start()
    shards[0].start(0)
    vectors.start()
    shards[0].start(1)
    fill_segments(lengths_ref, here.mine, seg_col, seg_row)
    rows_in.forward()
    shards[0].relay(0)
    shards[0].start(2)
    shards[0].relay(1)
    shards[0].start(3)
    shards[0].share(0)
    vectors.ready()
    shards[0].share(1)

    later = []

    def tick():
        if later:
            later.pop(0)[1]()

    def upto(wanted):
        while any(label == wanted for label, _ in later):
            tick()

    def plan(label, *tasks):
        later.append((label, lambda: [task() for task in tasks]))

    plan("")
    plan("")
    plan("", partial(shards[0].relay, 2), partial(shards[1].start, 0))
    plan("", partial(shards[0].relay, 3))
    plan("", partial(shards[0].share, 2), partial(shards[1].start, 1))
    plan("units 0", partial(shards[0].share, 3))
    plan("", partial(shards[1].relay, 0), partial(shards[1].start, 2))
    plan("", partial(shards[1].relay, 1), partial(shards[1].start, 3))
    plan("heads 1", partial(shards[1].share, 0), partial(shards[1].share, 1))
    plan("", partial(shards[1].relay, 2))
    plan("", partial(shards[1].share, 2), grad_in.start)
    plan("", partial(shards[1].relay, 3))
    plan("", grad_in.forward)
    plan("units 1", partial(shards[1].share, 3))

    def layer_forward(layer):
        w_ref = kept["weights"].at[layer]
        v_ref = vec.at[layer]
        state_ref = states.at[layer]
        normed_ref, qkv_ref, logsum_ref, att_ref, middle_ref, upper_ref, hidden_ref, slope_ref = (
            kept[name].at[layer] for name in KEPT
        )

        def row(number, slot=0):
            return v_ref[slot, number : number + 1, :]

        def bias(slot, part):
            if part == 1:
                return 0.0
            number = row_query if part == 0 else row_value
            return v_ref[slot, number : number + 1, 0:local]

        def low_copy(index, rows):
            return mail.copy(
                ("low", layer, index, rows.start),
                low.at[layer, index, rows],
                got.at[layer, index, rows],
                here.partner,
            )

        def send_low(index, rows, value):
            low[layer, index, rows, :] = value.astype(bf16)
            low_copy(index, rows).start()

        def received(index, rows):
            low_copy(index, rows).wait()
            return low[layer, index, rows, :].astype(f32) + got[layer, index, rows, :].astype(f32)

        def save(name):
            moves.start((name, layer), kept[name].at[layer], out[name].at[layer])

        def qkv_copy(j):
            there = pl.ds(pl.multiple_of(first + j * block, block), block)
            return mail.copy(("qkv", layer, j), qkv_out.at[layer, j], qkv_ref.at[:, there, :], here.sibling)

        def project(j):
            rows = slice(j * block, (j + 1) * block)
            normal, _ = normalize(state_ref[rows, :].astype(f32))
            normed = (normal * row(row_gain) + row(row_shift)).astype(bf16)
            normed_ref[rows, :] = normed
            for part in range(3):
                weight = w_ref[1 - core, where.qkv[part], :]
                qkv_out[layer, j, part] = (mm_nt(normed, weight) + bias(1 - core, part)).astype(bf16)
            qkv_copy(j).start()
            there = pl.ds(pl.multiple_of(first + j * block, block), block)
            for part in range(3):
                weight = w_ref[core, where.qkv[part], :]
                qkv_ref[part, there, :] = (mm_nt(normed, weight) + bias(core, part)).astype(bf16)

        def att_copy(j):
            own = slice(j * block, (j + 1) * block)
            return mail.copy(("att", layer, j), att_out.at[layer, j], att_ref.at[core, own], here.sibling)

        upto(f"heads {layer}")
        if layer == 0:
            rows_in.ready()
        shards[layer].ready(0)
        shards[layer].ready(1)
        for i in range(2 * blocks):
            owner, j = i // blocks, i % blocks
            rows = slice(i * block, (i + 1) * block)
            own = slice(j * block, (j + 1) * block)
            count = (i + 1) * block
            if layer == 0:
                if i < blocks:
                    project(i)
                    tick()
            else:

                @pl.when(core == owner)
                def _():
                    result = before["middle"](own) + branch_scale * (
                        before["received"](1, own) + before["row"](row_branch + 1)
                    )
                    state_ref[own, :] = result.astype(bf16)
                    project(j)

            @pl.when(core != owner)
            def _():
                qkv_copy(j).wait_recv()

            mask = block_mask(seg_col, seg_row, rows, count)
            found = attend_block(qkv_ref, mask, rows, count, logsum_ref)

            @pl.when(core == owner)
            def _():
                for lane, lanes, result in found:
                    att_ref[core, own, lane : lane + lanes] = result
                att_copy(j).wait_recv()
                send_low(0, own, sum(mm(att_ref[k, own, :], w_ref[k, where.out, :]) for k in range(2)))

            @pl.when(core != owner)
            def _():
                for lane, lanes, result in found:
                    att_out[layer, j, :, lane : lane + lanes] = result
                att_copy(j).start()

            tick()
        for j in range(blocks):
            qkv_copy(j).wait_send()
            att_copy(j).wait_send()
        save("normed")
        save("qkv")
        save("att")
        save("logsum")

        for j in range(blocks):
            rows = slice(j * block, (j + 1) * block)
            middle = state_ref[rows, :].astype(f32) + branch_scale * (received(0, rows) + row(row_branch))
            middle_ref[rows, :] = middle
            normal, _ = normalize(middle)
            upper = (normal * row(row_gain + 1) + row(row_shift + 1)).astype(bf16)
            upper_ref[rows, :] = upper
            if j == 0:
                upto(f"units {layer}")
                shards[layer].ready(2)
                shards[layer].ready(3)
            total = None
            for k in range(2):
                pre = mm(upper, w_ref[k, where.up, :]) + row(row_up, k)
                square = pre * pre
                curve = jnp.tanh(root * pre * (1.0 + cube * square))
                rise = 0.5 * (1.0 + curve)
                hidden = (pre * rise).astype(bf16)
                hidden_ref[k, rows, :] = hidden
                slope = rise + pre * (rise * (1.0 - curve)) * (root * (1.0 + 3.0 * cube * square))
                slope_ref[k, rows, :] = slope.astype(bf16)
                term = mm(hidden, w_ref[k, where.down, :])
                total = term if total is None else total + term
            if layer == 0:
                send_low(1, rows, total)
            else:
                kept["tail"][rows, :] = total.astype(bf16)
            tick()
        for name in ("middle", "upper", "hidden", "slope"):
            save(name)
        moves.start(("weights", layer), w_ref, out["weights"].at[layer])
        if layer == 1:
            moves.start("tail", kept["tail"], out["tail"])
            return
        before.update(middle=lambda rows: middle_ref[rows, :], received=received, row=row)

    before = {}
    for layer in range(2):
        layer_forward(layer)
    while later:
        tick()
    moves.start("states", states, out["states"])
    grad_in.ready()
    moves.start("grad", kept["grad"], out["grad"])
    rows_in.finish()
    grad_in.finish()
    for shard in shards:
        for piece in range(len(pieces)):
            shard.finish(piece)
    moves.finish()


def forward_pass(where, inputs, cotangent, shard, vectors, lengths):
    quarter, width = inputs.shape[1:]
    half, length = 2 * quarter, 4 * quarter
    local = where.qkv[0].stop
    units = where.down.stop - where.down.start
    blocks = half // block
    top = 4 * local
    pieces = [(0, top // 2, 0), (top // 2, top // 2, 0), (top, width, top), (top + width, units, top + width)]
    vmem = pl.BlockSpec(memory_space=pltpu.VMEM)
    hbm = pl.BlockSpec(memory_space=pl.ANY)
    shapes = {
        "weights": ((2, 2, where.rows, width), bf16),
        "vec": ((2, 2, 16, width), f32),
        "grad": ((half, width), bf16),
        "states": ((2, half, width), bf16),
        "tail": ((half, width), bf16),
        "normed": ((2, half, width), bf16),
        "qkv": ((2, 3, length, local), bf16),
        "logsum": ((2, local // HEAD, length), f32),
        "att": ((2, 2, half, local), bf16),
        "middle": ((2, half, width), f32),
        "upper": ((2, half, width), bf16),
        "hidden": ((2, 2, half, units), bf16),
        "slope": ((2, 2, half, units), bf16),
    }
    found = pl.pallas_call(
        partial(forward_kernel, where, pieces),
        out_shape=[jax.ShapeDtypeStruct(*entry) for entry in shapes.values()],
        in_specs=[hbm] * 5 + [vmem] * 5 + [pl.BlockSpec(memory_space=pltpu.SMEM)],
        out_specs=[vmem if name == "vec" else hbm for name in shapes],
        scratch_shapes=[pltpu.VMEM(*entry) for name, entry in shapes.items() if name != "vec"]
        + [
            pltpu.VMEM((length, 1), jnp.int32),
            pltpu.VMEM((1, length), jnp.int32),
            pltpu.VMEM((16, width), f32),
            pltpu.VMEM((2, blocks, 3, block, local), bf16),
            pltpu.VMEM((2, blocks, block, local), bf16),
            pltpu.VMEM((2, 2, half, width), bf16),
            pltpu.VMEM((2, 2, half, width), bf16),
            pltpu.SemaphoreType.DMA((2, 128)),
            pltpu.SemaphoreType.DMA((64,)),
        ],
        compiler_params=pltpu.CompilerParams(
            vmem_limit_bytes=58 * 2**20, collective_id=1, has_side_effects=True
        ),
        name="forward_pass",
    )(inputs, cotangent, *shard, *vectors, lengths)
    return dict(zip(shapes, found))


def attend_back_block(qkv_ref, grad_ref, mask, rows, count, logsum_ref, dqkv_ref, dk_sum, dv_sum):
    heads = qkv_ref.shape[2] // HEAD
    scale = bf16(HEAD ** (-0.5))
    mixed = []
    for head, (lane, lanes, upper) in enumerate(head_lanes(heads)):
        cols = slice(lane, lane + lanes)
        queries = own_lanes(qkv_ref[0, rows, cols], lanes, upper) * scale
        grads = own_lanes(grad_ref[rows, cols], lanes, upper)
        keys = qkv_ref[1, 0:count, cols]
        scores = mm_nt(keys, queries)
        scores = jnp.where(mask, scores, masked_score)
        probs = jnp.exp(scores - logsum_ref[head : head + 1, rows])
        grad_probs = mm_nt(qkv_ref[2, 0:count, cols], grads)
        dv_sum[0:count, cols] += mm(probs.astype(bf16), grads)
        term = probs * grad_probs
        delta = jnp.sum(term, axis=0, keepdims=True)
        grad_scores = (term - probs * delta).astype(bf16)
        dk_sum[0:count, cols] += mm(grad_scores, queries)
        mixed.append((lanes, mm_tn(keys, grad_scores)))
    for pair in range(0, heads, 2):
        lane = pair * HEAD
        lanes, result = mixed[pair]
        if lanes > HEAD:
            result = jnp.concatenate([result[:HEAD], mixed[pair + 1][1][HEAD:]], axis=0)
        dqkv_ref[0, rows, lane : lane + lanes] = (result.T * HEAD ** (-0.5)).astype(bf16)


class RowsOut:
    def __init__(self, name, layer, src, dst, here, mail, moves):
        self.name, self.layer, self.src, self.dst = name, layer, src, dst
        self.here, self.mail, self.moves = here, mail, moves

    def ends(self):
        quarter = self.dst.shape[1]
        rows = pl.ds(pl.multiple_of(self.here.side * quarter, quarter), quarter)
        src = self.src if self.src.shape[0] == quarter else self.src.at[rows]
        return src, self.dst.at[self.here.mine]

    def home(self):
        return self.mail.copy((self.name, self.layer, "home"), *self.ends(), self.here.sibling)

    def away(self):
        device = (self.layer, self.here.far_z, self.here.dp)
        return self.mail.copy((self.name, self.layer, "away"), *self.ends(), device)

    def local(self):
        return self.moves.copy((self.name, self.layer), *self.ends())

    def cases(self, away, home, local):
        core, mine = self.here.core, self.here.mine
        pl.when(core != mine)(away)
        pl.when((core == mine) & (core != self.layer))(home)
        pl.when((core == mine) & (core == self.layer))(local)

    def start(self):
        self.cases(
            lambda: self.away().start(), lambda: self.home().start(), lambda: self.local().start()
        )

    def finish(self):
        self.cases(
            lambda: self.away().wait_send(), lambda: self.home().wait_send(), lambda: self.local().wait()
        )

        @pl.when(self.here.core == self.layer)
        def _():
            self.away().wait_recv()

            @pl.when(self.here.core != self.here.mine)
            def _():
                self.home().wait_recv()


def more_bits(copies):
    return [1 << n for n in range(2, copies.bit_length()) if (1 << n) < copies]


def flipped(dp, bit):
    return dp + bit - 2 * bit * lax.rem(dp // bit, 2)


class GradSum:
    def __init__(self, layer, part, buffers, final, here, mail, moves, pieces, place, copies):
        self.layer, self.part, self.final, self.pieces = layer, part, final, pieces
        self.place = place
        self.twin, self.first, self.second, self.cross, self.groups = buffers
        self.here, self.mail, self.moves = here, mail, moves
        self.bits_above = more_bits(copies)
        self.slot = lax.rem(here.core + layer, 2)
        self.bits = [lax.rem(here.dp, 2), lax.rem(here.dp // 2, 2)]
        self.stages = 6 + len(self.bits_above)

    @staticmethod
    def scratch(rows, places, width, copies):
        above = len(more_bits(copies))
        return [
            pltpu.VMEM((places, rows, width), bf16),
            pltpu.VMEM((places, 2, rows // 4, width), bf16),
            pltpu.VMEM((places, 2, rows // 8, width), bf16),
            pltpu.VMEM((2 * places, 2, rows // 8, width), bf16),
            pltpu.VMEM((max(1, above), 2 * places if above else 1, 2, rows // 8, width), bf16),
        ]

    def name(self, piece, kind, half=0):
        return ("sum", self.layer, self.pieces[piece], kind, half)

    def span(self, piece, start, count):
        return pl.ds(pl.multiple_of(self.pieces[piece][0] + start, 16), count)

    def chunk(self, piece, half, outer, inner):
        eighth = self.pieces[piece][1] // 8
        return half * 4 * eighth + outer * 2 * eighth + inner * eighth

    def device(self, axis):
        return self.here.peers[axis]

    def ring(self, piece):
        return self.place[piece] % self.twin.shape[0]

    def twin_copy(self, piece):
        start, count = self.pieces[piece]
        return self.mail.copy(
            self.name(piece, "twin"),
            self.part.at[1 - self.slot, slice(start, start + count)],
            self.twin.at[self.ring(piece)],
            self.here.sibling,
        )

    def first_copy(self, piece, half):
        src = self.span(piece, self.chunk(piece, half, 1 - self.bits[half], 0), self.pieces[piece][1] // 4)
        dst = self.first.at[self.ring(piece), half]
        return self.mail.copy(self.name(piece, "first", half), self.part.at[self.slot, src], dst, self.device(half))

    def second_copy(self, piece, half):
        axis = 1 - half
        src = self.span(
            piece, self.chunk(piece, half, self.bits[half], 1 - self.bits[axis]), self.pieces[piece][1] // 8
        )
        dst = self.second.at[self.ring(piece), half]
        return self.mail.copy(self.name(piece, "second", half), self.part.at[self.slot, src], dst, self.device(axis))

    def own(self, piece, half):
        return self.span(
            piece, self.chunk(piece, half, self.bits[half], self.bits[1 - half]), self.pieces[piece][1] // 8
        )

    def cross_copy(self, piece, half):
        return self.mail.copy(
            self.name(piece, "cross", half),
            self.part.at[self.slot, self.own(piece, half)],
            self.cross.at[self.place[piece], half],
            (1 - self.here.core, self.here.far_z, self.here.dp),
        )

    def group_copy(self, step, piece, half):
        here = self.here
        return self.mail.copy(
            self.name(piece, ("group", step), half),
            self.part.at[self.slot, self.own(piece, half)],
            self.groups.at[step, self.place[piece], half],
            (here.core, here.z, flipped(here.dp, self.bits_above[step])),
        )

    def gather_copies(self, piece, half):
        rows = self.own(piece, half)
        return [
            self.mail.copy(
                self.name(piece, ("gather", n), half),
                self.part.at[self.slot, rows],
                self.final.at[rows],
                self.here.peers[n],
            )
            for n in range(3)
        ]

    def keep_copy(self, piece, half):
        rows = self.own(piece, half)
        return self.moves.copy(self.name(piece, "keep", half), self.part.at[self.slot, rows], self.final.at[rows])

    def stage(self, number, piece):
        if number < 4:
            (self.stage0, self.stage1, self.stage2, self.stage3)[number](piece)
        elif number < self.stages - 1:
            self.stage4(number - 4, piece)
        else:
            self.stage5(piece)

    def add(self, rows, other):
        value = self.part[self.slot, rows, :].astype(f32) + other.astype(f32)
        self.part[self.slot, rows, :] = value.astype(bf16)

    def stage0(self, piece):
        self.twin_copy(piece).start()

    def stage1(self, piece):
        self.twin_copy(piece).wait_recv()
        start, count = self.pieces[piece]
        self.add(slice(start, start + count), self.twin[self.ring(piece)])
        for half in range(2):
            self.first_copy(piece, half).start()

    def stage2(self, piece):
        count = self.pieces[piece][1] // 4
        for half in range(2):
            self.first_copy(piece, half).wait()
            rows = self.span(piece, self.chunk(piece, half, self.bits[half], 0), count)
            self.add(rows, self.first[self.ring(piece), half])
            self.second_copy(piece, half).start()

    def stage3(self, piece):
        for half in range(2):
            self.second_copy(piece, half).wait()
            self.add(self.own(piece, half), self.second[self.ring(piece), half])

            @pl.when(self.here.core != self.layer)
            def _():
                self.cross_copy(piece, half).start()

    def stage4(self, step, piece):
        @pl.when(self.here.core == self.layer)
        def _():
            for half in range(2):
                if step == 0:
                    self.cross_copy(piece, half).wait_recv()
                    self.add(self.own(piece, half), self.cross[self.place[piece], half])
                else:
                    self.group_copy(step - 1, piece, half).wait()
                    self.add(self.own(piece, half), self.groups[step - 1, self.place[piece], half])
                if step < len(self.bits_above):
                    self.group_copy(step, piece, half).start()
                else:
                    for copy in self.gather_copies(piece, half):
                        copy.start()
                    self.keep_copy(piece, half).start()

    def stage5(self, piece):
        self.twin_copy(piece).wait_send()

        @pl.when(self.here.core == self.layer)
        def _():
            for half in range(2):
                for copy in self.gather_copies(piece, half):
                    copy.wait()
                self.keep_copy(piece, half).wait()

        @pl.when(self.here.core != self.layer)
        def _():
            for half in range(2):
                self.cross_copy(piece, half).wait_send()


class VectorSum:
    def __init__(self, layer, part, got, out, here, mail, copies):
        self.layer, self.part, self.got, self.out, self.mail = layer, part, got, out, mail
        self.devices = [here.partner, here.sibling] + here.peers[:2]
        self.devices += [(here.core, here.z, flipped(here.dp, bit)) for bit in more_bits(copies)]
        self.devices.append((here.core, here.far_z, here.dp))
        self.stages = len(self.devices) + 1

    def copy(self, step):
        return self.mail.copy(("vec", self.layer, step), self.part, self.got.at[step], self.devices[step])

    def stage(self, number, _):
        if number > 0:
            step = number - 1
            self.copy(step).wait()
            if number == 1:
                self.part[12:14, :] += self.got[step, 12:14, :]
            elif number < self.stages - 1:
                self.part[...] += self.got[step]
            else:
                self.out[...] = self.part[...] + self.got[step]
                self.out[8:10, :] = self.part[8:10, :] + self.got[step, 10:12, :]
        if number < self.stages - 1:
            self.copy(number).start()


class Pipeline:
    def __init__(self, gap):
        self.gap, self.now = gap, 0
        self.waiting, self.running = [], []

    def add(self, one, piece=0):
        self.waiting.append((one, piece))

    def tick(self, fresh=1):
        self.now += 1
        for item in self.running:
            one, piece, stage, due = item
            if due <= self.now:
                one.stage(stage, piece)
                item[2:] = [stage + 1, self.now + self.gap]
        for one, piece in self.waiting[:fresh]:
            one.stage(0, piece)
            self.running.append([one, piece, 1, self.now + self.gap])
        self.waiting = self.waiting[fresh:]
        self.running = [item for item in self.running if item[2] < item[0].stages]

    def hurry(self, ticks=0):
        self.gap = 1
        for item in self.running:
            item[3] = self.now + 1
        for _ in range(ticks):
            self.tick(fresh=3)

    def drain(self):
        self.hurry()
        while self.waiting or self.running:
            self.now += 1000
            self.tick(fresh=2)


SAVED = ("state",) + KEPT


def backward_kernel(where, copies, *refs):
    refs = list(refs)

    def take(count):
        found = refs[:count]
        del refs[:count]
        return found

    (grad_hbm, w_hbm, vec_ref, lengths_ref, states_hbm, tail_hbm) = take(6)
    kept_hbm = dict(zip(KEPT, take(len(KEPT))))
    (states_out, grads_out, final, vec_out) = take(4)
    grads, w_ref = take(2)
    saved = dict(zip(SAVED, take(len(SAVED))))
    (
        d_refs,
        gz_ref,
        dmiddle_ref,
        datt_out,
        datt_ref,
        dqkv_ref,
        dk_sum,
        dv_sum,
        dmix_ref,
        low,
        got,
        tail_low,
        tail_got,
        seg_col,
        seg_row,
        d_vecs,
        got_vecs,
    ) = take(17)
    buffers = take(5)
    mail_sems, move_sems = take(2)
    start_ref, normed_ref, qkv_ref, logsum_ref, att_ref, middle_ref, upper_ref, hidden_ref, slope_ref = (
        saved[name] for name in SAVED
    )
    dpre_ref = slope_ref
    gy_ref = gz_ref

    here = Here()
    core = here.core
    mail, moves = Mail(mail_sems), Moves(move_sems)
    half = dmiddle_ref.shape[0]
    blocks = half // block
    first = pl.multiple_of(core * half, half)
    order = list(range(blocks))[::-1]
    heads = slice(0, where.out.start)

    def load_copy(layer, name):
        if isinstance(name, slice):
            return moves.copy((layer, name.start), w_hbm.at[layer, :, name], w_ref.at[:, name])
        src = states_hbm if name == "state" else kept_hbm[name]
        return moves.copy((layer, name), src.at[layer], saved[name])

    def load(layer, *names):
        for name in names:
            load_copy(layer, name).start()

    def need(layer, *names):
        for name in names:
            load_copy(layer, name).wait()

    groups = [
        (where.down, "slope", where.up, "hidden", "upper"),
        ("middle", where.out),
        ("qkv", "logsum", "att"),
        (heads, "normed", "state"),
    ]
    grad_load = moves.copy("grad", grad_hbm, grads.at[1])
    grad_load.start()
    for group in groups:
        load(1, *group)
    tail_load = moves.copy("tail", tail_hbm, tail_low)
    tail_load.start()
    top = where.out.stop
    pieces = [
        (rows.start + n * ((rows.stop - rows.start) // 2), (rows.stop - rows.start) // 2)
        for rows in (where.down, where.up, slice(0, top))
        for n in range(2)
    ]
    meet(
        [here.sibling, here.partner]
        + here.peers
        + [(core, here.far_z, here.dp), (1 - core, here.far_z, here.dp)]
        + [(core, here.z, flipped(here.dp, bit)) for bit in more_bits(copies)]
    )
    line = Pipeline(4)
    sums = [
        GradSum(
            layer,
            d_refs.at[layer],
            buffers,
            final,
            here,
            mail,
            moves,
            pieces,
            [(1 - layer) * len(pieces) + n for n in range(len(pieces))],
            copies,
        )
        for layer in range(2)
    ]
    vectors = [
        VectorSum(layer, d_vecs.at[layer], got_vecs.at[layer], vec_out.at[layer], here, mail, copies)
        for layer in range(2)
    ]
    fill_segments(lengths_ref, here.mine, seg_col, seg_row)
    d_vecs[...] = jnp.zeros_like(d_vecs)
    rows_out = [
        RowsOut("state", 0, states_hbm.at[1], states_out, here, mail, moves),
        RowsOut("state", 1, tail_got, states_out, here, mail, moves),
        RowsOut("grad", 1, grads.at[0], grads_out, here, mail, moves),
        RowsOut("grad", 0, grads.at[1], grads_out, here, mail, moves),
    ]

    def pair_copy(layer, index, rows):
        return mail.copy(
            ("low", layer, index, rows.start), low.at[index, rows], got.at[index, rows], here.partner
        )

    def send_low(layer, index, rows, value):
        low[index, rows, :] = value.astype(bf16)
        pair_copy(layer, index, rows).start()

    def received(layer, index, rows):
        pair_copy(layer, index, rows).wait()
        return low[index, rows, :].astype(f32) + got[index, rows, :].astype(f32)

    def own_rows(j):
        return slice(j * block, (j + 1) * block)

    def total(value):
        return jnp.sum(value, axis=0, keepdims=True)

    def vector(layer, number):
        return vec_ref[layer, 0, number : number + 1, :]

    def note(layer, number, value):
        d_vecs[layer, number : number + 1, :] += total(value)

    def units_back(layer, j):
        rows = own_rows(j)
        gz = branch_scale * grads[layer, rows, :].astype(f32)
        note(layer, 5, gz)
        gz = gz.astype(bf16)
        gz_ref[rows, :] = gz
        part = None
        for k in range(2):
            dpre = (mm_nt(gz, w_ref[k, where.down, :]) * slope_ref[k, rows, :].astype(f32)).astype(bf16)
            dpre_ref[k, rows, :] = dpre
            term = mm_nt(dpre, w_ref[k, where.up, :])
            part = term if part is None else part + term
        send_low(layer, 0, rows, part)

    def units_weights(layer):
        d_ref = d_refs.at[layer]
        need(layer, "hidden", "upper")
        for k in range(2):
            d_ref[k, where.down, :] = mm_tn(hidden_ref[k], gz_ref[...]).astype(bf16)
            line.tick()
        line.add(sums[layer], 0)
        line.add(sums[layer], 1)
        for k in range(2):
            d_ref[k, where.up, :] = mm_tn(upper_ref[...], dpre_ref[k]).astype(bf16)
            note(layer, 8 + 2 * k, dpre_ref[k].astype(f32))
            line.tick()
        line.add(sums[layer], 2)
        line.add(sums[layer], 3)
        line.tick()

    def datt_copy(layer, j):
        there = pl.ds(pl.multiple_of(first + j * block, block), block)
        return mail.copy(("datt", layer, j), datt_out.at[j], datt_ref.at[there, :], here.sibling)

    def middle_back(layer, j):
        rows = own_rows(j)
        d_upper = received(layer, 0, rows)
        normal, rstd = normalize(middle_ref[rows, :])
        note(layer, 1, d_upper * normal)
        note(layer, 3, d_upper)
        d_middle = grads[layer, rows, :].astype(f32) + norm_back(
            normal, rstd, d_upper, vector(layer, row_gain + 1)
        )
        dmiddle_ref[rows, :] = d_middle
        gy = branch_scale * d_middle
        note(layer, 4, gy)
        gy = gy.astype(bf16)
        gy_ref[rows, :] = gy
        datt_out[j] = mm_nt(gy, w_ref[1 - core, where.out, :]).astype(bf16)
        datt_copy(layer, j).start()
        there = pl.ds(pl.multiple_of(first + j * block, block), block)
        datt_ref[there, :] = mm_nt(gy, w_ref[core, where.out, :]).astype(bf16)

    def mix_copy(layer, j):
        return mail.copy(
            ("mix", layer, j),
            dqkv_ref.at[:, pl.ds(pl.multiple_of(half - first + j * block, block), block), :],
            dmix_ref.at[core, :, pl.ds(j * block, block), :],
            here.sibling,
        )

    def finish(layer, i):
        owner, j = i // blocks, i % blocks
        rows = slice(i * block, (i + 1) * block)
        dqkv_ref[1, rows, :] = dk_sum[rows, :].astype(bf16)
        dqkv_ref[2, rows, :] = dv_sum[rows, :].astype(bf16)

        @pl.when(core == owner)
        def _():
            dmix_ref[core, :, own_rows(j), :] = dqkv_ref[:, rows, :]

        @pl.when(core != owner)
        def _():
            mix_copy(layer, j).start()

    def attention_back(layer):
        dk_sum[...] = jnp.zeros_like(dk_sum)
        dv_sum[...] = jnp.zeros_like(dv_sum)
        need(layer, "qkv", "logsum", "att")
        left = list(range(2 * blocks))
        for j in order:
            datt_copy(layer, j).wait()
            for i in (blocks + j, j):
                rows = slice(i * block, (i + 1) * block)
                count = (i + 1) * block
                mask = block_mask(seg_col, seg_row, rows, count)
                attend_back_block(
                    qkv_ref, datt_ref, mask, rows, count, logsum_ref, dqkv_ref, dk_sum, dv_sum
                )
                left.remove(i)
                if j == 0:
                    for done in range(2 * blocks)[::-1]:
                        if done > max(left, default=-1) and done // blocks == i // blocks:
                            finish(layer, done)
                line.tick()

    def heads_part(rows):
        part = None
        for k in range(2):
            for p in range(3):
                term = mm(dmix_ref[k, p, rows, :], w_ref[k, where.qkv[p], :])
                part = term if part is None else part + term
        return part

    def heads_back(layer, j):
        rows = own_rows(j)
        mix_copy(layer, j).wait_recv()
        send_low(layer, 1, rows, heads_part(rows))
        line.tick()

    quarter = states_out.shape[1]

    def side_rows(side):
        return pl.ds(pl.multiple_of(side * quarter, quarter), quarter)

    def last_copy():
        rows = side_rows(1 - here.side)
        return mail.copy("last", low.at[1, rows], got.at[1, rows], here.partner)

    def last_heads_back():
        for j in order:
            mix_copy(0, j).wait_recv()
        for side in (1 - here.side, here.side):
            rows = side_rows(side)
            part = heads_part(rows)
            low[1, rows, :] = part.astype(bf16)
            if side is not here.side:
                last_copy().start()
            normal, _ = normalize(start_ref[rows, :].astype(f32))
            note(0, 12, part * normal)
            note(0, 13, part)
            line.tick()

    def last_state_back():
        rows = side_rows(here.side)
        last_copy().wait()
        d_normed = low[1, rows, :].astype(f32) + got[1, rows, :].astype(f32)
        normal, rstd = normalize(start_ref[rows, :].astype(f32))
        d_state = dmiddle_ref[rows, :] + norm_back(normal, rstd, d_normed, vector(0, row_gain))
        grads[1, rows, :] = d_state.astype(bf16)

    def heads_weights(layer):
        d_ref = d_refs.at[layer]
        for k in range(2):
            d_ref[k, where.out, :] = mm_tn(att_ref[k], gy_ref[...]).astype(bf16)
        line.tick()
        for k in range(2):
            for p in range(3):
                d_ref[k, where.qkv[p], :] = mm_tn(dmix_ref[k, p], normed_ref[...]).astype(bf16)
            for n, p in enumerate((0, 2)):
                local = dmix_ref.shape[3]
                lanes = slice(n * 2 * block, n * 2 * block + local)
                d_vecs[layer, 9 + 2 * k : 10 + 2 * k, lanes] = total(dmix_ref[k, p].astype(f32))
            if k == 0:
                line.tick()
        line.add(sums[layer], 4)
        line.add(sums[layer], 5)
        line.tick()

    def state_back(layer, j):
        rows = own_rows(j)
        d_normed = received(layer, 1, rows)
        normal, rstd = normalize(start_ref[rows, :].astype(f32))
        note(layer, 0, d_normed * normal)
        note(layer, 2, d_normed)
        d_state = dmiddle_ref[rows, :] + norm_back(normal, rstd, d_normed, vector(layer, row_gain))
        grads[1 - layer, rows, :] = d_state.astype(bf16)

    def tail_copy():
        return mail.copy("tail", tail_low.at[side_rows(1 - here.side)], tail_got, here.partner)

    grad_load.wait()
    need(1, where.down, "slope", where.up)
    for j in order:
        units_back(1, j)
    for layer in (1, 0):
        units_weights(layer)
        if layer == 1:
            load(0, *groups[0])
            rows_out[0].start()
        need(layer, "middle", where.out)
        for j in order:
            line.tick()
            middle_back(layer, j)
            line.tick()
        if layer == 1:
            tail_load.wait()
            tail_copy().start()
        attention_back(layer)
        need(layer, heads, "normed", "state")
        if layer == 1:
            for j in order:
                heads_back(layer, j)
            tail_copy().wait()
            rows = side_rows(here.side)
            branch = tail_low[rows, :].astype(f32) + tail_got[...].astype(f32) + vector(1, row_branch + 1)
            tail_got[...] = (middle_ref[rows, :] + branch_scale * branch).astype(bf16)
            rows_out[1].start()
            load(0, *groups[1])
        else:
            last_heads_back()
        heads_weights(layer)
        if layer == 1:
            load(0, *groups[2])
            need(0, where.down, "slope", where.up)
        if layer == 1:
            for j in order:
                line.tick()
                state_back(1, j)
                units_back(0, j)
                line.tick()
            load(0, *groups[3])
            rows_out[2].start()
            line.add(vectors[1])
        else:
            line.add(vectors[0])
            line.tick(fresh=3)
            line.hurry()
            last_state_back()
            rows_out[3].start()
        for j in order:
            mix_copy(layer, j).wait_send()
    line.drain()
    for one in rows_out:
        one.finish()


def backward_pass(where, copies, kept, lengths):
    grad = kept["grad"]
    half, width = grad.shape
    quarter, length = half // 2, 2 * half
    local = where.qkv[0].stop
    blocks = half // block
    shape = jax.ShapeDtypeStruct
    vmem = pl.BlockSpec(memory_space=pltpu.VMEM)
    hbm = pl.BlockSpec(memory_space=pl.ANY)
    smem = pl.BlockSpec(memory_space=pltpu.SMEM)
    operands = [grad, kept["weights"], kept["vec"], lengths, kept["states"], kept["tail"]]
    operands += [kept[name] for name in KEPT]
    above = len(more_bits(copies))
    scratch = [
        pltpu.VMEM((2, half, width), bf16),
        pltpu.VMEM((2, where.rows, width), bf16),
        pltpu.VMEM((half, width), bf16),
    ]
    scratch += [pltpu.VMEM(kept[name].shape[1:], kept[name].dtype) for name in KEPT]
    scratch += [
        pltpu.VMEM((2, 2, where.rows, width), bf16),
        pltpu.VMEM((half, width), bf16),
        pltpu.VMEM((half, width), f32),
        pltpu.VMEM((blocks, block, local), bf16),
        pltpu.VMEM((length, local), bf16),
        pltpu.VMEM((3, length, local), bf16),
        pltpu.VMEM((length, local), f32),
        pltpu.VMEM((length, local), f32),
        pltpu.VMEM((2, 3, half, local), bf16),
        pltpu.VMEM((2, half, width), bf16),
        pltpu.VMEM((2, half, width), bf16),
        pltpu.VMEM((half, width), bf16),
        pltpu.VMEM((quarter, width), bf16),
        pltpu.VMEM((length, 1), jnp.int32),
        pltpu.VMEM((1, length), jnp.int32),
        pltpu.VMEM((2, 16, width), f32),
        pltpu.VMEM((2, 5 + above, 16, width), f32),
    ]
    scratch += GradSum.scratch(where.out.stop // 2, 6, width, copies)
    scratch += [pltpu.SemaphoreType.DMA((2, 192 + 96 * above)), pltpu.SemaphoreType.DMA((64,))]
    return pl.pallas_call(
        partial(backward_kernel, where, copies),
        out_shape=[
            shape((2, quarter, width), bf16),
            shape((2, quarter, width), bf16),
            shape((where.rows, width), bf16),
            shape((2, 16, width), f32),
        ],
        in_specs=[hbm, hbm, vmem, smem, hbm, hbm] + [hbm] * len(KEPT),
        out_specs=[hbm, hbm, hbm, vmem],
        scratch_shapes=scratch,
        compiler_params=pltpu.CompilerParams(
            vmem_limit_bytes=61 * 2**20, collective_id=2, has_side_effects=True
        ),
        name="backward_pass",
    )(*operands)


def per_device(
    inputs,
    cotangent,
    lengths,
    norm_gains,
    norm_shifts,
    in_weight,
    in_bias,
    out_weight,
    up_weight,
    up_bias,
    down_weight,
    branch_bias,
):
    core = lax.axis_index("section")
    copies = lax.axis_size("dp")
    width = inputs.shape[2]
    local = in_weight.shape[3]
    units = up_weight.shape[2]

    def pick(flag, yes, no):
        return jnp.where(flag, yes, no)

    where = Places(local, units, width)
    top = jnp.concatenate([in_weight[0].transpose(1, 2, 0).reshape(3 * local, width), out_weight[0]])
    kept = forward_pass(
        where,
        inputs,
        cotangent,
        (top, up_weight[0], down_weight[0]),
        (norm_gains[0], norm_shifts[0], branch_bias[0], up_bias, in_bias[0]),
        lengths,
    )
    section_outputs, input_grads, final, vecs = backward_pass(where, copies, kept, lengths)
    vec = pick(core == 0, vecs[0], vecs[1])
    g_in = final[: 3 * local].astype(f32).reshape(3, local, width).transpose(2, 0, 1)
    g_out, g_up, g_down = (final[rows].astype(f32) for rows in (where.out, where.up, where.down))
    b_in = jnp.stack([vec[9, :local], vec[9, 2 * block : 2 * block + local]])

    return (
        section_outputs[None],
        input_grads.astype(f32)[None],
        (vec[0:2] + jnp.pad(vec[12:13], ((0, 1), (0, 0))))[None],
        (vec[2:4] + jnp.pad(vec[13:14], ((0, 1), (0, 0))))[None],
        g_in[None],
        b_in[None],
        g_out[None],
        g_up[None],
        vec[8][None],
        g_down[None],
        vec[4:6][None],
    )


def solution(mesh):
    in_specs = (
        P("dp", "mp", None),
        P("dp", "mp", None),
        P("dp", None),
        P("section", None, None),
        P("section", None, None),
        P("section", None, None, "mp"),
        P("section", None, "mp"),
        P("section", "mp", None),
        P("section", None, "mp"),
        P("section", "mp"),
        P("section", "mp", None),
        P("section", None, None),
    )
    out_specs = (
        P("section", "dp", "mp", None),
        P("section", "dp", "mp", None),
        P("section", None, None),
        P("section", None, None),
        P("section", None, None, "mp"),
        P("section", None, "mp"),
        P("section", "mp", None),
        P("section", None, "mp"),
        P("section", "mp"),
        P("section", "mp", None),
        P("section", None, None),
    )
    return jax.shard_map(
        per_device, mesh=mesh, in_specs=in_specs, out_specs=out_specs, check_vma=False
    )
```

```python
from functools import partial

import jax
import jax.numpy as jnp
from jax import lax
from jax.experimental import pallas as pl
from jax.experimental.pallas import tpu as pltpu
from jax.sharding import PartitionSpec as P

HEAD = 64
branch_scale = 12.0 ** (-0.5)
norm_eps = 1e-05
masked_score = -1000000000.0
block = 256
cube = 0.044715
root = 0.7978845608

f32 = jnp.float32
bf16 = jnp.bfloat16


def mm(left, right):
    return jnp.dot(left, right, preferred_element_type=f32)


def mm_nt(left, right):
    return lax.dot_general(left, right, (((1,), (1,)), ((), ())), preferred_element_type=f32)


def mm_tn(left, right):
    return lax.dot_general(left, right, (((0,), (0,)), ((), ())), preferred_element_type=f32)


def normalize(values):
    mean = jnp.mean(values, axis=-1, keepdims=True)
    centred = values - mean
    spread = jnp.mean(centred * centred, axis=-1, keepdims=True)
    rstd = lax.rsqrt(spread + norm_eps)
    return centred * rstd, rstd


def norm_back(normal, rstd, grad, gain):
    scaled = grad * gain
    first = jnp.mean(scaled, axis=-1, keepdims=True)
    second = jnp.mean(scaled * normal, axis=-1, keepdims=True)
    return (scaled - first - normal * second) * rstd


def head_lanes(heads):
    found = []
    for head in range(heads):
        start = (head // 2) * 2 * HEAD
        width = min(2 * HEAD, heads * HEAD - start)
        found.append((start, width, head % 2))
    return found


def own_lanes(value, width, upper):
    if width == HEAD:
        return value
    lane = lax.broadcasted_iota(jnp.int32, value.shape, 1)
    keep = (lane >= HEAD) if upper else (lane < HEAD)
    return jnp.where(keep, value, jnp.zeros_like(value))


def block_mask(seg_col, seg_row, rows, count):
    same = seg_col[0:count, :] == seg_row[:, rows]
    key = lax.broadcasted_iota(jnp.int32, (count, rows.stop - rows.start), 0)
    query = lax.broadcasted_iota(jnp.int32, (count, rows.stop - rows.start), 1) + rows.start
    return same & (key <= query)


MESH = pl.DeviceIdType.MESH


def attend_block(qkv_ref, mask, rows, count, logsum_ref):
    heads = qkv_ref.shape[2] // HEAD
    mixed = []
    for head, (lane, lanes, upper) in enumerate(head_lanes(heads)):
        cols = slice(lane, lane + lanes)
        queries = own_lanes(qkv_ref[0, rows, cols], lanes, upper) * bf16(HEAD ** (-0.5))
        scores = mm_nt(qkv_ref[1, 0:count, cols], queries)
        scores = jnp.where(mask, scores, masked_score)
        top = jnp.max(scores, axis=0, keepdims=True)
        weights = jnp.exp(scores - top)
        total = jnp.sum(weights, axis=0, keepdims=True)
        result = mm_tn(qkv_ref[2, 0:count, cols], weights.astype(bf16)) / total
        logsum_ref[head : head + 1, rows] = top + jnp.log(total)
        mixed.append((lanes, result))
    found = []
    for pair in range(0, heads, 2):
        lanes, result = mixed[pair]
        if lanes > HEAD:
            result = jnp.concatenate([result[:HEAD], mixed[pair + 1][1][HEAD:]], axis=0)
        found.append((pair * HEAD, lanes, result.T.astype(bf16)))
    return found


class Places:
    def __init__(self, local, units, width):
        self.qkv = [slice(part * local, (part + 1) * local) for part in range(3)]
        self.out = slice(3 * local, 4 * local)
        self.up = slice(4 * local, 4 * local + width)
        self.down = slice(4 * local + width, 4 * local + width + units)
        self.rows = 4 * local + width + units


class Places:
    def __init__(self, local, units, width):
        self.qkv = [slice(part * local, (part + 1) * local) for part in range(3)]
        self.out = slice(3 * local, 4 * local)
        self.up = slice(4 * local, 4 * local + width)
        self.down = slice(4 * local + width, 4 * local + width + units)
        self.rows = 4 * local + width + units


class Mail:
    def __init__(self, sems):
        self.sems, self.names = sems, {}

    def number(self, name):
        return self.names.setdefault(name, len(self.names))

    def copy(self, name, src, dst, device, sent=None):
        return pltpu.make_async_remote_copy(
            src_ref=src,
            dst_ref=dst,
            send_sem=self.sems.at[0, self.number(sent or name)],
            recv_sem=self.sems.at[1, self.number(name)],
            device_id=device,
            device_id_type=MESH,
        )


class Moves:
    def __init__(self, sems):
        self.sems, self.names, self.open = sems, {}, []

    def copy(self, name, src, dst):
        return pltpu.make_async_copy(src, dst, self.sems.at[self.names.setdefault(name, len(self.names))])

    def start(self, name, src, dst):
        copy = self.copy(name, src, dst)
        copy.start()
        self.open.append(copy)

    def finish(self):
        for copy in self.open:
            copy.wait()


def others(dp, copies):
    return [dp + 1 - 2 * lax.rem(dp, 2), dp + 2 - 4 * lax.rem(dp // 2, 2)]


class Here:
    def __init__(self):
        self.core, self.z, self.dp = (lax.axis_index(name) for name in ("section", "mp", "dp"))
        self.mine, self.side = self.z // 2, lax.rem(self.z, 2)
        self.next_z = self.z + 1 - 2 * self.side
        self.far_z = self.z + 2 - 4 * self.mine
        self.sibling = (1 - self.core, self.z, self.dp)
        self.partner = (self.core, self.next_z, self.dp)
        near = others(self.dp, 4)
        self.copies = near + [near[0] + near[1] - self.dp]
        self.peers = [(self.core, self.z, dp) for dp in self.copies]


def meet(devices):
    barrier = pltpu.get_barrier_semaphore()
    for device in devices:
        pl.semaphore_signal(barrier, inc=1, device_id=device, device_id_type=MESH)
    pl.semaphore_wait(barrier, len(devices))


def fill_segments(lengths_ref, row, seg_col, seg_row):
    docs = lengths_ref.shape[1]
    for ref, axis in ((seg_col, 0), (seg_row, 1)):
        positions = lax.broadcasted_iota(jnp.int32, ref.shape, axis)
        segs = jnp.zeros(ref.shape, jnp.int32)
        end = 0
        for doc in range(docs):
            end = end + lengths_ref[row, doc]
            segs = segs + (positions >= end).astype(jnp.int32)
        ref[...] = jnp.where(segs < docs, segs, docs + positions)


class RowsIn:
    def __init__(self, name, src, dst, here, mail, moves):
        self.name, self.src, self.dst, self.here, self.mail, self.moves = name, src, dst, here, mail, moves
        self.quarter = src.shape[1]

    def place(self, side):
        return self.dst.at[pl.ds(pl.multiple_of(side * self.quarter, self.quarter), self.quarter)]

    def near(self, src):
        return self.mail.copy((self.name, "near"), src, self.place(self.here.side), self.here.partner)

    def far(self):
        here = self.here
        return self.mail.copy(
            (self.name, "far"), self.src.at[1 - here.mine], self.place(here.side), (here.core, here.far_z, here.dp)
        )

    def own(self):
        return self.moves.copy((self.name, "own"), self.src.at[self.here.mine], self.place(self.here.side))

    def start(self):
        @pl.when(self.here.core == self.here.mine)
        def _():
            self.far().start()
            self.near(self.src.at[self.here.mine]).start()
            self.own().start()

    def forward(self):
        @pl.when(self.here.core != self.here.mine)
        def _():
            self.far().wait_recv()
            self.near(self.place(self.here.side)).start()

    def ready(self):
        self.mail.copy(
            (self.name, "near"), self.src.at[0], self.place(1 - self.here.side), self.here.partner
        ).wait_recv()

        @pl.when(self.here.core == self.here.mine)
        def _():
            self.own().wait()

    def finish(self):
        self.near(self.place(self.here.side)).wait_send()

        @pl.when(self.here.core == self.here.mine)
        def _():
            self.far().wait_send()


class ShardsIn:
    def __init__(self, layer, src, dst, here, mail, moves, pieces):
        self.layer, self.src, self.dst, self.here, self.mail, self.moves = layer, src, dst, here, mail, moves
        self.pieces = pieces

    def whole(self, piece):
        start, count, _ = self.pieces[piece]
        return slice(start, start + count)

    def given(self, piece):
        start, count, before = self.pieces[piece]
        return self.src[piece].at[slice(start - before, start - before + count)]

    def eighth(self, piece, dp, core, given=False):
        start, count, before = self.pieces[piece]
        part = count // 8
        start -= before if given else 0
        return pl.ds(pl.multiple_of(start + (lax.rem(dp, 4) * 2 + core) * part, 16), part)

    def own(self, piece):
        rows = self.whole(piece)
        return self.moves.copy((self.layer, "own", piece), self.given(piece), self.dst.at[0, rows])

    def twin(self, piece):
        rows = self.whole(piece)
        return self.mail.copy((self.layer, "twin", piece), self.given(piece), self.dst.at[0, rows], self.here.sibling)

    def far(self, piece, core):
        here = self.here
        rows = self.eighth(piece, here.dp, core)
        return self.mail.copy(
            (self.layer, "far", piece),
            self.src[piece].at[self.eighth(piece, here.dp, core, given=True)],
            self.dst.at[1, rows],
            (core, here.far_z, here.dp),
            sent=(self.layer, "far", piece, core),
        )

    def spread(self, piece, n):
        rows = self.eighth(piece, self.here.dp, self.here.core)
        return self.mail.copy(
            (self.layer, "spread", piece, n), self.dst.at[1, rows], self.dst.at[1, rows], self.here.peers[n]
        )

    def across(self, piece, n):
        dp = self.here.dp if n == 3 else self.here.copies[n]
        rows = self.eighth(piece, dp, self.here.core)
        return self.mail.copy(
            (self.layer, "across", piece, n), self.dst.at[1, rows], self.dst.at[1, rows], self.here.sibling
        )

    def start(self, piece):
        @pl.when(self.here.core == self.layer)
        def _():
            for core in range(2):
                self.far(piece, core).start()
            self.own(piece).start()
            self.twin(piece).start()

    def relay(self, piece):
        self.far(piece, 0).wait_recv()
        for n in range(3):
            self.spread(piece, n).start()
        self.across(piece, 3).start()

    def share(self, piece):
        for n in range(3):
            self.spread(piece, n).wait_recv()
            self.across(piece, n).start()

    def ready(self, piece):
        for n in range(4):
            self.across(piece, n).wait_recv()

        @pl.when(self.here.core == self.layer)
        def _():
            self.own(piece).wait()

        @pl.when(self.here.core != self.layer)
        def _():
            self.twin(piece).wait_recv()

    def finish(self, piece):
        for n in range(3):
            self.spread(piece, n).wait_send()
        for n in range(4):
            self.across(piece, n).wait_send()

        @pl.when(self.here.core == self.layer)
        def _():
            for core in range(2):
                self.far(piece, core).wait_send()
            self.twin(piece).wait_send()


class Vectors:
    def __init__(self, src, dst, here, mail):
        self.src, self.dst, self.here, self.mail = src, dst, here, mail

    def copies(self):
        here, mail = self.here, self.mail
        own, far = self.dst.at[here.core, 0], self.dst.at[here.core, 1]
        return [
            mail.copy("vec twin", self.src, own, here.sibling),
            mail.copy("vec far", self.src, far, (here.core, here.far_z, here.dp)),
            mail.copy("vec cross", self.src, far, (1 - here.core, here.far_z, here.dp)),
        ]

    def start(self):
        for copy in self.copies():
            copy.start()
        self.dst[self.here.core, 0] = self.src[...]

    def ready(self):
        for copy in self.copies():
            copy.wait()


KEPT = ("normed", "qkv", "logsum", "att", "middle", "upper", "hidden", "slope")
row_gain, row_shift, row_branch, row_up, row_query, row_value = 0, 2, 4, 6, 7, 8


def forward_kernel(
    where,
    pieces,
    inputs_ref,
    cotangent_ref,
    top_ref,
    up_ref,
    down_ref,
    gains_ref,
    shifts_ref,
    branch_ref,
    up_bias_ref,
    in_bias_ref,
    lengths_ref,
    *refs,
):
    names = ("weights", "vec", "grad", "states", "tail") + KEPT
    count = len(names)
    out = dict(zip(names, refs[:count]))
    kept = dict(zip(("weights", "grad", "states", "tail") + KEPT, refs[count : 2 * count - 1]))
    vec = out["vec"]
    seg_col, seg_row, pack_ref, qkv_out, att_out, low, got, mail_sems, move_sems = refs[2 * count - 1 :]
    here = Here()
    core = here.core
    mail, moves = Mail(mail_sems), Moves(move_sems)
    states = kept["states"]
    half = states.shape[1]
    local = where.qkv[0].stop
    blocks = half // block
    first = pl.multiple_of(core * half, half)
    rows_in = RowsIn("state", inputs_ref, states.at[0], here, mail, moves)
    grad_in = RowsIn("grad", cotangent_ref, kept["grad"], here, mail, moves)
    sources = (top_ref, top_ref, up_ref, down_ref)
    shards = [ShardsIn(n, sources, kept["weights"].at[n], here, mail, moves, pieces) for n in range(2)]
    vectors = Vectors(pack_ref, vec, here, mail)
    pack_ref[...] = jnp.zeros_like(pack_ref)
    pack_ref[row_gain : row_gain + 2, :] = gains_ref[...]
    pack_ref[row_shift : row_shift + 2, :] = shifts_ref[...]
    pack_ref[row_branch : row_branch + 2, :] = branch_ref[...]
    pack_ref[row_up : row_up + 1, :] = up_bias_ref[...]
    pack_ref[row_query : row_query + 1, 0:local] = in_bias_ref[0:1, :]
    pack_ref[row_value : row_value + 1, 0:local] = in_bias_ref[1:2, :]

    meet(
        [here.sibling, here.partner]
        + here.peers
        + [(here.core, here.far_z, here.dp), (1 - here.core, here.far_z, here.dp)]
    )
    rows_in.start()
    shards[0].start(0)
    vectors.start()
    shards[0].start(1)
    fill_segments(lengths_ref, here.mine, seg_col, seg_row)
    rows_in.forward()
    shards[0].relay(0)
    shards[0].start(2)
    shards[0].relay(1)
    shards[0].start(3)
    shards[0].share(0)
    vectors.ready()
    shards[0].share(1)

    later = []

    def tick():
        if later:
            later.pop(0)[1]()

    def upto(wanted):
        while any(label == wanted for label, _ in later):
            tick()

    def plan(label, *tasks):
        later.append((label, lambda: [task() for task in tasks]))

    plan("")
    plan("")
    plan("", partial(shards[0].relay, 2), partial(shards[1].start, 0))
    plan("", partial(shards[0].relay, 3))
    plan("", partial(shards[0].share, 2), partial(shards[1].start, 1))
    plan("units 0", partial(shards[0].share, 3))
    plan("", partial(shards[1].relay, 0), partial(shards[1].start, 2))
    plan("", partial(shards[1].relay, 1), partial(shards[1].start, 3))
    plan("heads 1", partial(shards[1].share, 0), partial(shards[1].share, 1))
    plan("", partial(shards[1].relay, 2))
    plan("", partial(shards[1].share, 2), grad_in.start)
    plan("", partial(shards[1].relay, 3))
    plan("", grad_in.forward)
    plan("units 1", partial(shards[1].share, 3))

    def layer_forward(layer):
        w_ref = kept["weights"].at[layer]
        v_ref = vec.at[layer]
        state_ref = states.at[layer]
        normed_ref, qkv_ref, logsum_ref, att_ref, middle_ref, upper_ref, hidden_ref, slope_ref = (
            kept[name].at[layer] for name in KEPT
        )

        def row(number, slot=0):
            return v_ref[slot, number : number + 1, :]

        def bias(slot, part):
            if part == 1:
                return 0.0
            number = row_query if part == 0 else row_value
            return v_ref[slot, number : number + 1, 0:local]

        def low_copy(index, rows):
            return mail.copy(
                ("low", layer, index, rows.start),
                low.at[layer, index, rows],
                got.at[layer, index, rows],
                here.partner,
            )

        def send_low(index, rows, value):
            low[layer, index, rows, :] = value.astype(bf16)
            low_copy(index, rows).start()

        def received(index, rows):
            low_copy(index, rows).wait()
            return low[layer, index, rows, :].astype(f32) + got[layer, index, rows, :].astype(f32)

        def save(name):
            moves.start((name, layer), kept[name].at[layer], out[name].at[layer])

        def qkv_copy(j):
            there = pl.ds(pl.multiple_of(first + j * block, block), block)
            return mail.copy(("qkv", layer, j), qkv_out.at[layer, j], qkv_ref.at[:, there, :], here.sibling)

        def project(j):
            rows = slice(j * block, (j + 1) * block)
            normal, _ = normalize(state_ref[rows, :].astype(f32))
            normed = (normal * row(row_gain) + row(row_shift)).astype(bf16)
            normed_ref[rows, :] = normed
            for part in range(3):
                weight = w_ref[1 - core, where.qkv[part], :]
                qkv_out[layer, j, part] = (mm_nt(normed, weight) + bias(1 - core, part)).astype(bf16)
            qkv_copy(j).start()
            there = pl.ds(pl.multiple_of(first + j * block, block), block)
            for part in range(3):
                weight = w_ref[core, where.qkv[part], :]
                qkv_ref[part, there, :] = (mm_nt(normed, weight) + bias(core, part)).astype(bf16)

        def att_copy(j):
            own = slice(j * block, (j + 1) * block)
            return mail.copy(("att", layer, j), att_out.at[layer, j], att_ref.at[core, own], here.sibling)

        upto(f"heads {layer}")
        if layer == 0:
            rows_in.ready()
        shards[layer].ready(0)
        shards[layer].ready(1)
        for i in range(2 * blocks):
            owner, j = i // blocks, i % blocks
            rows = slice(i * block, (i + 1) * block)
            own = slice(j * block, (j + 1) * block)
            count = (i + 1) * block
            if layer == 0:
                if i < blocks:
                    project(i)
                    tick()
            else:

                @pl.when(core == owner)
                def _():
                    result = before["middle"](own) + branch_scale * (
                        before["received"](1, own) + before["row"](row_branch + 1)
                    )
                    state_ref[own, :] = result.astype(bf16)
                    project(j)

            @pl.when(core != owner)
            def _():
                qkv_copy(j).wait_recv()

            mask = block_mask(seg_col, seg_row, rows, count)
            found = attend_block(qkv_ref, mask, rows, count, logsum_ref)

            @pl.when(core == owner)
            def _():
                for lane, lanes, result in found:
                    att_ref[core, own, lane : lane + lanes] = result
                att_copy(j).wait_recv()
                send_low(0, own, sum(mm(att_ref[k, own, :], w_ref[k, where.out, :]) for k in range(2)))

            @pl.when(core != owner)
            def _():
                for lane, lanes, result in found:
                    att_out[layer, j, :, lane : lane + lanes] = result
                att_copy(j).start()

            tick()
        for j in range(blocks):
            qkv_copy(j).wait_send()
            att_copy(j).wait_send()
        save("normed")
        save("qkv")
        save("att")
        save("logsum")

        for j in range(blocks):
            rows = slice(j * block, (j + 1) * block)
            middle = state_ref[rows, :].astype(f32) + branch_scale * (received(0, rows) + row(row_branch))
            middle_ref[rows, :] = middle
            normal, _ = normalize(middle)
            upper = (normal * row(row_gain + 1) + row(row_shift + 1)).astype(bf16)
            upper_ref[rows, :] = upper
            if j == 0:
                upto(f"units {layer}")
                shards[layer].ready(2)
                shards[layer].ready(3)
            total = None
            for k in range(2):
                pre = mm(upper, w_ref[k, where.up, :]) + row(row_up, k)
                square = pre * pre
                curve = jnp.tanh(root * pre * (1.0 + cube * square))
                rise = 0.5 * (1.0 + curve)
                hidden = (pre * rise).astype(bf16)
                hidden_ref[k, rows, :] = hidden
                slope = rise + pre * (rise * (1.0 - curve)) * (root * (1.0 + 3.0 * cube * square))
                slope_ref[k, rows, :] = slope.astype(bf16)
                term = mm(hidden, w_ref[k, where.down, :])
                total = term if total is None else total + term
            if layer == 0:
                send_low(1, rows, total)
            else:
                kept["tail"][rows, :] = total.astype(bf16)
            tick()
        for name in ("middle", "upper", "hidden", "slope"):
            save(name)
        moves.start(("weights", layer), w_ref, out["weights"].at[layer])
        if layer == 1:
            moves.start("tail", kept["tail"], out["tail"])
            return
        before.update(middle=lambda rows: middle_ref[rows, :], received=received, row=row)

    before = {}
    for layer in range(2):
        layer_forward(layer)
    while later:
        tick()
    moves.start("states", states, out["states"])
    grad_in.ready()
    moves.start("grad", kept["grad"], out["grad"])
    rows_in.finish()
    grad_in.finish()
    for shard in shards:
        for piece in range(len(pieces)):
            shard.finish(piece)
    moves.finish()


def forward_pass(where, inputs, cotangent, shard, vectors, lengths):
    quarter, width = inputs.shape[1:]
    half, length = 2 * quarter, 4 * quarter
    local = where.qkv[0].stop
    units = where.down.stop - where.down.start
    blocks = half // block
    top = 4 * local
    pieces = [(0, top // 2, 0), (top // 2, top // 2, 0), (top, width, top), (top + width, units, top + width)]
    vmem = pl.BlockSpec(memory_space=pltpu.VMEM)
    hbm = pl.BlockSpec(memory_space=pl.ANY)
    shapes = {
        "weights": ((2, 2, where.rows, width), bf16),
        "vec": ((2, 2, 16, width), f32),
        "grad": ((half, width), bf16),
        "states": ((2, half, width), bf16),
        "tail": ((half, width), bf16),
        "normed": ((2, half, width), bf16),
        "qkv": ((2, 3, length, local), bf16),
        "logsum": ((2, local // HEAD, length), f32),
        "att": ((2, 2, half, local), bf16),
        "middle": ((2, half, width), f32),
        "upper": ((2, half, width), bf16),
        "hidden": ((2, 2, half, units), bf16),
        "slope": ((2, 2, half, units), bf16),
    }
    found = pl.pallas_call(
        partial(forward_kernel, where, pieces),
        out_shape=[jax.ShapeDtypeStruct(*entry) for entry in shapes.values()],
        in_specs=[hbm] * 5 + [vmem] * 5 + [pl.BlockSpec(memory_space=pltpu.SMEM)],
        out_specs=[vmem if name == "vec" else hbm for name in shapes],
        scratch_shapes=[pltpu.VMEM(*entry) for name, entry in shapes.items() if name != "vec"]
        + [
            pltpu.VMEM((length, 1), jnp.int32),
            pltpu.VMEM((1, length), jnp.int32),
            pltpu.VMEM((16, width), f32),
            pltpu.VMEM((2, blocks, 3, block, local), bf16),
            pltpu.VMEM((2, blocks, block, local), bf16),
            pltpu.VMEM((2, 2, half, width), bf16),
            pltpu.VMEM((2, 2, half, width), bf16),
            pltpu.SemaphoreType.DMA((2, 128)),
            pltpu.SemaphoreType.DMA((64,)),
        ],
        compiler_params=pltpu.CompilerParams(
            vmem_limit_bytes=58 * 2**20, collective_id=1, has_side_effects=True
        ),
        name="forward_pass",
    )(inputs, cotangent, *shard, *vectors, lengths)
    return dict(zip(shapes, found))


def attend_back_block(qkv_ref, grad_ref, mask, rows, count, logsum_ref, dqkv_ref, dk_sum, dv_sum):
    heads = qkv_ref.shape[2] // HEAD
    scale = bf16(HEAD ** (-0.5))
    mixed = []
    for head, (lane, lanes, upper) in enumerate(head_lanes(heads)):
        cols = slice(lane, lane + lanes)
        queries = own_lanes(qkv_ref[0, rows, cols], lanes, upper) * scale
        grads = own_lanes(grad_ref[rows, cols], lanes, upper)
        keys = qkv_ref[1, 0:count, cols]
        scores = mm_nt(keys, queries)
        scores = jnp.where(mask, scores, masked_score)
        probs = jnp.exp(scores - logsum_ref[head : head + 1, rows])
        grad_probs = mm_nt(qkv_ref[2, 0:count, cols], grads)
        dv_sum[0:count, cols] += mm(probs.astype(bf16), grads)
        term = probs * grad_probs
        delta = jnp.sum(term, axis=0, keepdims=True)
        grad_scores = (term - probs * delta).astype(bf16)
        dk_sum[0:count, cols] += mm(grad_scores, queries)
        mixed.append((lanes, mm_tn(keys, grad_scores)))
    for pair in range(0, heads, 2):
        lane = pair * HEAD
        lanes, result = mixed[pair]
        if lanes > HEAD:
            result = jnp.concatenate([result[:HEAD], mixed[pair + 1][1][HEAD:]], axis=0)
        dqkv_ref[0, rows, lane : lane + lanes] = (result.T * HEAD ** (-0.5)).astype(bf16)


class RowsOut:
    def __init__(self, name, layer, src, dst, here, mail, moves):
        self.name, self.layer, self.src, self.dst = name, layer, src, dst
        self.here, self.mail, self.moves = here, mail, moves

    def ends(self):
        quarter = self.dst.shape[1]
        rows = pl.ds(pl.multiple_of(self.here.side * quarter, quarter), quarter)
        src = self.src if self.src.shape[0] == quarter else self.src.at[rows]
        return src, self.dst.at[self.here.mine]

    def home(self):
        return self.mail.copy((self.name, self.layer, "home"), *self.ends(), self.here.sibling)

    def away(self):
        device = (self.layer, self.here.far_z, self.here.dp)
        return self.mail.copy((self.name, self.layer, "away"), *self.ends(), device)

    def local(self):
        return self.moves.copy((self.name, self.layer), *self.ends())

    def cases(self, away, home, local):
        core, mine = self.here.core, self.here.mine
        pl.when(core != mine)(away)
        pl.when((core == mine) & (core != self.layer))(home)
        pl.when((core == mine) & (core == self.layer))(local)

    def start(self):
        self.cases(
            lambda: self.away().start(), lambda: self.home().start(), lambda: self.local().start()
        )

    def finish(self):
        self.cases(
            lambda: self.away().wait_send(), lambda: self.home().wait_send(), lambda: self.local().wait()
        )

        @pl.when(self.here.core == self.layer)
        def _():
            self.away().wait_recv()

            @pl.when(self.here.core != self.here.mine)
            def _():
                self.home().wait_recv()


def more_bits(copies):
    return [1 << n for n in range(2, copies.bit_length()) if (1 << n) < copies]


def flipped(dp, bit):
    return dp + bit - 2 * bit * lax.rem(dp // bit, 2)


class GradSum:
    def __init__(self, layer, part, buffers, final, here, mail, moves, pieces, place, copies):
        self.layer, self.part, self.final, self.pieces = layer, part, final, pieces
        self.place = place
        self.twin, self.first, self.second, self.cross, self.groups = buffers
        self.here, self.mail, self.moves = here, mail, moves
        self.bits_above = more_bits(copies)
        self.slot = lax.rem(here.core + layer, 2)
        self.bits = [lax.rem(here.dp, 2), lax.rem(here.dp // 2, 2)]
        self.stages = 6 + len(self.bits_above)

    @staticmethod
    def scratch(rows, places, width, copies):
        above = len(more_bits(copies))
        return [
            pltpu.VMEM((places, rows, width), bf16),
            pltpu.VMEM((places, 2, rows // 4, width), bf16),
            pltpu.VMEM((places, 2, rows // 8, width), bf16),
            pltpu.VMEM((2 * places, 2, rows // 8, width), bf16),
            pltpu.VMEM((max(1, above), 2 * places if above else 1, 2, rows // 8, width), bf16),
        ]

    def name(self, piece, kind, half=0):
        return ("sum", self.layer, self.pieces[piece], kind, half)

    def span(self, piece, start, count):
        return pl.ds(pl.multiple_of(self.pieces[piece][0] + start, 16), count)

    def chunk(self, piece, half, outer, inner):
        eighth = self.pieces[piece][1] // 8
        return half * 4 * eighth + outer * 2 * eighth + inner * eighth

    def device(self, axis):
        return self.here.peers[axis]

    def ring(self, piece):
        return self.place[piece] % self.twin.shape[0]

    def twin_copy(self, piece):
        start, count = self.pieces[piece]
        return self.mail.copy(
            self.name(piece, "twin"),
            self.part.at[1 - self.slot, slice(start, start + count)],
            self.twin.at[self.ring(piece)],
            self.here.sibling,
        )

    def first_copy(self, piece, half):
        src = self.span(piece, self.chunk(piece, half, 1 - self.bits[half], 0), self.pieces[piece][1] // 4)
        dst = self.first.at[self.ring(piece), half]
        return self.mail.copy(self.name(piece, "first", half), self.part.at[self.slot, src], dst, self.device(half))

    def second_copy(self, piece, half):
        axis = 1 - half
        src = self.span(
            piece, self.chunk(piece, half, self.bits[half], 1 - self.bits[axis]), self.pieces[piece][1] // 8
        )
        dst = self.second.at[self.ring(piece), half]
        return self.mail.copy(self.name(piece, "second", half), self.part.at[self.slot, src], dst, self.device(axis))

    def own(self, piece, half):
        return self.span(
            piece, self.chunk(piece, half, self.bits[half], self.bits[1 - half]), self.pieces[piece][1] // 8
        )

    def result(self, piece, half):
        ref, before = self.final[piece]
        start = self.pieces[piece][0] - before
        offset = self.chunk(piece, half, self.bits[half], self.bits[1 - half])
        return ref.at[pl.ds(pl.multiple_of(start + offset, 16), self.pieces[piece][1] // 8)]

    def cross_copy(self, piece, half):
        return self.mail.copy(
            self.name(piece, "cross", half),
            self.part.at[self.slot, self.own(piece, half)],
            self.cross.at[self.place[piece], half],
            (1 - self.here.core, self.here.far_z, self.here.dp),
        )

    def group_copy(self, step, piece, half):
        here = self.here
        return self.mail.copy(
            self.name(piece, ("group", step), half),
            self.part.at[self.slot, self.own(piece, half)],
            self.groups.at[step, self.place[piece], half],
            (here.core, here.z, flipped(here.dp, self.bits_above[step])),
        )

    def gather_copies(self, piece, half):
        rows = self.own(piece, half)
        return [
            self.mail.copy(
                self.name(piece, ("gather", n), half),
                self.part.at[self.slot, rows],
                self.result(piece, half),
                self.here.peers[n],
            )
            for n in range(3)
        ]

    def keep_copy(self, piece, half):
        rows = self.own(piece, half)
        return self.moves.copy(self.name(piece, "keep", half), self.part.at[self.slot, rows], self.result(piece, half))

    def stage(self, number, piece):
        if number < 4:
            (self.stage0, self.stage1, self.stage2, self.stage3)[number](piece)
        elif number < self.stages - 1:
            self.stage4(number - 4, piece)
        else:
            self.stage5(piece)

    def add(self, rows, other):
        self.part[self.slot, rows, :] += other

    def stage0(self, piece):
        self.twin_copy(piece).start()

    def stage1(self, piece):
        self.twin_copy(piece).wait_recv()
        start, count = self.pieces[piece]
        self.add(slice(start, start + count), self.twin[self.ring(piece)])
        for half in range(2):
            self.first_copy(piece, half).start()

    def stage2(self, piece):
        count = self.pieces[piece][1] // 4
        for half in range(2):
            self.first_copy(piece, half).wait()
            rows = self.span(piece, self.chunk(piece, half, self.bits[half], 0), count)
            self.add(rows, self.first[self.ring(piece), half])
            self.second_copy(piece, half).start()

    def stage3(self, piece):
        for half in range(2):
            self.second_copy(piece, half).wait()
            self.add(self.own(piece, half), self.second[self.ring(piece), half])

            @pl.when(self.here.core != self.layer)
            def _():
                self.cross_copy(piece, half).start()

    def stage4(self, step, piece):
        @pl.when(self.here.core == self.layer)
        def _():
            for half in range(2):
                if step == 0:
                    self.cross_copy(piece, half).wait_recv()
                    self.add(self.own(piece, half), self.cross[self.place[piece], half])
                else:
                    self.group_copy(step - 1, piece, half).wait()
                    self.add(self.own(piece, half), self.groups[step - 1, self.place[piece], half])
                if step < len(self.bits_above):
                    self.group_copy(step, piece, half).start()
                else:
                    for copy in self.gather_copies(piece, half):
                        copy.start()
                    self.keep_copy(piece, half).start()

    def stage5(self, piece):
        self.twin_copy(piece).wait_send()

        @pl.when(self.here.core == self.layer)
        def _():
            for half in range(2):
                for copy in self.gather_copies(piece, half):
                    copy.wait()
                self.keep_copy(piece, half).wait()

        @pl.when(self.here.core != self.layer)
        def _():
            for half in range(2):
                self.cross_copy(piece, half).wait_send()


class VectorSum:
    def __init__(self, layer, part, got, out, here, mail, copies):
        self.layer, self.part, self.got, self.out, self.mail = layer, part, got, out, mail
        self.devices = [here.partner, here.sibling] + here.peers[:2]
        self.devices += [(here.core, here.z, flipped(here.dp, bit)) for bit in more_bits(copies)]
        self.devices.append((here.core, here.far_z, here.dp))
        self.stages = len(self.devices) + 1

    def copy(self, step):
        return self.mail.copy(("vec", self.layer, step), self.part, self.got.at[step], self.devices[step])

    def stage(self, number, _):
        if number > 0:
            step = number - 1
            self.copy(step).wait()
            if number == 1:
                self.part[12:14, :] += self.got[step, 12:14, :]
            elif number < self.stages - 1:
                self.part[...] += self.got[step]
            else:
                self.out[...] = self.part[...] + self.got[step]
                self.out[8:10, :] = self.part[8:10, :] + self.got[step, 10:12, :]
        if number < self.stages - 1:
            self.copy(number).start()


class Pipeline:
    def __init__(self, gap):
        self.gap, self.now = gap, 0
        self.waiting, self.running = [], []

    def wait(self, one, stage):
        return 1 if self.gap == 1 else 4 if one.layer else (2, 3, 3, 3, 3, 3)[min(stage, 5)]

    def add(self, one, piece=0):
        self.waiting.append((one, piece))

    def tick(self, fresh=1):
        self.now += 1
        for item in self.running:
            one, piece, stage, due = item
            if due <= self.now:
                one.stage(stage, piece)
                item[2:] = [stage + 1, self.now + self.wait(one, stage)]
        for one, piece in self.waiting[:fresh]:
            one.stage(0, piece)
            self.running.append([one, piece, 1, self.now + self.wait(one, 0)])
        self.waiting = self.waiting[fresh:]
        self.running = [item for item in self.running if item[2] < item[0].stages]

    def hurry(self, ticks=0):
        self.gap = 1
        for item in self.running:
            item[3] = self.now + 1
        for _ in range(ticks):
            self.tick(fresh=3)

    def drain(self):
        self.hurry()
        while self.waiting or self.running:
            self.now += 1000
            self.tick(fresh=2)


SAVED = ("state",) + KEPT


def backward_kernel(where, copies, *refs):
    refs = list(refs)

    def take(count):
        found = refs[:count]
        del refs[:count]
        return found

    (grad_hbm, w_hbm, vec_ref, lengths_ref, states_hbm, tail_hbm) = take(6)
    kept_hbm = dict(zip(KEPT, take(len(KEPT))))
    (states_out, grads_out, final_top, final_up, final_down, vec_out) = take(6)
    grads, w_ref = take(2)
    saved = dict(zip(SAVED, take(len(SAVED))))
    (
        d_refs,
        gz_ref,
        dmiddle_ref,
        datt_out,
        datt_ref,
        dqkv_ref,
        dk_sum,
        dv_sum,
        dmix_ref,
        low,
        got,
        tail_low,
        tail_got,
        seg_col,
        seg_row,
        d_vecs,
        got_vecs,
    ) = take(17)
    buffers = take(5)
    mail_sems, move_sems = take(2)
    start_ref, normed_ref, qkv_ref, logsum_ref, att_ref, middle_ref, upper_ref, hidden_ref, slope_ref = (
        saved[name] for name in SAVED
    )
    dpre_ref = slope_ref
    gy_ref = gz_ref

    here = Here()
    core = here.core
    mail, moves = Mail(mail_sems), Moves(move_sems)
    half = dmiddle_ref.shape[0]
    blocks = half // block
    first = pl.multiple_of(core * half, half)
    order = list(range(blocks))[::-1]
    heads = slice(0, where.out.start)

    def load_copy(layer, name):
        if isinstance(name, slice):
            return moves.copy((layer, name.start), w_hbm.at[layer, :, name], w_ref.at[:, name])
        src = states_hbm if name == "state" else kept_hbm[name]
        return moves.copy((layer, name), src.at[layer], saved[name])

    def load(layer, *names):
        for name in names:
            load_copy(layer, name).start()

    def need(layer, *names):
        for name in names:
            load_copy(layer, name).wait()

    groups = [
        (where.down, "slope", where.up, "hidden", "upper"),
        ("middle", where.out),
        ("qkv", "logsum", "att"),
        (heads, "normed", "state"),
    ]
    grad_load = moves.copy("grad", grad_hbm, grads.at[1])
    grad_load.start()
    for group in groups:
        load(1, *group)
    tail_load = moves.copy("tail", tail_hbm, tail_low)
    tail_load.start()
    top = where.out.stop
    pieces = [
        (rows.start + n * ((rows.stop - rows.start) // 2), (rows.stop - rows.start) // 2)
        for rows in (where.down, where.up, slice(0, top))
        for n in range(2)
    ]
    meet(
        [here.sibling, here.partner]
        + here.peers
        + [(core, here.far_z, here.dp), (1 - core, here.far_z, here.dp)]
        + [(core, here.z, flipped(here.dp, bit)) for bit in more_bits(copies)]
    )
    line = Pipeline(4)
    sums = [
        GradSum(
            layer,
            d_refs.at[layer],
            buffers,
            [(final_down, where.down.start)] * 2 + [(final_up, where.up.start)] * 2 + [(final_top, 0)] * 2,
            here,
            mail,
            moves,
            pieces,
            [(1 - layer) * len(pieces) + n for n in range(len(pieces))],
            copies,
        )
        for layer in range(2)
    ]
    vectors = [
        VectorSum(layer, d_vecs.at[layer], got_vecs.at[layer], vec_out.at[layer], here, mail, copies)
        for layer in range(2)
    ]
    fill_segments(lengths_ref, here.mine, seg_col, seg_row)
    d_vecs[...] = jnp.zeros_like(d_vecs)
    rows_out = [
        RowsOut("state", 0, states_hbm.at[1], states_out, here, mail, moves),
        RowsOut("state", 1, tail_got, states_out, here, mail, moves),
        RowsOut("grad", 1, grads.at[0], grads_out, here, mail, moves),
        RowsOut("grad", 0, grads.at[1], grads_out, here, mail, moves),
    ]

    def pair_copy(layer, index, rows):
        return mail.copy(
            ("low", layer, index, rows.start), low.at[index, rows], got.at[index, rows], here.partner
        )

    def send_low(layer, index, rows, value):
        low[index, rows, :] = value.astype(bf16)
        pair_copy(layer, index, rows).start()

    def received(layer, index, rows):
        pair_copy(layer, index, rows).wait()
        return low[index, rows, :].astype(f32) + got[index, rows, :].astype(f32)

    def own_rows(j):
        return slice(j * block, (j + 1) * block)

    def total(value):
        return jnp.sum(value, axis=0, keepdims=True)

    def vector(layer, number):
        return vec_ref[layer, 0, number : number + 1, :]

    def note(layer, number, value):
        d_vecs[layer, number : number + 1, :] += total(value)

    def units_back(layer, j):
        rows = own_rows(j)
        gz = branch_scale * grads[layer, rows, :].astype(f32)
        note(layer, 5, gz)
        gz = gz.astype(bf16)
        gz_ref[rows, :] = gz
        part = None
        for k in range(2):
            dpre = (mm_nt(gz, w_ref[k, where.down, :]) * slope_ref[k, rows, :].astype(f32)).astype(bf16)
            dpre_ref[k, rows, :] = dpre
            term = mm_nt(dpre, w_ref[k, where.up, :])
            part = term if part is None else part + term
        send_low(layer, 0, rows, part)

    def units_weights(layer):
        d_ref = d_refs.at[layer]
        need(layer, "hidden", "upper")
        for k in range(2):
            d_ref[k, where.down, :] = mm_tn(hidden_ref[k], gz_ref[...]).astype(bf16)
            line.tick()
        line.add(sums[layer], 0)
        line.add(sums[layer], 1)
        for k in range(2):
            d_ref[k, where.up, :] = mm_tn(upper_ref[...], dpre_ref[k]).astype(bf16)
            note(layer, 8 + 2 * k, dpre_ref[k].astype(f32))
            line.tick()
        line.add(sums[layer], 2)
        line.add(sums[layer], 3)
        line.tick()

    def datt_copy(layer, j):
        there = pl.ds(pl.multiple_of(first + j * block, block), block)
        return mail.copy(("datt", layer, j), datt_out.at[j], datt_ref.at[there, :], here.sibling)

    def middle_back(layer, j):
        rows = own_rows(j)
        d_upper = received(layer, 0, rows)
        normal, rstd = normalize(middle_ref[rows, :])
        note(layer, 1, d_upper * normal)
        note(layer, 3, d_upper)
        d_middle = grads[layer, rows, :].astype(f32) + norm_back(
            normal, rstd, d_upper, vector(layer, row_gain + 1)
        )
        dmiddle_ref[rows, :] = d_middle
        gy = branch_scale * d_middle
        note(layer, 4, gy)
        gy = gy.astype(bf16)
        gy_ref[rows, :] = gy
        datt_out[j] = mm_nt(gy, w_ref[1 - core, where.out, :]).astype(bf16)
        datt_copy(layer, j).start()
        there = pl.ds(pl.multiple_of(first + j * block, block), block)
        datt_ref[there, :] = mm_nt(gy, w_ref[core, where.out, :]).astype(bf16)

    def mix_copy(layer, j):
        return mail.copy(
            ("mix", layer, j),
            dqkv_ref.at[:, pl.ds(pl.multiple_of(half - first + j * block, block), block), :],
            dmix_ref.at[core, :, pl.ds(j * block, block), :],
            here.sibling,
        )

    def finish(layer, i):
        owner, j = i // blocks, i % blocks
        rows = slice(i * block, (i + 1) * block)
        dqkv_ref[1, rows, :] = dk_sum[rows, :].astype(bf16)
        dqkv_ref[2, rows, :] = dv_sum[rows, :].astype(bf16)

        @pl.when(core == owner)
        def _():
            dmix_ref[core, :, own_rows(j), :] = dqkv_ref[:, rows, :]

        @pl.when(core != owner)
        def _():
            mix_copy(layer, j).start()

    def attention_back(layer):
        dk_sum[...] = jnp.zeros_like(dk_sum)
        dv_sum[...] = jnp.zeros_like(dv_sum)
        need(layer, "qkv", "logsum", "att")
        left = list(range(2 * blocks))
        for j in order:
            datt_copy(layer, j).wait()
            for i in (blocks + j, j):
                rows = slice(i * block, (i + 1) * block)
                count = (i + 1) * block
                mask = block_mask(seg_col, seg_row, rows, count)
                attend_back_block(
                    qkv_ref, datt_ref, mask, rows, count, logsum_ref, dqkv_ref, dk_sum, dv_sum
                )
                left.remove(i)
                if j == 0:
                    for done in range(2 * blocks)[::-1]:
                        if done > max(left, default=-1) and done // blocks == i // blocks:
                            finish(layer, done)
                line.tick()

    def heads_part(rows):
        part = None
        for k in range(2):
            for p in range(3):
                term = mm(dmix_ref[k, p, rows, :], w_ref[k, where.qkv[p], :])
                part = term if part is None else part + term
        return part

    def heads_back(layer, j):
        rows = own_rows(j)
        mix_copy(layer, j).wait_recv()
        send_low(layer, 1, rows, heads_part(rows))
        line.tick()

    quarter = states_out.shape[1]

    def side_rows(side):
        return pl.ds(pl.multiple_of(side * quarter, quarter), quarter)

    def last_copy():
        rows = side_rows(1 - here.side)
        return mail.copy("last", low.at[1, rows], got.at[1, rows], here.partner)

    def last_heads_back():
        for j in order:
            mix_copy(0, j).wait_recv()
        for side in (1 - here.side, here.side):
            rows = side_rows(side)
            part = heads_part(rows)
            low[1, rows, :] = part.astype(bf16)
            if side is not here.side:
                last_copy().start()
            normal, _ = normalize(start_ref[rows, :].astype(f32))
            note(0, 12, part * normal)
            note(0, 13, part)
            line.tick()

    def last_state_back():
        rows = side_rows(here.side)
        last_copy().wait()
        d_normed = low[1, rows, :].astype(f32) + got[1, rows, :].astype(f32)
        normal, rstd = normalize(start_ref[rows, :].astype(f32))
        d_state = dmiddle_ref[rows, :] + norm_back(normal, rstd, d_normed, vector(0, row_gain))
        grads[1, rows, :] = d_state.astype(bf16)

    def heads_weights(layer):
        d_ref = d_refs.at[layer]
        for k in range(2):
            d_ref[k, where.out, :] = mm_tn(att_ref[k], gy_ref[...]).astype(bf16)
        line.tick()
        for k in range(2):
            for p in range(3):
                d_ref[k, where.qkv[p], :] = mm_tn(dmix_ref[k, p], normed_ref[...]).astype(bf16)
            for n, p in enumerate((0, 2)):
                local = dmix_ref.shape[3]
                lanes = slice(n * 2 * block, n * 2 * block + local)
                d_vecs[layer, 9 + 2 * k : 10 + 2 * k, lanes] = total(dmix_ref[k, p].astype(f32))
            if k == 0:
                line.tick()
        line.add(sums[layer], 4)
        line.add(sums[layer], 5)
        line.tick()

    def state_back(layer, j):
        rows = own_rows(j)
        d_normed = received(layer, 1, rows)
        normal, rstd = normalize(start_ref[rows, :].astype(f32))
        note(layer, 0, d_normed * normal)
        note(layer, 2, d_normed)
        d_state = dmiddle_ref[rows, :] + norm_back(normal, rstd, d_normed, vector(layer, row_gain))
        grads[1 - layer, rows, :] = d_state.astype(bf16)

    def tail_copy():
        return mail.copy("tail", tail_low.at[side_rows(1 - here.side)], tail_got, here.partner)

    grad_load.wait()
    need(1, where.down, "slope", where.up)
    for j in order:
        units_back(1, j)
    for layer in (1, 0):
        units_weights(layer)
        if layer == 1:
            load(0, *groups[0])
            rows_out[0].start()
        need(layer, "middle", where.out)
        for j in order:
            line.tick()
            middle_back(layer, j)
            line.tick()
        if layer == 1:
            tail_load.wait()
            tail_copy().start()
        attention_back(layer)
        need(layer, heads, "normed", "state")
        if layer == 1:
            for j in order:
                heads_back(layer, j)
            tail_copy().wait()
            rows = side_rows(here.side)
            branch = tail_low[rows, :].astype(f32) + tail_got[...].astype(f32) + vector(1, row_branch + 1)
            tail_got[...] = (middle_ref[rows, :] + branch_scale * branch).astype(bf16)
            rows_out[1].start()
            load(0, *groups[1])
        else:
            last_heads_back()
        heads_weights(layer)
        if layer == 1:
            load(0, *groups[2])
            need(0, where.down, "slope", where.up)
        if layer == 1:
            for j in order:
                line.tick()
                state_back(1, j)
                units_back(0, j)
                line.tick()
            load(0, *groups[3])
            rows_out[2].start()
            line.add(vectors[1])
        else:
            line.add(vectors[0])
            line.tick(fresh=3)
            line.hurry()
            last_state_back()
            rows_out[3].start()
        for j in order:
            mix_copy(layer, j).wait_send()
    line.drain()
    for one in rows_out:
        one.finish()


def backward_pass(where, copies, kept, lengths):
    grad = kept["grad"]
    half, width = grad.shape
    quarter, length = half // 2, 2 * half
    local = where.qkv[0].stop
    blocks = half // block
    shape = jax.ShapeDtypeStruct
    vmem = pl.BlockSpec(memory_space=pltpu.VMEM)
    hbm = pl.BlockSpec(memory_space=pl.ANY)
    smem = pl.BlockSpec(memory_space=pltpu.SMEM)
    operands = [grad, kept["weights"], kept["vec"], lengths, kept["states"], kept["tail"]]
    operands += [kept[name] for name in KEPT]
    above = len(more_bits(copies))
    scratch = [
        pltpu.VMEM((2, half, width), bf16),
        pltpu.VMEM((2, where.rows, width), bf16),
        pltpu.VMEM((half, width), bf16),
    ]
    scratch += [pltpu.VMEM(kept[name].shape[1:], kept[name].dtype) for name in KEPT]
    scratch += [
        pltpu.VMEM((2, 2, where.rows, width), bf16),
        pltpu.VMEM((half, width), bf16),
        pltpu.VMEM((half, width), f32),
        pltpu.VMEM((blocks, block, local), bf16),
        pltpu.VMEM((length, local), bf16),
        pltpu.VMEM((3, length, local), bf16),
        pltpu.VMEM((length, local), f32),
        pltpu.VMEM((length, local), f32),
        pltpu.VMEM((2, 3, half, local), bf16),
        pltpu.VMEM((2, half, width), bf16),
        pltpu.VMEM((2, half, width), bf16),
        pltpu.VMEM((half, width), bf16),
        pltpu.VMEM((quarter, width), bf16),
        pltpu.VMEM((length, 1), jnp.int32),
        pltpu.VMEM((1, length), jnp.int32),
        pltpu.VMEM((2, 16, width), f32),
        pltpu.VMEM((2, 5 + above, 16, width), f32),
    ]
    scratch += GradSum.scratch(where.out.stop // 2, 6, width, copies)
    scratch += [pltpu.SemaphoreType.DMA((2, 192 + 96 * above)), pltpu.SemaphoreType.DMA((64,))]
    return pl.pallas_call(
        partial(backward_kernel, where, copies),
        out_shape=[
            shape((2, quarter, width), bf16),
            shape((2, quarter, width), bf16),
            shape((where.out.stop, width), bf16),
            shape((where.up.stop - where.up.start, width), bf16),
            shape((where.down.stop - where.down.start, width), bf16),
            shape((2, 16, width), f32),
        ],
        in_specs=[hbm, hbm, vmem, smem, hbm, hbm] + [hbm] * len(KEPT),
        out_specs=[hbm] * 5 + [vmem],
        scratch_shapes=scratch,
        compiler_params=pltpu.CompilerParams(
            vmem_limit_bytes=61 * 2**20, collective_id=2, has_side_effects=True
        ),
        name="backward_pass",
    )(*operands)


def per_device(
    inputs,
    cotangent,
    lengths,
    norm_gains,
    norm_shifts,
    in_weight,
    in_bias,
    out_weight,
    up_weight,
    up_bias,
    down_weight,
    branch_bias,
):
    core = lax.axis_index("section")
    copies = lax.axis_size("dp")
    width = inputs.shape[2]
    local = in_weight.shape[3]
    units = up_weight.shape[2]

    def pick(flag, yes, no):
        return jnp.where(flag, yes, no)

    where = Places(local, units, width)
    top = jnp.concatenate([in_weight[0].transpose(1, 2, 0).reshape(3 * local, width), out_weight[0]])
    kept = forward_pass(
        where,
        inputs,
        cotangent,
        (top, up_weight[0], down_weight[0]),
        (norm_gains[0], norm_shifts[0], branch_bias[0], up_bias, in_bias[0]),
        lengths,
    )
    section_outputs, input_grads, final, g_up, g_down, vecs = backward_pass(where, copies, kept, lengths)
    vec = pick(core == 0, vecs[0], vecs[1])
    g_in = final[: 3 * local].astype(f32).reshape(3, local, width).transpose(2, 0, 1)
    g_out, g_up, g_down = (grad.astype(f32) for grad in (final[where.out], g_up, g_down))
    b_in = jnp.stack([vec[9, :local], vec[9, 2 * block : 2 * block + local]])

    return (
        section_outputs[None],
        input_grads.astype(f32)[None],
        (vec[0:2] + jnp.pad(vec[12:13], ((0, 1), (0, 0))))[None],
        (vec[2:4] + jnp.pad(vec[13:14], ((0, 1), (0, 0))))[None],
        g_in[None],
        b_in[None],
        g_out[None],
        g_up[None],
        vec[8][None],
        g_down[None],
        vec[4:6][None],
    )


def solution(mesh):
    in_specs = (
        P("dp", "mp", None),
        P("dp", "mp", None),
        P("dp", None),
        P("section", None, None),
        P("section", None, None),
        P("section", None, None, "mp"),
        P("section", None, "mp"),
        P("section", "mp", None),
        P("section", None, "mp"),
        P("section", "mp"),
        P("section", "mp", None),
        P("section", None, None),
    )
    out_specs = (
        P("section", "dp", "mp", None),
        P("section", "dp", "mp", None),
        P("section", None, None),
        P("section", None, None),
        P("section", None, None, "mp"),
        P("section", None, "mp"),
        P("section", "mp", None),
        P("section", None, "mp"),
        P("section", "mp"),
        P("section", "mp", None),
        P("section", None, None),
    )
    return jax.shard_map(
        per_device, mesh=mesh, in_specs=in_specs, out_specs=out_specs, check_vma=False
    )
```

```python
from functools import partial

import jax
import jax.numpy as jnp
from jax import lax
from jax.experimental import pallas as pl
from jax.experimental.pallas import tpu as pltpu
from jax.sharding import PartitionSpec as P

HEAD = 64
branch_scale = 12.0 ** (-0.5)
norm_eps = 1e-05
masked_score = -1000000000.0
block = 256
cube = 0.044715
root = 0.7978845608

f32 = jnp.float32
bf16 = jnp.bfloat16


def mm(left, right):
    return jnp.dot(left, right, preferred_element_type=f32)


def mm_nt(left, right):
    return lax.dot_general(left, right, (((1,), (1,)), ((), ())), preferred_element_type=f32)


def mm_tn(left, right):
    return lax.dot_general(left, right, (((0,), (0,)), ((), ())), preferred_element_type=f32)


def normalize(values):
    mean = jnp.mean(values, axis=-1, keepdims=True)
    centred = values - mean
    spread = jnp.mean(centred * centred, axis=-1, keepdims=True)
    rstd = lax.rsqrt(spread + norm_eps)
    return centred * rstd, rstd


def norm_back(normal, rstd, grad, gain):
    scaled = grad * gain
    first = jnp.mean(scaled, axis=-1, keepdims=True)
    second = jnp.mean(scaled * normal, axis=-1, keepdims=True)
    return (scaled - first - normal * second) * rstd


def head_lanes(heads):
    found = []
    for head in range(heads):
        start = (head // 2) * 2 * HEAD
        width = min(2 * HEAD, heads * HEAD - start)
        found.append((start, width, head % 2))
    return found


def own_lanes(value, width, upper):
    if width == HEAD:
        return value
    lane = lax.broadcasted_iota(jnp.int32, value.shape, 1)
    keep = (lane >= HEAD) if upper else (lane < HEAD)
    return jnp.where(keep, value, jnp.zeros_like(value))


def block_mask(seg_col, seg_row, rows, count):
    same = seg_col[0:count, :] == seg_row[:, rows]
    key = lax.broadcasted_iota(jnp.int32, (count, rows.stop - rows.start), 0)
    query = lax.broadcasted_iota(jnp.int32, (count, rows.stop - rows.start), 1) + rows.start
    return same & (key <= query)


MESH = pl.DeviceIdType.MESH


def attend_block(qkv_ref, mask, rows, count, logsum_ref):
    heads = qkv_ref.shape[2] // HEAD
    mixed = []
    for head, (lane, lanes, upper) in enumerate(head_lanes(heads)):
        cols = slice(lane, lane + lanes)
        queries = own_lanes(qkv_ref[0, rows, cols], lanes, upper) * bf16(HEAD ** (-0.5))
        scores = mm_nt(qkv_ref[1, 0:count, cols], queries)
        scores = jnp.where(mask, scores, masked_score)
        top = jnp.max(scores, axis=0, keepdims=True)
        weights = jnp.exp(scores - top)
        total = jnp.sum(weights, axis=0, keepdims=True)
        result = mm_tn(qkv_ref[2, 0:count, cols], weights.astype(bf16)) / total
        logsum_ref[head : head + 1, rows] = top + jnp.log(total)
        mixed.append((lanes, result))
    found = []
    for pair in range(0, heads, 2):
        lanes, result = mixed[pair]
        if lanes > HEAD:
            result = jnp.concatenate([result[:HEAD], mixed[pair + 1][1][HEAD:]], axis=0)
        found.append((pair * HEAD, lanes, result.T.astype(bf16)))
    return found


class Places:
    def __init__(self, local, units, width):
        self.qkv = [slice(part * local, (part + 1) * local) for part in range(3)]
        self.out = slice(3 * local, 4 * local)
        self.up = slice(4 * local, 4 * local + width)
        self.down = slice(4 * local + width, 4 * local + width + units)
        self.rows = 4 * local + width + units


class Places:
    def __init__(self, local, units, width):
        self.qkv = [slice(part * local, (part + 1) * local) for part in range(3)]
        self.out = slice(3 * local, 4 * local)
        self.up = slice(4 * local, 4 * local + width)
        self.down = slice(4 * local + width, 4 * local + width + units)
        self.rows = 4 * local + width + units


class Mail:
    def __init__(self, sems):
        self.sems, self.names = sems, {}

    def number(self, name):
        return self.names.setdefault(name, len(self.names))

    def copy(self, name, src, dst, device, sent=None):
        return pltpu.make_async_remote_copy(
            src_ref=src,
            dst_ref=dst,
            send_sem=self.sems.at[0, self.number(sent or name)],
            recv_sem=self.sems.at[1, self.number(name)],
            device_id=device,
            device_id_type=MESH,
        )


class Moves:
    def __init__(self, sems):
        self.sems, self.names, self.open = sems, {}, []

    def copy(self, name, src, dst):
        return pltpu.make_async_copy(src, dst, self.sems.at[self.names.setdefault(name, len(self.names))])

    def start(self, name, src, dst):
        copy = self.copy(name, src, dst)
        copy.start()
        self.open.append(copy)

    def finish(self):
        for copy in self.open:
            copy.wait()


def others(dp, copies):
    return [dp + 1 - 2 * lax.rem(dp, 2), dp + 2 - 4 * lax.rem(dp // 2, 2)]


class Here:
    def __init__(self):
        self.core, self.z, self.dp = (lax.axis_index(name) for name in ("section", "mp", "dp"))
        self.mine, self.side = self.z // 2, lax.rem(self.z, 2)
        self.next_z = self.z + 1 - 2 * self.side
        self.far_z = self.z + 2 - 4 * self.mine
        self.sibling = (1 - self.core, self.z, self.dp)
        self.partner = (self.core, self.next_z, self.dp)
        near = others(self.dp, 4)
        self.copies = near + [near[0] + near[1] - self.dp]
        self.peers = [(self.core, self.z, dp) for dp in self.copies]


def meet(devices):
    barrier = pltpu.get_barrier_semaphore()
    for device in devices:
        pl.semaphore_signal(barrier, inc=1, device_id=device, device_id_type=MESH)
    pl.semaphore_wait(barrier, len(devices))


def fill_segments(lengths_ref, row, seg_col, seg_row):
    docs = lengths_ref.shape[1]
    for ref, axis in ((seg_col, 0), (seg_row, 1)):
        positions = lax.broadcasted_iota(jnp.int32, ref.shape, axis)
        segs = jnp.zeros(ref.shape, jnp.int32)
        end = 0
        for doc in range(docs):
            end = end + lengths_ref[row, doc]
            segs = segs + (positions >= end).astype(jnp.int32)
        ref[...] = jnp.where(segs < docs, segs, docs + positions)


class RowsIn:
    def __init__(self, name, src, dst, here, mail, moves):
        self.name, self.src, self.dst, self.here, self.mail, self.moves = name, src, dst, here, mail, moves
        self.quarter = src.shape[1]

    def place(self, side):
        return self.dst.at[pl.ds(pl.multiple_of(side * self.quarter, self.quarter), self.quarter)]

    def near(self, src):
        return self.mail.copy((self.name, "near"), src, self.place(self.here.side), self.here.partner)

    def far(self):
        here = self.here
        return self.mail.copy(
            (self.name, "far"), self.src.at[1 - here.mine], self.place(here.side), (here.core, here.far_z, here.dp)
        )

    def own(self):
        return self.moves.copy((self.name, "own"), self.src.at[self.here.mine], self.place(self.here.side))

    def start(self):
        @pl.when(self.here.core == self.here.mine)
        def _():
            self.far().start()
            self.near(self.src.at[self.here.mine]).start()
            self.own().start()

    def forward(self):
        @pl.when(self.here.core != self.here.mine)
        def _():
            self.far().wait_recv()
            self.near(self.place(self.here.side)).start()

    def ready(self):
        self.mail.copy(
            (self.name, "near"), self.src.at[0], self.place(1 - self.here.side), self.here.partner
        ).wait_recv()

        @pl.when(self.here.core == self.here.mine)
        def _():
            self.own().wait()

    def finish(self):
        self.near(self.place(self.here.side)).wait_send()

        @pl.when(self.here.core == self.here.mine)
        def _():
            self.far().wait_send()


class ShardsIn:
    def __init__(self, layer, src, dst, here, mail, moves, pieces):
        self.layer, self.src, self.dst, self.here, self.mail, self.moves = layer, src, dst, here, mail, moves
        self.pieces = pieces

    def whole(self, piece):
        start, count, _ = self.pieces[piece]
        return slice(start, start + count)

    def given(self, piece):
        start, count, before = self.pieces[piece]
        return self.src[piece].at[slice(start - before, start - before + count)]

    def eighth(self, piece, dp, core, given=False):
        start, count, before = self.pieces[piece]
        part = count // 8
        start -= before if given else 0
        return pl.ds(pl.multiple_of(start + (lax.rem(dp, 4) * 2 + core) * part, 16), part)

    def own(self, piece):
        rows = self.whole(piece)
        return self.moves.copy((self.layer, "own", piece), self.given(piece), self.dst.at[0, rows])

    def twin(self, piece):
        rows = self.whole(piece)
        return self.mail.copy((self.layer, "twin", piece), self.given(piece), self.dst.at[0, rows], self.here.sibling)

    def far(self, piece, core):
        here = self.here
        rows = self.eighth(piece, here.dp, core)
        return self.mail.copy(
            (self.layer, "far", piece),
            self.src[piece].at[self.eighth(piece, here.dp, core, given=True)],
            self.dst.at[1, rows],
            (core, here.far_z, here.dp),
            sent=(self.layer, "far", piece, core),
        )

    def spread(self, piece, n):
        rows = self.eighth(piece, self.here.dp, self.here.core)
        return self.mail.copy(
            (self.layer, "spread", piece, n), self.dst.at[1, rows], self.dst.at[1, rows], self.here.peers[n]
        )

    def across(self, piece, n):
        dp = self.here.dp if n == 3 else self.here.copies[n]
        rows = self.eighth(piece, dp, self.here.core)
        return self.mail.copy(
            (self.layer, "across", piece, n), self.dst.at[1, rows], self.dst.at[1, rows], self.here.sibling
        )

    def start(self, piece):
        @pl.when(self.here.core == self.layer)
        def _():
            for core in range(2):
                self.far(piece, core).start()
            self.own(piece).start()
            self.twin(piece).start()

    def relay(self, piece):
        self.far(piece, 0).wait_recv()
        for n in range(3):
            self.spread(piece, n).start()
        self.across(piece, 3).start()

    def share(self, piece):
        for n in range(3):
            self.spread(piece, n).wait_recv()
            self.across(piece, n).start()

    def ready(self, piece):
        for n in range(4):
            self.across(piece, n).wait_recv()

        @pl.when(self.here.core == self.layer)
        def _():
            self.own(piece).wait()

        @pl.when(self.here.core != self.layer)
        def _():
            self.twin(piece).wait_recv()

    def finish(self, piece):
        for n in range(3):
            self.spread(piece, n).wait_send()
        for n in range(4):
            self.across(piece, n).wait_send()

        @pl.when(self.here.core == self.layer)
        def _():
            for core in range(2):
                self.far(piece, core).wait_send()
            self.twin(piece).wait_send()


class Vectors:
    def __init__(self, src, dst, here, mail):
        self.src, self.dst, self.here, self.mail = src, dst, here, mail

    def copies(self):
        here, mail = self.here, self.mail
        own, far = self.dst.at[here.core, 0], self.dst.at[here.core, 1]
        return [
            mail.copy("vec twin", self.src, own, here.sibling),
            mail.copy("vec far", self.src, far, (here.core, here.far_z, here.dp)),
            mail.copy("vec cross", self.src, far, (1 - here.core, here.far_z, here.dp)),
        ]

    def start(self):
        for copy in self.copies():
            copy.start()
        self.dst[self.here.core, 0] = self.src[...]

    def ready(self):
        for copy in self.copies():
            copy.wait()


KEPT = ("normed", "qkv", "logsum", "att", "middle", "upper", "hidden", "slope")
row_gain, row_shift, row_branch, row_up, row_query, row_value = 0, 2, 4, 6, 7, 8


def forward_kernel(
    where,
    pieces,
    inputs_ref,
    cotangent_ref,
    top_ref,
    up_ref,
    down_ref,
    gains_ref,
    shifts_ref,
    branch_ref,
    up_bias_ref,
    in_bias_ref,
    lengths_ref,
    *refs,
):
    names = ("weights", "vec", "grad", "states", "tail") + KEPT
    count = len(names)
    out = dict(zip(names, refs[:count]))
    kept = dict(zip(("weights", "grad", "states", "tail") + KEPT, refs[count : 2 * count - 1]))
    vec = out["vec"]
    seg_col, seg_row, pack_ref, qkv_out, att_out, low, got, mail_sems, move_sems = refs[2 * count - 1 :]
    here = Here()
    core = here.core
    mail, moves = Mail(mail_sems), Moves(move_sems)
    states = kept["states"]
    half = states.shape[1]
    local = where.qkv[0].stop
    blocks = half // block
    first = pl.multiple_of(core * half, half)
    rows_in = RowsIn("state", inputs_ref, states.at[0], here, mail, moves)
    grad_in = RowsIn("grad", cotangent_ref, kept["grad"], here, mail, moves)
    sources = (top_ref, top_ref, up_ref, down_ref)
    shards = [ShardsIn(n, sources, kept["weights"].at[n], here, mail, moves, pieces) for n in range(2)]
    vectors = Vectors(pack_ref, vec, here, mail)
    pack_ref[...] = jnp.zeros_like(pack_ref)
    pack_ref[row_gain : row_gain + 2, :] = gains_ref[...]
    pack_ref[row_shift : row_shift + 2, :] = shifts_ref[...]
    pack_ref[row_branch : row_branch + 2, :] = branch_ref[...]
    pack_ref[row_up : row_up + 1, :] = up_bias_ref[...]
    pack_ref[row_query : row_query + 1, 0:local] = in_bias_ref[0:1, :]
    pack_ref[row_value : row_value + 1, 0:local] = in_bias_ref[1:2, :]

    meet(
        [here.sibling, here.partner]
        + here.peers
        + [(here.core, here.far_z, here.dp), (1 - here.core, here.far_z, here.dp)]
    )
    rows_in.start()
    shards[0].start(0)
    vectors.start()
    shards[0].start(1)
    fill_segments(lengths_ref, here.mine, seg_col, seg_row)
    rows_in.forward()
    shards[0].relay(0)
    shards[0].start(2)
    shards[0].relay(1)
    shards[0].start(3)
    shards[0].share(0)
    vectors.ready()
    shards[0].share(1)

    later = []

    def tick():
        if later:
            later.pop(0)[1]()

    def upto(wanted):
        while any(label == wanted for label, _ in later):
            tick()

    def plan(label, *tasks):
        later.append((label, lambda: [task() for task in tasks]))

    plan("", partial(shards[1].start, 0), partial(shards[1].start, 1))
    plan("", partial(shards[0].relay, 2), partial(shards[1].start, 2))
    plan("", partial(shards[0].relay, 3), partial(shards[1].start, 3))
    plan("", partial(shards[0].share, 2))
    plan("", partial(shards[1].relay, 0))
    plan("units 0", partial(shards[0].share, 3))
    plan("", partial(shards[1].relay, 1))
    plan("heads 1", partial(shards[1].share, 0), partial(shards[1].share, 1))
    plan("", partial(shards[1].relay, 2))
    plan("", partial(shards[1].relay, 3), grad_in.start)
    plan("", partial(shards[1].share, 2))
    plan("", grad_in.forward)
    plan("units 1", partial(shards[1].share, 3))

    def layer_forward(layer):
        w_ref = kept["weights"].at[layer]
        v_ref = vec.at[layer]
        state_ref = states.at[layer]
        normed_ref, qkv_ref, logsum_ref, att_ref, middle_ref, upper_ref, hidden_ref, slope_ref = (
            kept[name].at[layer] for name in KEPT
        )

        def row(number, slot=0):
            return v_ref[slot, number : number + 1, :]

        def bias(slot, part):
            if part == 1:
                return 0.0
            number = row_query if part == 0 else row_value
            return v_ref[slot, number : number + 1, 0:local]

        def low_copy(index, rows):
            return mail.copy(
                ("low", layer, index, rows.start),
                low.at[layer, index, rows],
                got.at[layer, index, rows],
                here.partner,
            )

        def send_low(index, rows, value):
            low[layer, index, rows, :] = value.astype(bf16)
            low_copy(index, rows).start()

        def received(index, rows):
            low_copy(index, rows).wait()
            return low[layer, index, rows, :].astype(f32) + got[layer, index, rows, :].astype(f32)

        def save(name):
            moves.start((name, layer), kept[name].at[layer], out[name].at[layer])

        def qkv_copy(j):
            there = pl.ds(pl.multiple_of(first + j * block, block), block)
            return mail.copy(("qkv", layer, j), qkv_out.at[layer, j], qkv_ref.at[:, there, :], here.sibling)

        def project(j):
            rows = slice(j * block, (j + 1) * block)
            normal, _ = normalize(state_ref[rows, :].astype(f32))
            normed = (normal * row(row_gain) + row(row_shift)).astype(bf16)
            normed_ref[rows, :] = normed
            for part in range(3):
                weight = w_ref[1 - core, where.qkv[part], :]
                qkv_out[layer, j, part] = (mm_nt(normed, weight) + bias(1 - core, part)).astype(bf16)
            qkv_copy(j).start()
            there = pl.ds(pl.multiple_of(first + j * block, block), block)
            for part in range(3):
                weight = w_ref[core, where.qkv[part], :]
                qkv_ref[part, there, :] = (mm_nt(normed, weight) + bias(core, part)).astype(bf16)

        def att_copy(j):
            own = slice(j * block, (j + 1) * block)
            return mail.copy(("att", layer, j), att_out.at[layer, j], att_ref.at[core, own], here.sibling)

        upto(f"heads {layer}")
        if layer == 0:
            rows_in.ready()
        shards[layer].ready(0)
        shards[layer].ready(1)
        for i in range(2 * blocks):
            owner, j = i // blocks, i % blocks
            rows = slice(i * block, (i + 1) * block)
            own = slice(j * block, (j + 1) * block)
            count = (i + 1) * block
            if layer == 0:
                if i < blocks:
                    project(i)
                    tick()
            else:

                @pl.when(core == owner)
                def _():
                    result = before["middle"](own) + branch_scale * (
                        before["received"](1, own) + before["row"](row_branch + 1)
                    )
                    state_ref[own, :] = result.astype(bf16)
                    project(j)

            @pl.when(core != owner)
            def _():
                qkv_copy(j).wait_recv()

            mask = block_mask(seg_col, seg_row, rows, count)
            found = attend_block(qkv_ref, mask, rows, count, logsum_ref)

            @pl.when(core == owner)
            def _():
                for lane, lanes, result in found:
                    att_ref[core, own, lane : lane + lanes] = result
                att_copy(j).wait_recv()
                send_low(0, own, sum(mm(att_ref[k, own, :], w_ref[k, where.out, :]) for k in range(2)))

            @pl.when(core != owner)
            def _():
                for lane, lanes, result in found:
                    att_out[layer, j, :, lane : lane + lanes] = result
                att_copy(j).start()

            tick()
        for j in range(blocks):
            qkv_copy(j).wait_send()
            att_copy(j).wait_send()
        save("normed")
        save("qkv")
        save("att")
        save("logsum")

        for j in range(blocks):
            rows = slice(j * block, (j + 1) * block)
            middle = state_ref[rows, :].astype(f32) + branch_scale * (received(0, rows) + row(row_branch))
            middle_ref[rows, :] = middle
            normal, _ = normalize(middle)
            upper = (normal * row(row_gain + 1) + row(row_shift + 1)).astype(bf16)
            upper_ref[rows, :] = upper
            if j == 0:
                upto(f"units {layer}")
                shards[layer].ready(2)
                shards[layer].ready(3)
            total = None
            for k in range(2):
                pre = mm(upper, w_ref[k, where.up, :]) + row(row_up, k)
                square = pre * pre
                curve = jnp.tanh(root * pre * (1.0 + cube * square))
                rise = 0.5 * (1.0 + curve)
                hidden = (pre * rise).astype(bf16)
                hidden_ref[k, rows, :] = hidden
                slope = rise + pre * (rise * (1.0 - curve)) * (root * (1.0 + 3.0 * cube * square))
                slope_ref[k, rows, :] = slope.astype(bf16)
                term = mm(hidden, w_ref[k, where.down, :])
                total = term if total is None else total + term
            if layer == 0:
                send_low(1, rows, total)
            else:
                kept["tail"][rows, :] = total.astype(bf16)
            tick()
        for name in ("middle", "upper", "hidden", "slope"):
            save(name)
        moves.start(("weights", layer), w_ref, out["weights"].at[layer])
        if layer == 1:
            moves.start("tail", kept["tail"], out["tail"])
            return
        before.update(middle=lambda rows: middle_ref[rows, :], received=received, row=row)

    before = {}
    for layer in range(2):
        layer_forward(layer)
    while later:
        tick()
    moves.start("states", states, out["states"])
    grad_in.ready()
    moves.start("grad", kept["grad"], out["grad"])
    rows_in.finish()
    grad_in.finish()
    for shard in shards:
        for piece in range(len(pieces)):
            shard.finish(piece)
    moves.finish()


def forward_pass(where, inputs, cotangent, shard, vectors, lengths):
    quarter, width = inputs.shape[1:]
    half, length = 2 * quarter, 4 * quarter
    local = where.qkv[0].stop
    units = where.down.stop - where.down.start
    blocks = half // block
    top = 4 * local
    pieces = [(0, top // 2, 0), (top // 2, top // 2, 0), (top, width, top), (top + width, units, top + width)]
    vmem = pl.BlockSpec(memory_space=pltpu.VMEM)
    hbm = pl.BlockSpec(memory_space=pl.ANY)
    shapes = {
        "weights": ((2, 2, where.rows, width), bf16),
        "vec": ((2, 2, 16, width), f32),
        "grad": ((half, width), bf16),
        "states": ((2, half, width), bf16),
        "tail": ((half, width), bf16),
        "normed": ((2, half, width), bf16),
        "qkv": ((2, 3, length, local), bf16),
        "logsum": ((2, local // HEAD, length), f32),
        "att": ((2, 2, half, local), bf16),
        "middle": ((2, half, width), f32),
        "upper": ((2, half, width), bf16),
        "hidden": ((2, 2, half, units), bf16),
        "slope": ((2, 2, half, units), bf16),
    }
    found = pl.pallas_call(
        partial(forward_kernel, where, pieces),
        out_shape=[jax.ShapeDtypeStruct(*entry) for entry in shapes.values()],
        in_specs=[hbm] * 5 + [vmem] * 5 + [pl.BlockSpec(memory_space=pltpu.SMEM)],
        out_specs=[vmem if name == "vec" else hbm for name in shapes],
        scratch_shapes=[pltpu.VMEM(*entry) for name, entry in shapes.items() if name != "vec"]
        + [
            pltpu.VMEM((length, 1), jnp.int32),
            pltpu.VMEM((1, length), jnp.int32),
            pltpu.VMEM((16, width), f32),
            pltpu.VMEM((2, blocks, 3, block, local), bf16),
            pltpu.VMEM((2, blocks, block, local), bf16),
            pltpu.VMEM((2, 2, half, width), bf16),
            pltpu.VMEM((2, 2, half, width), bf16),
            pltpu.SemaphoreType.DMA((2, 128)),
            pltpu.SemaphoreType.DMA((64,)),
        ],
        compiler_params=pltpu.CompilerParams(
            vmem_limit_bytes=58 * 2**20, collective_id=1, has_side_effects=True
        ),
        name="forward_pass",
    )(inputs, cotangent, *shard, *vectors, lengths)
    return dict(zip(shapes, found))


def attend_back_block(qkv_ref, grad_ref, mask, rows, count, logsum_ref, dqkv_ref, dk_sum, dv_sum):
    heads = qkv_ref.shape[2] // HEAD
    scale = bf16(HEAD ** (-0.5))
    mixed = []
    for head, (lane, lanes, upper) in enumerate(head_lanes(heads)):
        cols = slice(lane, lane + lanes)
        queries = own_lanes(qkv_ref[0, rows, cols], lanes, upper) * scale
        grads = own_lanes(grad_ref[rows, cols], lanes, upper)
        keys = qkv_ref[1, 0:count, cols]
        scores = mm_nt(keys, queries)
        scores = jnp.where(mask, scores, masked_score)
        probs = jnp.exp(scores - logsum_ref[head : head + 1, rows])
        grad_probs = mm_nt(qkv_ref[2, 0:count, cols], grads)
        dv_sum[0:count, cols] += mm(probs.astype(bf16), grads)
        term = probs * grad_probs
        delta = jnp.sum(term, axis=0, keepdims=True)
        grad_scores = (term - probs * delta).astype(bf16)
        dk_sum[0:count, cols] += mm(grad_scores, queries)
        mixed.append((lanes, mm_tn(keys, grad_scores)))
    for pair in range(0, heads, 2):
        lane = pair * HEAD
        lanes, result = mixed[pair]
        if lanes > HEAD:
            result = jnp.concatenate([result[:HEAD], mixed[pair + 1][1][HEAD:]], axis=0)
        dqkv_ref[0, rows, lane : lane + lanes] = (result.T * HEAD ** (-0.5)).astype(bf16)


class RowsOut:
    def __init__(self, name, layer, src, dst, here, mail, moves):
        self.name, self.layer, self.src, self.dst = name, layer, src, dst
        self.here, self.mail, self.moves = here, mail, moves

    def ends(self):
        quarter = self.dst.shape[1]
        rows = pl.ds(pl.multiple_of(self.here.side * quarter, quarter), quarter)
        src = self.src if self.src.shape[0] == quarter else self.src.at[rows]
        return src, self.dst.at[self.here.mine]

    def home(self):
        return self.mail.copy((self.name, self.layer, "home"), *self.ends(), self.here.sibling)

    def away(self):
        device = (self.layer, self.here.far_z, self.here.dp)
        return self.mail.copy((self.name, self.layer, "away"), *self.ends(), device)

    def local(self):
        return self.moves.copy((self.name, self.layer), *self.ends())

    def cases(self, away, home, local):
        core, mine = self.here.core, self.here.mine
        pl.when(core != mine)(away)
        pl.when((core == mine) & (core != self.layer))(home)
        pl.when((core == mine) & (core == self.layer))(local)

    def start(self):
        self.cases(
            lambda: self.away().start(), lambda: self.home().start(), lambda: self.local().start()
        )

    def finish(self):
        self.cases(
            lambda: self.away().wait_send(), lambda: self.home().wait_send(), lambda: self.local().wait()
        )

        @pl.when(self.here.core == self.layer)
        def _():
            self.away().wait_recv()

            @pl.when(self.here.core != self.here.mine)
            def _():
                self.home().wait_recv()


def more_bits(copies):
    return [1 << n for n in range(2, copies.bit_length()) if (1 << n) < copies]


def flipped(dp, bit):
    return dp + bit - 2 * bit * lax.rem(dp // bit, 2)


class GradSum:
    def __init__(self, layer, part, buffers, final, here, mail, moves, pieces, place, copies):
        self.layer, self.part, self.final, self.pieces = layer, part, final, pieces
        self.place = place
        self.twin, self.first, self.second, self.cross, self.groups = buffers
        self.here, self.mail, self.moves = here, mail, moves
        self.bits_above = more_bits(copies)
        self.slot = lax.rem(here.core + layer, 2)
        self.bits = [lax.rem(here.dp, 2), lax.rem(here.dp // 2, 2)]
        self.stages = 6 + len(self.bits_above)

    @staticmethod
    def scratch(rows, places, width, copies):
        above = len(more_bits(copies))
        return [
            pltpu.VMEM((places, rows, width), bf16),
            pltpu.VMEM((places, 2, rows // 4, width), bf16),
            pltpu.VMEM((places, 2, rows // 8, width), bf16),
            pltpu.VMEM((2 * places, 2, rows // 8, width), bf16),
            pltpu.VMEM((max(1, above), 2 * places if above else 1, 2, rows // 8, width), bf16),
        ]

    def name(self, piece, kind, half=0):
        return ("sum", self.layer, self.pieces[piece], kind, half)

    def span(self, piece, start, count):
        return pl.ds(pl.multiple_of(self.pieces[piece][0] + start, 16), count)

    def chunk(self, piece, half, outer, inner):
        eighth = self.pieces[piece][1] // 8
        return half * 4 * eighth + outer * 2 * eighth + inner * eighth

    def device(self, axis):
        return self.here.peers[axis]

    def ring(self, piece):
        return self.place[piece] % self.twin.shape[0]

    def twin_copy(self, piece):
        start, count = self.pieces[piece]
        return self.mail.copy(
            self.name(piece, "twin"),
            self.part.at[1 - self.slot, slice(start, start + count)],
            self.twin.at[self.ring(piece)],
            self.here.sibling,
        )

    def first_copy(self, piece, half):
        src = self.span(piece, self.chunk(piece, half, 1 - self.bits[half], 0), self.pieces[piece][1] // 4)
        dst = self.first.at[self.ring(piece), half]
        return self.mail.copy(self.name(piece, "first", half), self.part.at[self.slot, src], dst, self.device(half))

    def second_copy(self, piece, half):
        axis = 1 - half
        src = self.span(
            piece, self.chunk(piece, half, self.bits[half], 1 - self.bits[axis]), self.pieces[piece][1] // 8
        )
        dst = self.second.at[self.ring(piece), half]
        return self.mail.copy(self.name(piece, "second", half), self.part.at[self.slot, src], dst, self.device(axis))

    def own(self, piece, half):
        return self.span(
            piece, self.chunk(piece, half, self.bits[half], self.bits[1 - half]), self.pieces[piece][1] // 8
        )

    def result(self, piece, half):
        ref, before = self.final[piece]
        start = self.pieces[piece][0] - before
        offset = self.chunk(piece, half, self.bits[half], self.bits[1 - half])
        return ref.at[pl.ds(pl.multiple_of(start + offset, 16), self.pieces[piece][1] // 8)]

    def cross_copy(self, piece, half):
        return self.mail.copy(
            self.name(piece, "cross", half),
            self.part.at[self.slot, self.own(piece, half)],
            self.cross.at[self.place[piece], half],
            (1 - self.here.core, self.here.far_z, self.here.dp),
        )

    def group_copy(self, step, piece, half):
        here = self.here
        return self.mail.copy(
            self.name(piece, ("group", step), half),
            self.part.at[self.slot, self.own(piece, half)],
            self.groups.at[step, self.place[piece], half],
            (here.core, here.z, flipped(here.dp, self.bits_above[step])),
        )

    def gather_copies(self, piece, half):
        rows = self.own(piece, half)
        return [
            self.mail.copy(
                self.name(piece, ("gather", n), half),
                self.part.at[self.slot, rows],
                self.result(piece, half),
                self.here.peers[n],
            )
            for n in range(3)
        ]

    def keep_copy(self, piece, half):
        rows = self.own(piece, half)
        return self.moves.copy(self.name(piece, "keep", half), self.part.at[self.slot, rows], self.result(piece, half))

    def stage(self, number, piece):
        if number < 4:
            (self.stage0, self.stage1, self.stage2, self.stage3)[number](piece)
        elif number < self.stages - 1:
            self.stage4(number - 4, piece)
        else:
            self.stage5(piece)

    def add(self, rows, other):
        self.part[self.slot, rows, :] += other

    def stage0(self, piece):
        self.twin_copy(piece).start()

    def stage1(self, piece):
        self.twin_copy(piece).wait_recv()
        start, count = self.pieces[piece]
        self.add(slice(start, start + count), self.twin[self.ring(piece)])
        for half in range(2):
            self.first_copy(piece, half).start()

    def stage2(self, piece):
        count = self.pieces[piece][1] // 4
        for half in range(2):
            self.first_copy(piece, half).wait()
            rows = self.span(piece, self.chunk(piece, half, self.bits[half], 0), count)
            self.add(rows, self.first[self.ring(piece), half])
            self.second_copy(piece, half).start()

    def stage3(self, piece):
        for half in range(2):
            self.second_copy(piece, half).wait()
            self.add(self.own(piece, half), self.second[self.ring(piece), half])

            @pl.when(self.here.core != self.layer)
            def _():
                self.cross_copy(piece, half).start()

    def stage4(self, step, piece):
        @pl.when(self.here.core == self.layer)
        def _():
            for half in range(2):
                if step == 0:
                    self.cross_copy(piece, half).wait_recv()
                    self.add(self.own(piece, half), self.cross[self.place[piece], half])
                else:
                    self.group_copy(step - 1, piece, half).wait()
                    self.add(self.own(piece, half), self.groups[step - 1, self.place[piece], half])
                if step < len(self.bits_above):
                    self.group_copy(step, piece, half).start()
                else:
                    for copy in self.gather_copies(piece, half):
                        copy.start()
                    self.keep_copy(piece, half).start()

    def stage5(self, piece):
        self.twin_copy(piece).wait_send()

        @pl.when(self.here.core == self.layer)
        def _():
            for half in range(2):
                for copy in self.gather_copies(piece, half):
                    copy.wait()
                self.keep_copy(piece, half).wait()

        @pl.when(self.here.core != self.layer)
        def _():
            for half in range(2):
                self.cross_copy(piece, half).wait_send()


class VectorSum:
    def __init__(self, layer, part, got, out, here, mail, copies):
        self.layer, self.part, self.got, self.out, self.mail = layer, part, got, out, mail
        self.devices = [here.partner, here.sibling] + here.peers[:2]
        self.devices += [(here.core, here.z, flipped(here.dp, bit)) for bit in more_bits(copies)]
        self.devices.append((here.core, here.far_z, here.dp))
        self.stages = len(self.devices) + 1

    def copy(self, step):
        return self.mail.copy(("vec", self.layer, step), self.part, self.got.at[step], self.devices[step])

    def stage(self, number, _):
        if number > 0:
            step = number - 1
            self.copy(step).wait()
            if number == 1:
                self.part[12:14, :] += self.got[step, 12:14, :]
            elif number < self.stages - 1:
                self.part[...] += self.got[step]
            else:
                self.out[...] = self.part[...] + self.got[step]
                self.out[8:10, :] = self.part[8:10, :] + self.got[step, 10:12, :]
        if number < self.stages - 1:
            self.copy(number).start()


class Pipeline:
    def __init__(self, gap):
        self.gap, self.now = gap, 0
        self.waiting, self.running = [], []

    def wait(self, one, stage):
        return 1 if self.gap == 1 else 4 if one.layer else (2, 3, 3, 3, 3, 3)[min(stage, 5)]

    def add(self, one, piece=0):
        self.waiting.append((one, piece))

    def tick(self, fresh=1):
        self.now += 1
        for item in self.running:
            one, piece, stage, due = item
            if due <= self.now:
                one.stage(stage, piece)
                item[2:] = [stage + 1, self.now + self.wait(one, stage)]
        for one, piece in self.waiting[:fresh]:
            one.stage(0, piece)
            self.running.append([one, piece, 1, self.now + self.wait(one, 0)])
        self.waiting = self.waiting[fresh:]
        self.running = [item for item in self.running if item[2] < item[0].stages]

    def hurry(self, ticks=0):
        self.gap = 1
        for item in self.running:
            item[3] = self.now + 1
        for _ in range(ticks):
            self.tick(fresh=3)

    def drain(self):
        self.hurry()
        while self.waiting or self.running:
            self.now += 1000
            self.tick(fresh=2)


SAVED = ("state",) + KEPT


def backward_kernel(where, copies, *refs):
    refs = list(refs)

    def take(count):
        found = refs[:count]
        del refs[:count]
        return found

    (grad_hbm, w_hbm, vec_ref, lengths_ref, states_hbm, tail_hbm) = take(6)
    kept_hbm = dict(zip(KEPT, take(len(KEPT))))
    (states_out, grads_out, final_top, final_up, final_down, vec_out) = take(6)
    grads, w_ref = take(2)
    saved = dict(zip(SAVED, take(len(SAVED))))
    (
        d_refs,
        gz_ref,
        dmiddle_ref,
        datt_out,
        datt_ref,
        dqkv_ref,
        dk_sum,
        dv_sum,
        dmix_ref,
        low,
        got,
        tail_low,
        tail_got,
        seg_col,
        seg_row,
        d_vecs,
        got_vecs,
    ) = take(17)
    buffers = take(5)
    mail_sems, move_sems = take(2)
    start_ref, normed_ref, qkv_ref, logsum_ref, att_ref, middle_ref, upper_ref, hidden_ref, slope_ref = (
        saved[name] for name in SAVED
    )
    dpre_ref = slope_ref
    gy_ref = gz_ref

    here = Here()
    core = here.core
    mail, moves = Mail(mail_sems), Moves(move_sems)
    half = dmiddle_ref.shape[0]
    blocks = half // block
    first = pl.multiple_of(core * half, half)
    order = list(range(blocks))[::-1]
    heads = slice(0, where.out.start)

    def load_copy(layer, name):
        if isinstance(name, slice):
            return moves.copy((layer, name.start), w_hbm.at[layer, :, name], w_ref.at[:, name])
        src = states_hbm if name == "state" else kept_hbm[name]
        return moves.copy((layer, name), src.at[layer], saved[name])

    def load(layer, *names):
        for name in names:
            load_copy(layer, name).start()

    def need(layer, *names):
        for name in names:
            load_copy(layer, name).wait()

    groups = [
        (where.down, "slope", where.up, "hidden", "upper"),
        ("middle", where.out),
        ("qkv", "logsum", "att"),
        (heads, "normed", "state"),
    ]
    grad_load = moves.copy("grad", grad_hbm, grads.at[1])
    grad_load.start()
    for group in groups:
        load(1, *group)
    tail_load = moves.copy("tail", tail_hbm, tail_low)
    tail_load.start()
    top = where.out.stop
    pieces = [
        (rows.start + n * ((rows.stop - rows.start) // 2), (rows.stop - rows.start) // 2)
        for rows in (where.down, where.up, slice(0, top))
        for n in range(2)
    ]
    meet(
        [here.sibling, here.partner]
        + here.peers
        + [(core, here.far_z, here.dp), (1 - core, here.far_z, here.dp)]
        + [(core, here.z, flipped(here.dp, bit)) for bit in more_bits(copies)]
    )
    line = Pipeline(4)
    sums = [
        GradSum(
            layer,
            d_refs.at[layer],
            buffers,
            [(final_down, where.down.start)] * 2 + [(final_up, where.up.start)] * 2 + [(final_top, 0)] * 2,
            here,
            mail,
            moves,
            pieces,
            [(1 - layer) * len(pieces) + n for n in range(len(pieces))],
            copies,
        )
        for layer in range(2)
    ]
    vectors = [
        VectorSum(layer, d_vecs.at[layer], got_vecs.at[layer], vec_out.at[layer], here, mail, copies)
        for layer in range(2)
    ]
    fill_segments(lengths_ref, here.mine, seg_col, seg_row)
    d_vecs[...] = jnp.zeros_like(d_vecs)
    rows_out = [
        RowsOut("state", 0, states_hbm.at[1], states_out, here, mail, moves),
        RowsOut("state", 1, tail_got, states_out, here, mail, moves),
        RowsOut("grad", 1, grads.at[0], grads_out, here, mail, moves),
        RowsOut("grad", 0, grads.at[1], grads_out, here, mail, moves),
    ]

    def pair_copy(layer, index, rows):
        return mail.copy(
            ("low", layer, index, rows.start), low.at[index, rows], got.at[index, rows], here.partner
        )

    def send_low(layer, index, rows, value):
        low[index, rows, :] = value.astype(bf16)
        pair_copy(layer, index, rows).start()

    def received(layer, index, rows):
        pair_copy(layer, index, rows).wait()
        return low[index, rows, :].astype(f32) + got[index, rows, :].astype(f32)

    def own_rows(j):
        return slice(j * block, (j + 1) * block)

    def total(value):
        return jnp.sum(value, axis=0, keepdims=True)

    def vector(layer, number):
        return vec_ref[layer, 0, number : number + 1, :]

    def note(layer, number, value):
        d_vecs[layer, number : number + 1, :] += total(value)

    def units_back(layer, j):
        rows = own_rows(j)
        gz = branch_scale * grads[layer, rows, :].astype(f32)
        note(layer, 5, gz)
        gz = gz.astype(bf16)
        gz_ref[rows, :] = gz
        part = None
        for k in range(2):
            dpre = (mm_nt(gz, w_ref[k, where.down, :]) * slope_ref[k, rows, :].astype(f32)).astype(bf16)
            dpre_ref[k, rows, :] = dpre
            term = mm_nt(dpre, w_ref[k, where.up, :])
            part = term if part is None else part + term
        send_low(layer, 0, rows, part)

    def units_weights(layer):
        d_ref = d_refs.at[layer]
        need(layer, "hidden", "upper")
        for k in range(2):
            d_ref[k, where.down, :] = mm_tn(hidden_ref[k], gz_ref[...]).astype(bf16)
            line.tick()
        line.add(sums[layer], 0)
        line.add(sums[layer], 1)
        for k in range(2):
            d_ref[k, where.up, :] = mm_tn(upper_ref[...], dpre_ref[k]).astype(bf16)
            note(layer, 8 + 2 * k, dpre_ref[k].astype(f32))
            line.tick()
        line.add(sums[layer], 2)
        line.add(sums[layer], 3)
        line.tick()

    def datt_copy(layer, j):
        there = pl.ds(pl.multiple_of(first + j * block, block), block)
        return mail.copy(("datt", layer, j), datt_out.at[j], datt_ref.at[there, :], here.sibling)

    def middle_back(layer, j):
        rows = own_rows(j)
        d_upper = received(layer, 0, rows)
        normal, rstd = normalize(middle_ref[rows, :])
        note(layer, 1, d_upper * normal)
        note(layer, 3, d_upper)
        d_middle = grads[layer, rows, :].astype(f32) + norm_back(
            normal, rstd, d_upper, vector(layer, row_gain + 1)
        )
        dmiddle_ref[rows, :] = d_middle
        gy = branch_scale * d_middle
        note(layer, 4, gy)
        gy = gy.astype(bf16)
        gy_ref[rows, :] = gy
        datt_out[j] = mm_nt(gy, w_ref[1 - core, where.out, :]).astype(bf16)
        datt_copy(layer, j).start()
        there = pl.ds(pl.multiple_of(first + j * block, block), block)
        datt_ref[there, :] = mm_nt(gy, w_ref[core, where.out, :]).astype(bf16)

    def mix_copy(layer, j):
        return mail.copy(
            ("mix", layer, j),
            dqkv_ref.at[:, pl.ds(pl.multiple_of(half - first + j * block, block), block), :],
            dmix_ref.at[core, :, pl.ds(j * block, block), :],
            here.sibling,
        )

    def finish(layer, i):
        owner, j = i // blocks, i % blocks
        rows = slice(i * block, (i + 1) * block)
        dqkv_ref[1, rows, :] = dk_sum[rows, :].astype(bf16)
        dqkv_ref[2, rows, :] = dv_sum[rows, :].astype(bf16)

        @pl.when(core == owner)
        def _():
            dmix_ref[core, :, own_rows(j), :] = dqkv_ref[:, rows, :]

        @pl.when(core != owner)
        def _():
            mix_copy(layer, j).start()

    def attention_back(layer):
        dk_sum[...] = jnp.zeros_like(dk_sum)
        dv_sum[...] = jnp.zeros_like(dv_sum)
        need(layer, "qkv", "logsum", "att")
        left = list(range(2 * blocks))
        for j in order:
            datt_copy(layer, j).wait()
            for i in (blocks + j, j):
                rows = slice(i * block, (i + 1) * block)
                count = (i + 1) * block
                mask = block_mask(seg_col, seg_row, rows, count)
                attend_back_block(
                    qkv_ref, datt_ref, mask, rows, count, logsum_ref, dqkv_ref, dk_sum, dv_sum
                )
                left.remove(i)
                if j == 0:
                    for done in range(2 * blocks)[::-1]:
                        if done > max(left, default=-1) and done // blocks == i // blocks:
                            finish(layer, done)
                line.tick()

    def heads_part(rows):
        part = None
        for k in range(2):
            for p in range(3):
                term = mm(dmix_ref[k, p, rows, :], w_ref[k, where.qkv[p], :])
                part = term if part is None else part + term
        return part

    def heads_back(layer, j):
        rows = own_rows(j)
        mix_copy(layer, j).wait_recv()
        send_low(layer, 1, rows, heads_part(rows))
        line.tick()

    quarter = states_out.shape[1]

    def side_rows(side):
        return pl.ds(pl.multiple_of(side * quarter, quarter), quarter)

    def last_copy():
        rows = side_rows(1 - here.side)
        return mail.copy("last", low.at[1, rows], got.at[1, rows], here.partner)

    def last_heads_back():
        for j in order:
            mix_copy(0, j).wait_recv()
        for side in (1 - here.side, here.side):
            rows = side_rows(side)
            part = heads_part(rows)
            low[1, rows, :] = part.astype(bf16)
            if side is not here.side:
                last_copy().start()
            normal, _ = normalize(start_ref[rows, :].astype(f32))
            note(0, 12, part * normal)
            note(0, 13, part)
            line.tick()

    def last_state_back():
        rows = side_rows(here.side)
        last_copy().wait()
        d_normed = low[1, rows, :].astype(f32) + got[1, rows, :].astype(f32)
        normal, rstd = normalize(start_ref[rows, :].astype(f32))
        d_state = dmiddle_ref[rows, :] + norm_back(normal, rstd, d_normed, vector(0, row_gain))
        grads[1, rows, :] = d_state.astype(bf16)

    def heads_weights(layer):
        d_ref = d_refs.at[layer]
        for k in range(2):
            d_ref[k, where.out, :] = mm_tn(att_ref[k], gy_ref[...]).astype(bf16)
        line.tick()
        for k in range(2):
            for p in range(3):
                d_ref[k, where.qkv[p], :] = mm_tn(dmix_ref[k, p], normed_ref[...]).astype(bf16)
            for n, p in enumerate((0, 2)):
                local = dmix_ref.shape[3]
                lanes = slice(n * 2 * block, n * 2 * block + local)
                d_vecs[layer, 9 + 2 * k : 10 + 2 * k, lanes] = total(dmix_ref[k, p].astype(f32))
            if k == 0:
                line.tick()
        line.add(sums[layer], 4)
        line.add(sums[layer], 5)
        line.tick(fresh=2 - layer)

    def state_back(layer, j):
        rows = own_rows(j)
        d_normed = received(layer, 1, rows)
        normal, rstd = normalize(start_ref[rows, :].astype(f32))
        note(layer, 0, d_normed * normal)
        note(layer, 2, d_normed)
        d_state = dmiddle_ref[rows, :] + norm_back(normal, rstd, d_normed, vector(layer, row_gain))
        grads[1 - layer, rows, :] = d_state.astype(bf16)

    def tail_copy():
        return mail.copy("tail", tail_low.at[side_rows(1 - here.side)], tail_got, here.partner)

    grad_load.wait()
    need(1, where.down, "slope", where.up)
    for j in order:
        units_back(1, j)
    for layer in (1, 0):
        units_weights(layer)
        if layer == 1:
            load(0, *groups[0])
            rows_out[0].start()
        need(layer, "middle", where.out)
        for j in order:
            line.tick()
            middle_back(layer, j)
            line.tick()
        if layer == 1:
            tail_load.wait()
            tail_copy().start()
        attention_back(layer)
        need(layer, heads, "normed", "state")
        if layer == 1:
            for j in order:
                heads_back(layer, j)
            tail_copy().wait()
            rows = side_rows(here.side)
            branch = tail_low[rows, :].astype(f32) + tail_got[...].astype(f32) + vector(1, row_branch + 1)
            tail_got[...] = (middle_ref[rows, :] + branch_scale * branch).astype(bf16)
            rows_out[1].start()
            load(0, *groups[1])
        else:
            last_heads_back()
        heads_weights(layer)
        if layer == 1:
            load(0, *groups[2])
            need(0, where.down, "slope", where.up)
        if layer == 1:
            for j in order:
                line.tick()
                state_back(1, j)
                units_back(0, j)
                line.tick()
            load(0, *groups[3])
            rows_out[2].start()
            line.add(vectors[1])
        else:
            line.add(vectors[0])
            line.tick(fresh=3)
            line.hurry()
            last_state_back()
            rows_out[3].start()
        for j in order:
            mix_copy(layer, j).wait_send()
    line.drain()
    for one in rows_out:
        one.finish()


def backward_pass(where, copies, kept, lengths):
    grad = kept["grad"]
    half, width = grad.shape
    quarter, length = half // 2, 2 * half
    local = where.qkv[0].stop
    blocks = half // block
    shape = jax.ShapeDtypeStruct
    vmem = pl.BlockSpec(memory_space=pltpu.VMEM)
    hbm = pl.BlockSpec(memory_space=pl.ANY)
    smem = pl.BlockSpec(memory_space=pltpu.SMEM)
    operands = [grad, kept["weights"], kept["vec"], lengths, kept["states"], kept["tail"]]
    operands += [kept[name] for name in KEPT]
    above = len(more_bits(copies))
    scratch = [
        pltpu.VMEM((2, half, width), bf16),
        pltpu.VMEM((2, where.rows, width), bf16),
        pltpu.VMEM((half, width), bf16),
    ]
    scratch += [pltpu.VMEM(kept[name].shape[1:], kept[name].dtype) for name in KEPT]
    scratch += [
        pltpu.VMEM((2, 2, where.rows, width), bf16),
        pltpu.VMEM((half, width), bf16),
        pltpu.VMEM((half, width), f32),
        pltpu.VMEM((blocks, block, local), bf16),
        pltpu.VMEM((length, local), bf16),
        pltpu.VMEM((3, length, local), bf16),
        pltpu.VMEM((length, local), f32),
        pltpu.VMEM((length, local), f32),
        pltpu.VMEM((2, 3, half, local), bf16),
        pltpu.VMEM((2, half, width), bf16),
        pltpu.VMEM((2, half, width), bf16),
        pltpu.VMEM((half, width), bf16),
        pltpu.VMEM((quarter, width), bf16),
        pltpu.VMEM((length, 1), jnp.int32),
        pltpu.VMEM((1, length), jnp.int32),
        pltpu.VMEM((2, 16, width), f32),
        pltpu.VMEM((2, 5 + above, 16, width), f32),
    ]
    scratch += GradSum.scratch(where.out.stop // 2, 6, width, copies)
    scratch += [pltpu.SemaphoreType.DMA((2, 192 + 96 * above)), pltpu.SemaphoreType.DMA((64,))]
    return pl.pallas_call(
        partial(backward_kernel, where, copies),
        out_shape=[
            shape((2, quarter, width), bf16),
            shape((2, quarter, width), bf16),
            shape((where.out.stop, width), bf16),
            shape((where.up.stop - where.up.start, width), bf16),
            shape((where.down.stop - where.down.start, width), bf16),
            shape((2, 16, width), f32),
        ],
        in_specs=[hbm, hbm, vmem, smem, hbm, hbm] + [hbm] * len(KEPT),
        out_specs=[hbm] * 5 + [vmem],
        scratch_shapes=scratch,
        compiler_params=pltpu.CompilerParams(
            vmem_limit_bytes=61 * 2**20, collective_id=2, has_side_effects=True
        ),
        name="backward_pass",
    )(*operands)


def per_device(
    inputs,
    cotangent,
    lengths,
    norm_gains,
    norm_shifts,
    in_weight,
    in_bias,
    out_weight,
    up_weight,
    up_bias,
    down_weight,
    branch_bias,
):
    core = lax.axis_index("section")
    copies = lax.axis_size("dp")
    width = inputs.shape[2]
    local = in_weight.shape[3]
    units = up_weight.shape[2]

    def pick(flag, yes, no):
        return jnp.where(flag, yes, no)

    where = Places(local, units, width)
    top = jnp.concatenate([in_weight[0].transpose(1, 2, 0).reshape(3 * local, width), out_weight[0]])
    kept = forward_pass(
        where,
        inputs,
        cotangent,
        (top, up_weight[0], down_weight[0]),
        (norm_gains[0], norm_shifts[0], branch_bias[0], up_bias, in_bias[0]),
        lengths,
    )
    section_outputs, input_grads, final, g_up, g_down, vecs = backward_pass(where, copies, kept, lengths)
    vec = pick(core == 0, vecs[0], vecs[1])
    g_in = final[: 3 * local].astype(f32).reshape(3, local, width).transpose(2, 0, 1)
    g_out, g_up, g_down = (grad.astype(f32) for grad in (final[where.out], g_up, g_down))
    b_in = jnp.stack([vec[9, :local], vec[9, 2 * block : 2 * block + local]])

    return (
        section_outputs[None],
        input_grads.astype(f32)[None],
        (vec[0:2] + jnp.pad(vec[12:13], ((0, 1), (0, 0))))[None],
        (vec[2:4] + jnp.pad(vec[13:14], ((0, 1), (0, 0))))[None],
        g_in[None],
        b_in[None],
        g_out[None],
        g_up[None],
        vec[8][None],
        g_down[None],
        vec[4:6][None],
    )


def solution(mesh):
    in_specs = (
        P("dp", "mp", None),
        P("dp", "mp", None),
        P("dp", None),
        P("section", None, None),
        P("section", None, None),
        P("section", None, None, "mp"),
        P("section", None, "mp"),
        P("section", "mp", None),
        P("section", None, "mp"),
        P("section", "mp"),
        P("section", "mp", None),
        P("section", None, None),
    )
    out_specs = (
        P("section", "dp", "mp", None),
        P("section", "dp", "mp", None),
        P("section", None, None),
        P("section", None, None),
        P("section", None, None, "mp"),
        P("section", None, "mp"),
        P("section", "mp", None),
        P("section", None, "mp"),
        P("section", "mp"),
        P("section", "mp", None),
        P("section", None, None),
    )
    return jax.shard_map(
        per_device, mesh=mesh, in_specs=in_specs, out_specs=out_specs, check_vma=False
    )
```
